128 devices in a mesh: grp: 4 (over y_lo, core), tp: 16 (over x, z), ctx: 2 (over y_hi).
Axes of the slice: x: 4, y: 4 (y_hi: 2, y_lo: 2; y = y_hi * 2 + y_lo), z: 4, core: 2. Of those that a mesh axis runs over, the one named last changes fastest.
Arguments:
- layer_input: bfloat16 [4, 2048, 2048], P('grp', 'ctx'), may hold values from -6 to 6
- ln1_gain: bfloat16 [2048], replicated, may hold values from 0.25 to 1.75
- ln1_bias: bfloat16 [2048], replicated, may hold values from -2.5 to 2.5
- qkv_weight: bfloat16 [2048, 3, 2048], P(None, None, 'tp'), may hold values from -0.1875 to 0.1875
- qv_bias: bfloat16 [2, 2048], P(None, 'tp'), may hold values from -3 to 3
- out_weight: bfloat16 [2048, 2048], P('tp'), may hold values from -0.5 to 0.5
- out_bias: bfloat16 [2048], replicated, may hold values from -2.5 to 2.5
- ln2_gain: bfloat16 [2048], replicated, may hold values from 0.25 to 1.75
- ln2_bias: bfloat16 [2048], replicated, may hold values from -2.5 to 2.5
- up_weight: bfloat16 [2048, 8192], P(None, 'tp'), may hold values from -0.125 to 0.125
- up_bias: bfloat16 [8192], P('tp'), may hold values from -3 to 3
- down_weight: bfloat16 [8192, 2048], P('tp'), may hold values from -0.0625 to 0.0625
- down_bias: bfloat16 [2048], replicated, may hold values from -2.5 to 2.5
- cotangent: bfloat16 [4, 2048, 2048], P('grp', 'ctx'), may hold values from -6 to 6
- group_table: int32 [4], replicated, may hold values from 0 to 2, as said below
- group_counts: int32 [3], replicated, may hold values from 1024 to 16384, as said below
- block_order: int32 [4], replicated, may hold values from 0 to 3, as said below
Outputs:
- layer_output: bfloat16 [4, 2048, 2048], P('grp', 'ctx')
- input_grad: float32 [4, 2048, 2048], P('grp', 'ctx')
- ln1_gain_grad: float32 [2048], replicated
- ln1_bias_grad: float32 [2048], replicated
- qkv_weight_grad: float32 [2048, 3, 2048], P(None, None, 'tp')
- qv_bias_grad: float32 [2, 2048], P(None, 'tp')
- out_weight_grad: float32 [2048, 2048], P('tp')
- out_bias_grad: float32 [2048], replicated
- ln2_gain_grad: float32 [2048], replicated
- ln2_bias_grad: float32 [2048], replicated
- up_weight_grad: float32 [2048, 8192], P(None, 'tp')
- up_bias_grad: float32 [8192], P('tp')
- down_weight_grad: float32 [8192, 2048], P('tp')
- down_bias_grad: float32 [2048], replicated
The draws below stay inside these ranges and needn't reach their ends.
Inputs may be any that keep to these rules, and one draw needn't show every extreme that they name: `group_table`: every script group sits at one group position or more; group 0 sits at exactly two, each other group at one. `group_counts`: the largest count is exactly 16384. `block_order`: A permutation of the 4 blocks; slots 2 c and 2 c + 1 belong to ctx index c, and their two blocks add up to 3.
All inputs are finite; a program needn't handle non-finite values.
Results may differ from the reference program's by a relative error of at most 0.025.
Values may be sent and summed in bfloat16 or wider, within the bound.
No kernel may reach another device: no remote copies, remote signals or barrier semaphores. Data moves between devices by JAX's collectives and lax.ppermute only.
A program may use at most 192 MiB of HBM per device.

```python
import math
from functools import partial
import jax
import jax.numpy as jnp
from jax import lax

D = 2048
HEADS = 16
HD = 128
FF = 8192
GROUPS = 3
COUNT_MOST = 16384
SEQ = 2048
BLOCK = 512
BLOCKS = 4
N_GRP = 4


def draw_group_table(key, part):
    key = jax.random.fold_in(key, 11)
    return jax.random.permutation(key, jnp.array([0, 0, 1, 2], dtype=jnp.int32))


def draw_group_counts(key, part):
    key = jax.random.fold_in(key, 12)
    lower_ends = jnp.array([8192, 4096, 1024], dtype=jnp.int32)
    upper_ends = jnp.array([16385, 12289, 8193], dtype=jnp.int32)
    raw_counts = jax.random.randint(key, (GROUPS,), lower_ends, upper_ends, dtype=jnp.int32)
    slots = jnp.arange(GROUPS, dtype=jnp.int32)
    busiest = jnp.argmax(raw_counts).astype(jnp.int32)
    return jnp.where(slots == busiest, jnp.full_like(raw_counts, COUNT_MOST), raw_counts).astype(jnp.int32)


def draw_block_order(key, part):
    key = jax.random.fold_in(key, 13)
    first_key, second_key = jax.random.split(key)
    pairs_count = BLOCKS // 2
    pairing = jax.random.permutation(first_key, pairs_count).astype(jnp.int32)
    flipped = jax.random.randint(second_key, (pairs_count,), 0, 2, dtype=jnp.int32)
    last_block = BLOCKS - 1
    leading = jnp.where(flipped == 1, pairing, last_block - pairing)
    return jnp.stack([leading, last_block - leading], axis=1).reshape(BLOCKS).astype(jnp.int32)


def level_of(stream_key, extent, shards, least, high):
    def one(dim, parts):
        draws = jax.random.uniform(jax.random.fold_in(jax.random.fold_in(stream_key, 6), dim), (parts,), jnp.float32, least / len(shards), high / len(shards))
        return jnp.repeat(jnp.exp(draws), extent[dim] // parts).reshape((-1,) + (1,) * (len(extent) - dim - 1))

    level = one(*shards[0])
    for cut in shards[1:]:
        level = level * one(*cut)
    return level


def gaussian(stream_key, shape, spread, limit, pieces=(), kind=jnp.bfloat16):
    level = level_of(stream_key, shape, pieces, -0.22, 0.18) if pieces else 1.0
    values = jax.random.normal(stream_key, shape, jnp.float32) * spread * level
    return jnp.minimum(jnp.maximum(values, -limit), limit).astype(kind)


def setup_inputs(seed: int = 0) -> dict:
    arg_keys = jax.random.split(jax.random.key(seed), 18)
    layer_input = gaussian(arg_keys[0], (N_GRP, SEQ, D), 1.0, 6.0, ((0, 4), (1, 2)))
    ln1_gain = jnp.clip(1.0 + 0.15 * jax.random.normal(arg_keys[1], (D,), jnp.float32), 0.25, 1.75).astype(jnp.bfloat16)
    ln1_bias = gaussian(arg_keys[2], (D,), 0.3, 2.5)
    qkv_weight = gaussian(arg_keys[3], (D, 3, D), (D // 2) ** -0.5, 0.1875, ((2, 16),))
    qv_bias = gaussian(arg_keys[4], (2, D), 0.5, 3.0, ((1, 16),))
    out_weight = gaussian(arg_keys[5], (D, D), (D // 16) ** -0.5, 0.5, ((0, 16),))
    out_bias = gaussian(arg_keys[6], (D,), 0.3, 2.5)
    ln2_gain = jnp.clip(1.0 + 0.15 * jax.random.normal(arg_keys[7], (D,), jnp.float32), 0.25, 1.75).astype(jnp.bfloat16)
    ln2_bias = gaussian(arg_keys[8], (D,), 0.3, 2.5)
    up_weight = gaussian(arg_keys[9], (D, FF), D ** -0.5, 0.125, ((1, 16),))
    up_bias = gaussian(arg_keys[10], (FF,), 0.5, 3.0, ((0, 16),))
    down_weight = gaussian(arg_keys[11], (FF, D), FF ** -0.5, 0.0625, ((0, 16),))
    down_bias = gaussian(arg_keys[12], (D,), 0.3, 2.5)
    cotangent = gaussian(arg_keys[13], (N_GRP, SEQ, D), 1.0, 6.0, ((0, 4), (1, 2)))
    group_table = draw_group_table(jax.random.fold_in(arg_keys[17], 71), 0)
    group_counts = draw_group_counts(jax.random.fold_in(arg_keys[17], 71), 0)
    block_order = draw_block_order(jax.random.fold_in(arg_keys[17], 71), 0)
    return dict(layer_input=layer_input, ln1_gain=ln1_gain, ln1_bias=ln1_bias, qkv_weight=qkv_weight, qv_bias=qv_bias, out_weight=out_weight, out_bias=out_bias, ln2_gain=ln2_gain, ln2_bias=ln2_bias, up_weight=up_weight, up_bias=up_bias, down_weight=down_weight, down_bias=down_bias, cotangent=cotangent, group_table=group_table, group_counts=group_counts, block_order=block_order)


@jax.custom_vjp
def low(v):
    return lax.optimization_barrier(v.astype(jnp.bfloat16)).astype(jnp.float32)

@jax.custom_vjp
def low_back(v):
    return v

def low_keep(v):
    return (low(v), None)

def low_pass(kept, grad):
    return (grad,)

def back_keep(v):
    return (v, None)

def back_low(kept, grad):
    return (low(grad),)
low.defvjp(low_keep, low_pass)
low_back.defvjp(back_keep, back_low)

def layer_norm(values, gain_vec, bias_vec):
    average = lax.optimization_barrier(jnp.mean(values, axis=-1, keepdims=True))
    centred = values - average
    variance = lax.optimization_barrier(jnp.mean(centred * centred, axis=-1, keepdims=True))
    return centred * lax.rsqrt(variance + 1e-05) * gain_vec + bias_vec

def gelu_tanh(values):
    inner = math.sqrt(2.0 / math.pi) * (values + 0.044715 * values * values * values)
    return 0.5 * values * (1.0 + jnp.tanh(inner))

def token_places(block_order, layout_index, block_rows):
    slots = layout_index // block_rows
    column = jnp.arange(block_order.shape[0], dtype=jnp.int32)
    picked = lax.optimization_barrier(jnp.sum(jnp.where(slots[:, None] == column[None, :], block_order[None, :], jnp.zeros_like(block_order)[None, :]), axis=1))
    return picked * block_rows + layout_index % block_rows

def position_shares(group_table, group_counts):
    member = (group_table[:, None] == jnp.arange(GROUPS, dtype=jnp.int32)[None, :]).astype(jnp.float32)
    holders = lax.optimization_barrier(jnp.sum(member, axis=0))
    counts_float = group_counts.astype(jnp.float32)
    per_group = counts_float / (holders * jnp.sum(counts_float))
    return group_table.shape[0] * lax.optimization_barrier(jnp.sum(member * per_group[None, :], axis=1))

def forward(params, layer_rows, places):
    ln1_gain, ln1_bias, qkv_weight, qv_bias, out_weight, out_bias, ln2_gain, ln2_bias, up_weight, up_bias, down_weight, down_bias = params
    highest = lax.Precision.HIGHEST
    normed = low(layer_norm(layer_rows, ln1_gain, ln1_bias))
    mixed = jnp.dot(normed, qkv_weight.reshape(D, 3 * D), precision=highest).reshape(SEQ, 3, HEADS, HD)
    query_rows = low(low_back(mixed[:, 0] + qv_bias[0].reshape(HEADS, HD)))
    key_rows = low(low_back(mixed[:, 1]))
    value_rows = low(low_back(mixed[:, 2] + qv_bias[1].reshape(HEADS, HD)))
    scores = low_back(jnp.einsum('qhd,khd->hqk', query_rows, key_rows, precision=highest) * (1.0 / math.sqrt(HD)))
    causal = places[:, None] >= places[None, :]
    scores = jnp.where(causal[None], scores, -1e+30)
    top_score = lax.optimization_barrier(jnp.max(scores, axis=-1, keepdims=True))
    expo = jnp.exp(scores - top_score)
    attn_probs = expo / lax.optimization_barrier(jnp.sum(expo, axis=-1, keepdims=True))
    heads_out = jnp.einsum('hqk,khd->qhd', low(attn_probs), value_rows, precision=highest)
    heads_out = low(low_back(heads_out)).reshape(SEQ, D)
    middle = layer_rows + low_back(jnp.dot(heads_out, out_weight, precision=highest)) + out_bias
    normed_two = low(layer_norm(middle, ln2_gain, ln2_bias))
    hidden = low_back(jnp.dot(normed_two, up_weight, precision=highest) + up_bias)
    active = low(gelu_tanh(hidden))
    return middle + low_back(jnp.dot(active, down_weight, precision=highest)) + down_bias

def reference(layer_input, ln1_gain, ln1_bias, qkv_weight, qv_bias, out_weight, out_bias, ln2_gain, ln2_bias, up_weight, up_bias, down_weight, down_bias, cotangent, group_table, group_counts, block_order):
    params = tuple((array_in.astype(jnp.float32) for array_in in (ln1_gain, ln1_bias, qkv_weight, qv_bias, out_weight, out_bias, ln2_gain, ln2_bias, up_weight, up_bias, down_weight, down_bias)))
    shares = position_shares(group_table, group_counts)
    places = token_places(block_order, jnp.arange(SEQ, dtype=jnp.int32), BLOCK)
    single_pass = partial(forward, places=places)
    outputs = []
    in_grads = []
    totals = tuple((jnp.zeros_like(array_in) for array_in in params))
    for position in range(N_GRP):
        result, pull = jax.vjp(single_pass, params, layer_input[position].astype(jnp.float32))
        grad_params, grad_rows = pull(cotangent[position].astype(jnp.float32) * shares[position])
        outputs.append(result.astype(jnp.bfloat16))
        in_grads.append(grad_rows)
        totals = tuple((running + fresh for running, fresh in zip(totals, grad_params)))
    return (jnp.stack(outputs), jnp.stack(in_grads), totals[0], totals[1], totals[2], totals[3], totals[4], totals[5], totals[6], totals[7], totals[8], totals[9], totals[10], totals[11])
```

```python
import math

import jax
import jax.numpy as jnp
from jax import lax
from jax.sharding import PartitionSpec as P

HD = 128
GROUPS = 3
EVERY = ("grp", "tp", "ctx")
N_GRP, N_TP, N_CTX, SIDE = 4, 16, 2, 4
fp32 = jnp.float32
bf16 = jnp.bfloat16


def device_id(grp, tx, tz, ctx):
    return (grp * N_TP + tx * SIDE + tz) * N_CTX + ctx


def line_groups(first_axis):
    groups = []
    for grp in range(N_GRP):
        for ctx in range(N_CTX):
            for fixed in range(SIDE):
                along_z = (grp % 2 == 0) == first_axis
                groups.append(
                    [
                        device_id(grp, fixed, i, ctx) if along_z else device_id(grp, i, fixed, ctx)
                        for i in range(SIDE)
                    ]
                )
    return groups


GROUPS_A = line_groups(True)
GROUPS_B = line_groups(False)


def swap_lines(groups, bit):
    return [(line[i], line[i ^ bit]) for line in groups for i in range(SIDE)]


def swap_all(grp_bit, ctx_bit):
    return [
        (device_id(g, x, z, c), device_id(g ^ grp_bit, x, z, c ^ ctx_bit))
        for g in range(N_GRP)
        for x in range(SIDE)
        for z in range(SIDE)
        for c in range(N_CTX)
    ]


def exchange(pieces, groups):
    return lax.all_to_all(pieces, EVERY, 0, 0, axis_index_groups=groups)


def spread(piece, groups):
    return exchange(jnp.broadcast_to(piece[None], (SIDE,) + piece.shape), groups)


def gather_lines(piece, groups):
    return lax.all_gather(piece, EVERY, axis=0, axis_index_groups=groups)


def layer_norm(values, gain_vec, bias_vec):
    average = jnp.mean(values, axis=-1, keepdims=True)
    centred = values - average
    variance = jnp.mean(centred * centred, axis=-1, keepdims=True)
    return centred * lax.rsqrt(variance + 1e-05) * gain_vec + bias_vec


def gelu_tanh(values):
    inner = math.sqrt(2.0 / math.pi) * (values + 0.044715 * values * values * values)
    return 0.5 * values * (1.0 + jnp.tanh(inner))


def token_places(block_order, layout_index, block_rows):
    slots = layout_index // block_rows
    column = jnp.arange(block_order.shape[0], dtype=jnp.int32)
    picked = jnp.sum(
        jnp.where(
            slots[:, None] == column[None, :],
            block_order[None, :],
            jnp.zeros_like(block_order)[None, :],
        ),
        axis=1,
    )
    return picked * block_rows + layout_index % block_rows


def position_shares(group_table, group_counts):
    member = (group_table[:, None] == jnp.arange(GROUPS, dtype=jnp.int32)[None, :]).astype(fp32)
    holders = jnp.sum(member, axis=0)
    counts_float = group_counts.astype(fp32)
    per_group = counts_float / (holders * jnp.sum(counts_float))
    return group_table.shape[0] * jnp.sum(member * per_group[None, :], axis=1)


def per_device(
    layer_input,
    ln1_gain,
    ln1_bias,
    qkv_weight,
    qv_bias,
    out_weight,
    out_bias,
    ln2_gain,
    ln2_bias,
    up_weight,
    up_bias,
    down_weight,
    down_bias,
    cotangent,
    group_table,
    group_counts,
    block_order,
):
    width = layer_input.shape[-1]
    rows = layer_input.shape[1]
    local = qkv_weight.shape[2]
    hidden_local = up_weight.shape[1]
    block_rows = rows // 2
    line_rows = rows // SIDE
    own_rows = line_rows // SIDE
    score_scale = 1.0 / math.sqrt(HD)
    grp_at = lax.axis_index("grp")
    tp_at = lax.axis_index("tp")
    ctx_at = lax.axis_index("ctx")
    even = grp_at % 2 == 0
    a_at = jnp.where(even, tp_at % SIDE, tp_at // SIDE)
    b_at = jnp.where(even, tp_at // SIDE, tp_at % SIDE)
    line_start = a_at * line_rows
    own_start = line_start + b_at * own_rows

    gain_one = ln1_gain.astype(fp32)
    bias_one = ln1_bias.astype(fp32)
    gain_two = ln2_gain.astype(fp32)
    bias_two = ln2_bias.astype(fp32)
    tokens = layer_input.reshape(rows, width)
    cot = cotangent.reshape(rows, width)
    own_tokens = lax.dynamic_slice_in_dim(tokens, own_start, own_rows, 0).astype(fp32)
    own_cot = lax.dynamic_slice_in_dim(cot, own_start, own_rows, 0).astype(fp32)
    qkv_flat = qkv_weight.reshape(width, 3 * local)

    out_lines = gather_lines(out_weight, GROUPS_A).reshape(SIDE * local, width)
    qkv_lines = gather_lines(qkv_flat, GROUPS_A)

    shares = position_shares(group_table, group_counts)
    grp_slots = jnp.arange(shares.shape[0], dtype=jnp.int32)
    my_share = jnp.sum(jnp.where(grp_slots == grp_at, shares, jnp.zeros_like(shares)))
    grad_out = cot.astype(fp32) * my_share
    grad_low = grad_out.astype(bf16)
    down_bias_grad = jnp.sum(grad_out, axis=0)

    index = jnp.arange(rows, dtype=jnp.int32)
    query_places = token_places(block_order, ctx_at * rows + index, block_rows)
    other_places = token_places(block_order, (1 - ctx_at) * rows + index, block_rows)
    key_places = jnp.concatenate([query_places, other_places])
    causal = query_places[:, None] >= key_places[None, :]
    normed = layer_norm(tokens.astype(fp32), gain_one, bias_one).astype(bf16)
    mixed = jnp.dot(normed, qkv_flat, preferred_element_type=fp32)
    query = (mixed[:, :local] + qv_bias[0].astype(fp32)).astype(bf16)
    key_own = mixed[:, local : 2 * local].astype(bf16)
    value_own = (mixed[:, 2 * local :] + qv_bias[1].astype(fp32)).astype(bf16)
    pair = jnp.stack([key_own, value_own])
    swap_ctx = [(0, 1), (1, 0)]
    pair_other = lax.ppermute(pair, "ctx", swap_ctx)
    keys = jnp.concatenate([key_own, pair_other[0]], axis=0)
    values = jnp.concatenate([value_own, pair_other[1]], axis=0)
    scores = jnp.einsum("qd,kd->qk", query, keys, preferred_element_type=fp32) * score_scale
    scores = jnp.where(causal, scores, -1e30)
    top_score = jnp.max(scores, axis=-1, keepdims=True)
    expo = jnp.exp(scores - top_score)
    probs = expo / jnp.sum(expo, axis=-1, keepdims=True)
    probs_low = probs.astype(bf16)
    heads = jnp.einsum("qk,kd->qd", probs_low, values, preferred_element_type=fp32).astype(bf16)

    heads_line = exchange(heads.reshape(SIDE, line_rows, local), GROUPS_A)
    heads_line = heads_line.transpose(1, 0, 2).reshape(line_rows, SIDE * local)
    partial_out = jnp.dot(heads_line, out_lines, preferred_element_type=fp32).astype(bf16)
    partial_out = exchange(partial_out.reshape(SIDE, own_rows, width), GROUPS_B)
    middle = own_tokens + jnp.sum(partial_out.astype(fp32), axis=0) + out_bias.astype(fp32)
    normed_two_own = layer_norm(middle, gain_two, bias_two).astype(bf16)
    normed_two = spread(normed_two_own, GROUPS_B).reshape(line_rows, width)
    normed_two = gather_lines(normed_two, GROUPS_A).reshape(rows, width)

    hidden = jnp.dot(normed_two, up_weight, preferred_element_type=fp32) + up_bias.astype(fp32)
    active, gelu_pull = jax.vjp(gelu_tanh, hidden)
    active = active.astype(bf16)
    active_grad = jnp.einsum("rd,fd->rf", grad_low, down_weight, preferred_element_type=fp32)
    hidden_grad = gelu_pull(active_grad)[0].astype(bf16)

    def sum_rows(partial):
        parts = exchange(partial.reshape(SIDE, line_rows, width), GROUPS_A)
        parts = jnp.sum(parts.astype(fp32), axis=0).astype(bf16)
        parts = exchange(parts.reshape(SIDE, own_rows, width), GROUPS_B)
        return jnp.sum(parts.astype(fp32), axis=0)

    normed_two_grad = sum_rows(
        jnp.einsum("rf,df->rd", hidden_grad, up_weight, preferred_element_type=fp32).astype(bf16)
    )
    norm_value, norm_pull = jax.vjp(layer_norm, middle, gain_two, bias_two)
    middle_part, ln2_gain_part, ln2_bias_part = norm_pull(normed_two_grad)
    middle_grad = own_cot * my_share + middle_part
    middle_low = spread(middle_grad.astype(bf16), GROUPS_B).reshape(line_rows, width)

    head_grad = jnp.einsum("rd,fd->rf", middle_low, out_lines, preferred_element_type=fp32)
    head_grad = head_grad.astype(bf16).reshape(line_rows, SIDE, local).transpose(1, 0, 2)
    head_grad = exchange(head_grad, GROUPS_A).reshape(rows, local)
    prob_grad = jnp.einsum("qd,kd->qk", head_grad, values, preferred_element_type=fp32)
    values_grad = jnp.einsum("qk,qd->kd", probs_low, head_grad, preferred_element_type=fp32)
    score_grad = (
        probs * (prob_grad - jnp.sum(probs * prob_grad, axis=-1, keepdims=True))
    ).astype(bf16)
    query_grad = (
        jnp.einsum("qk,kd->qd", score_grad, keys, preferred_element_type=fp32) * score_scale
    ).astype(bf16)
    keys_grad = (
        jnp.einsum("qk,qd->kd", score_grad, query, preferred_element_type=fp32) * score_scale
    )
    pair_grad = jnp.stack([keys_grad, values_grad])
    pair_from = lax.ppermute(pair_grad[:, rows:].astype(bf16), "ctx", swap_ctx)
    pair_grad = (pair_grad[:, :rows] + pair_from.astype(fp32)).astype(bf16)
    qkv_grad = jnp.concatenate([query_grad, pair_grad[0], pair_grad[1]], axis=1)

    qkv_grad_line = exchange(qkv_grad.reshape(SIDE, line_rows, 3 * local), GROUPS_A)
    normed_grad = jnp.einsum(
        "arc,adc->rd", qkv_grad_line, qkv_lines, preferred_element_type=fp32
    ).astype(bf16)
    normed_grad = exchange(normed_grad.reshape(SIDE, own_rows, width), GROUPS_B)
    normed_grad = jnp.sum(normed_grad.astype(fp32), axis=0)
    first_value, first_pull = jax.vjp(layer_norm, own_tokens, gain_one, bias_one)
    input_part, ln1_gain_part, ln1_bias_part = first_pull(normed_grad)
    input_grad_own = (middle_grad + input_part).astype(bf16)
    vector_part = jnp.concatenate(
        [
            jnp.stack(
                [
                    ln1_gain_part,
                    ln1_bias_part,
                    ln2_gain_part,
                    ln2_bias_part,
                    jnp.sum(middle_grad, axis=0),
                ]
            ),
            jnp.zeros((11, width), fp32),
        ]
    ).astype(bf16)
    final_line = spread(jnp.concatenate([input_grad_own, vector_part]), GROUPS_B)
    input_grad = spread(final_line[:, :own_rows].reshape(line_rows, width), GROUPS_A)
    input_grad = input_grad.reshape(1, rows, width).astype(fp32)
    vectors = jnp.sum(final_line[:, own_rows : own_rows + 8].astype(fp32), axis=0)
    for pairs in (
        swap_lines(GROUPS_A, 1),
        swap_lines(GROUPS_A, 2),
        swap_all(1, 0),
        swap_all(2, 0),
        swap_all(0, 1),
    ):
        vectors = vectors + lax.ppermute(vectors, EVERY, pairs)

    partial_mlp = jnp.dot(active, down_weight, preferred_element_type=fp32).astype(bf16)
    output_own = (middle + sum_rows(partial_mlp) + down_bias.astype(fp32)).astype(bf16)
    output_line = spread(output_own, GROUPS_B).reshape(line_rows, width)
    layer_output = spread(output_line, GROUPS_A).reshape(1, rows, width)

    def total(value):
        return lax.psum(value, ("grp", "ctx"))

    down_weight_grad = jnp.einsum("rf,rd->fd", active, grad_low, preferred_element_type=fp32)
    up_weight_grad = jnp.einsum("rd,rf->df", normed_two, hidden_grad, preferred_element_type=fp32)
    down_weight_grad, up_weight_grad = total(
        (down_weight_grad.astype(bf16), up_weight_grad.astype(bf16))
    )
    middle_rows = gather_lines(middle_low, GROUPS_A).reshape(rows, width)
    out_weight_grad = jnp.einsum("rf,rd->fd", heads, middle_rows, preferred_element_type=fp32)
    up_bias_grad = jnp.sum(hidden_grad.astype(fp32), axis=0)
    qv_bias_grad = jnp.concatenate(
        [
            jnp.sum(query_grad.astype(fp32), axis=0),
            jnp.sum(pair_grad[1].astype(fp32), axis=0),
        ]
    )
    small_rows = jnp.concatenate(
        [
            down_bias_grad[None],
            jnp.concatenate(
                [up_bias_grad, qv_bias_grad, jnp.zeros((width - hidden_local - 2 * local,), fp32)]
            )[None],
            jnp.zeros((14, width), fp32),
        ]
    )
    out_and_small = jnp.concatenate([out_weight_grad, small_rows], axis=0).astype(bf16)
    qkv_weight_grad = jnp.einsum("rd,rc->dc", normed, qkv_grad, preferred_element_type=fp32)
    out_and_small, qkv_weight_grad = total((out_and_small, qkv_weight_grad.astype(bf16)))
    out_weight_grad = out_and_small[:local].astype(fp32)
    small_rows = out_and_small[local : local + 2].astype(fp32)
    return (
        layer_output,
        input_grad,
        vectors[0],
        vectors[1],
        qkv_weight_grad.astype(fp32).reshape(width, 3, local),
        small_rows[1, hidden_local : hidden_local + 2 * local].reshape(2, local),
        out_weight_grad,
        vectors[4],
        vectors[2],
        vectors[3],
        up_weight_grad.astype(fp32),
        small_rows[1, :hidden_local],
        down_weight_grad.astype(fp32),
        small_rows[0],
    )


def solution(mesh):
    placed = (
        P("grp", "ctx", None),
        P(),
        P(),
        P(None, None, "tp"),
        P(None, "tp"),
        P("tp", None),
        P(),
        P(),
        P(),
        P(None, "tp"),
        P("tp"),
        P("tp", None),
        P(),
        P("grp", "ctx", None),
        P(),
        P(),
        P(),
    )
    return jax.shard_map(
        per_device,
        mesh=mesh,
        in_specs=placed,
        out_specs=(
            P("grp", "ctx", None),
            P("grp", "ctx", None),
            P(),
            P(),
            P(None, None, "tp"),
            P(None, "tp"),
            P("tp", None),
            P(),
            P(),
            P(),
            P(None, "tp"),
            P("tp"),
            P("tp", None),
            P(),
        ),
        check_vma=False,
    )
```

```python
import math

import jax
import jax.numpy as jnp
from jax import lax
from jax.experimental import pallas as pl
from jax.experimental.pallas import tpu as pltpu
from jax.sharding import PartitionSpec as P

HD = 128
GROUPS = 3
EVERY = ("grp", "tp", "ctx")
N_GRP, N_TP, N_CTX, SIDE = 4, 16, 2, 4
fp32 = jnp.float32
bf16 = jnp.bfloat16


def device_id(grp, tx, tz, ctx):
    return (grp * N_TP + tx * SIDE + tz) * N_CTX + ctx


def line_groups(first_axis):
    groups = []
    for grp in range(N_GRP):
        for ctx in range(N_CTX):
            for fixed in range(SIDE):
                along_z = (grp % 2 == 0) == first_axis
                groups.append(
                    [
                        device_id(grp, fixed, i, ctx) if along_z else device_id(grp, i, fixed, ctx)
                        for i in range(SIDE)
                    ]
                )
    return groups


GROUPS_A = line_groups(True)
GROUPS_B = line_groups(False)


def swap_lines(groups, bit):
    return [(line[i], line[i ^ bit]) for line in groups for i in range(SIDE)]


def swap_all(grp_bit, ctx_bit):
    return [
        (device_id(g, x, z, c), device_id(g ^ grp_bit, x, z, c ^ ctx_bit))
        for g in range(N_GRP)
        for x in range(SIDE)
        for z in range(SIDE)
        for c in range(N_CTX)
    ]


def exchange(pieces, groups):
    return lax.all_to_all(pieces, EVERY, 0, 0, axis_index_groups=groups)


def spread(piece, groups):
    return exchange(jnp.broadcast_to(piece[None], (SIDE,) + piece.shape), groups)


def turn(groups, step):
    return [(line[i], line[(i + step) % SIDE]) for line in groups for i in range(SIDE)]


def sum_pieces(partial, place, groups):
    piece_rows = partial.shape[0] // SIDE
    total = lax.dynamic_slice_in_dim(partial, place * piece_rows, piece_rows, 0).astype(fp32)
    for step in (1, 3, 2):
        goes = (place + step) % SIDE
        piece = lax.dynamic_slice_in_dim(partial, goes * piece_rows, piece_rows, 0)
        total = total + lax.ppermute(piece, EVERY, turn(groups, step)).astype(fp32)
    return total


def join_pieces(piece, place, groups):
    piece_rows, width = piece.shape
    whole = jnp.zeros((SIDE * piece_rows, width), piece.dtype)
    whole = lax.dynamic_update_slice_in_dim(whole, piece, place * piece_rows, 0)
    for step in (1, 3, 2):
        come = lax.ppermute(piece, EVERY, turn(groups, step))
        origin = (place + SIDE - step) % SIDE
        whole = lax.dynamic_update_slice_in_dim(whole, come, origin * piece_rows, 0)
    return whole


def swap_pieces(pieces, place, groups):
    whole = jnp.zeros_like(pieces)
    own = lax.dynamic_index_in_dim(pieces, place, 0)
    whole = lax.dynamic_update_slice_in_dim(whole, own, place, 0)
    for step in (1, 3, 2):
        piece = lax.dynamic_index_in_dim(pieces, (place + step) % SIDE, 0)
        come = lax.ppermute(piece, EVERY, turn(groups, step))
        whole = lax.dynamic_update_slice_in_dim(whole, come, (place + SIDE - step) % SIDE, 0)
    return whole


def arriving(pieces, groups):
    come = {step: lax.ppermute(pieces(step), EVERY, turn(groups, step)) for step in (1, 3, 2)}
    return [pieces(0), come[1], come[2], come[3]]


def after(value, *earlier):
    return lax.optimization_barrier((value,) + earlier)[0]


def gather_lines(piece, groups):
    return lax.all_gather(piece, EVERY, axis=0, axis_index_groups=groups)


def layer_norm(values, gain_vec, bias_vec):
    average = jnp.mean(values, axis=-1, keepdims=True)
    centred = values - average
    variance = jnp.mean(centred * centred, axis=-1, keepdims=True)
    return centred * lax.rsqrt(variance + 1e-05) * gain_vec + bias_vec


def gelu_tanh(values):
    inner = math.sqrt(2.0 / math.pi) * (values + 0.044715 * values * values * values)
    return 0.5 * values * (1.0 + jnp.tanh(inner))


def token_places(block_order, layout_index, block_rows):
    slots = layout_index // block_rows
    column = jnp.arange(block_order.shape[0], dtype=jnp.int32)
    picked = jnp.sum(
        jnp.where(
            slots[:, None] == column[None, :],
            block_order[None, :],
            jnp.zeros_like(block_order)[None, :],
        ),
        axis=1,
    )
    return picked * block_rows + layout_index % block_rows


def position_shares(group_table, group_counts):
    member = (group_table[:, None] == jnp.arange(GROUPS, dtype=jnp.int32)[None, :]).astype(fp32)
    holders = jnp.sum(member, axis=0)
    counts_float = group_counts.astype(fp32)
    per_group = counts_float / (holders * jnp.sum(counts_float))
    return group_table.shape[0] * jnp.sum(member * per_group[None, :], axis=1)


def widen(down, up, out, qkv, whole):
    steps = 8
    small = out.shape[0] - HD
    width = out.shape[1]
    line_rows = whole.shape[1] - 16

    def body(
        down_in, up_in, qkv_in, whole_in, out_in, down_to, up_to, qkv_to, whole_to, out_to, small_to
    ):
        def block(down_in, up_in, qkv_in, whole_in, down_to, up_to, qkv_to, whole_to):
            down_to[...] = down_in[...].astype(fp32)
            up_to[...] = up_in[...].astype(fp32).T
            qkv_to[...] = qkv_in[...].astype(fp32)
            whole_to[...] = whole_in[...].astype(fp32)

        def rows(ref):
            return pl.BlockSpec((ref.shape[0] // steps, ref.shape[1]), lambda i: (i, 0))

        def columns(ref):
            return pl.BlockSpec((ref.shape[0], ref.shape[1] // steps), lambda i: (0, i))

        def planes(ref):
            return pl.BlockSpec(
                (ref.shape[0], ref.shape[1] // steps, ref.shape[2]), lambda i: (0, i, 0)
            )

        part = steps // SIDE
        lines = pl.BlockSpec((1, line_rows // part, width), lambda i: (i // part, i % part, 0))
        pltpu.emit_pipeline(
            block,
            grid=(steps,),
            in_specs=[rows(down_in), columns(up_in), planes(qkv_in), lines],
            out_specs=[rows(down_to), rows(up_to), planes(qkv_to), lines],
        )(down_in, up_in, qkv_in, whole_in, down_to, up_to, qkv_to, whole_to)
        out_to[...] = out_in[:HD].astype(fp32)
        small_to[...] = out_in[HD:].astype(fp32)

    hbm = pl.BlockSpec(memory_space=pltpu.HBM)
    vmem = pl.BlockSpec(memory_space=pltpu.VMEM)
    like = [down.shape, up.shape[::-1], qkv.shape, (SIDE, line_rows, width)]
    like += [(HD, width), (small, width)]
    return pl.pallas_call(
        body,
        in_specs=[hbm] * 4 + [vmem],
        out_specs=[hbm] * 4 + [vmem] * 2,
        out_shape=[jax.ShapeDtypeStruct(shape, fp32) for shape in like],
        compiler_params=pltpu.CompilerParams(vmem_limit_bytes=58 * 2**20),
        name="widen",
    )(down, up, qkv, whole, out)


def per_device(
    layer_input,
    ln1_gain,
    ln1_bias,
    qkv_weight,
    qv_bias,
    out_weight,
    out_bias,
    ln2_gain,
    ln2_bias,
    up_weight,
    up_bias,
    down_weight,
    down_bias,
    cotangent,
    group_table,
    group_counts,
    block_order,
):
    width = layer_input.shape[-1]
    rows = layer_input.shape[1]
    local = qkv_weight.shape[2]
    hidden_local = up_weight.shape[1]
    block_rows = rows // 2
    line_rows = rows // SIDE
    own_rows = line_rows // SIDE
    score_scale = 1.0 / math.sqrt(HD)
    grp_at = lax.axis_index("grp")
    tp_at = lax.axis_index("tp")
    ctx_at = lax.axis_index("ctx")
    even = grp_at % 2 == 0
    a_at = jnp.where(even, tp_at % SIDE, tp_at // SIDE)
    b_at = jnp.where(even, tp_at // SIDE, tp_at % SIDE)
    line_start = a_at * line_rows
    own_start = line_start + b_at * own_rows

    always = ctx_at < N_CTX

    def stage(work, *operands):
        shapes = jax.eval_shape(work, *operands)

        def empty(*operands):
            return jax.tree.map(lambda like: jnp.zeros(like.shape, like.dtype), shapes)

        return lax.cond(always, work, empty, *operands)

    gain_one = ln1_gain.astype(fp32)
    bias_one = ln1_bias.astype(fp32)
    gain_two = ln2_gain.astype(fp32)
    bias_two = ln2_bias.astype(fp32)
    tokens = layer_input.reshape(rows, width)
    cot = cotangent.reshape(rows, width)
    own_tokens = lax.dynamic_slice_in_dim(tokens, own_start, own_rows, 0).astype(fp32)
    own_cot = lax.dynamic_slice_in_dim(cot, own_start, own_rows, 0).astype(fp32)

    shares = position_shares(group_table, group_counts)
    grp_slots = jnp.arange(shares.shape[0], dtype=jnp.int32)
    my_share = jnp.sum(jnp.where(grp_slots == grp_at, shares, jnp.zeros_like(shares)))
    index = jnp.arange(rows, dtype=jnp.int32)
    query_places = token_places(block_order, ctx_at * rows + index, block_rows)
    other_places = token_places(block_order, (1 - ctx_at) * rows + index, block_rows)
    key_places = jnp.concatenate([query_places, other_places])
    causal = query_places[:, None] >= key_places[None, :]
    out_lines = gather_lines(out_weight, GROUPS_A).reshape(SIDE * local, width)
    up_lines = gather_lines(up_weight, GROUPS_A)
    qkv_turned = qkv_weight.transpose(1, 2, 0).reshape(3 * local, width)
    normed = layer_norm(tokens.astype(fp32), gain_one, bias_one).astype(bf16)
    mixed = jnp.einsum("rd,cd->rc", normed, qkv_turned, preferred_element_type=fp32)
    query = (mixed[:, :local] + qv_bias[0].astype(fp32)).astype(bf16)
    key_own = mixed[:, local : 2 * local].astype(bf16)
    value_own = (mixed[:, 2 * local :] + qv_bias[1].astype(fp32)).astype(bf16)
    pair = jnp.stack([key_own, value_own])
    swap_ctx = [(0, 1), (1, 0)]
    pair_other = lax.ppermute(pair, "ctx", swap_ctx)

    cot = after(cot, pair)
    grad_out = cot.astype(fp32) * my_share
    grad_low = grad_out.astype(bf16)
    down_bias_grad = jnp.sum(grad_out, axis=0)
    active_grad = jnp.einsum("rd,fd->rf", grad_low, down_weight, preferred_element_type=fp32)
    active_grad = active_grad.astype(bf16)
    bias_rows = jnp.broadcast_to(up_bias[None, None], (SIDE, 16, hidden_local))
    active_grad = jnp.concatenate(
        [active_grad.reshape(SIDE, line_rows, hidden_local), bias_rows], axis=1
    )
    pair_other, active_grad, down_bias_grad = lax.optimization_barrier(
        (pair_other, active_grad, down_bias_grad)
    )
    active_grad = exchange(active_grad, GROUPS_A)

    keys = jnp.concatenate([key_own, pair_other[0]], axis=0)
    values = jnp.concatenate([value_own, pair_other[1]], axis=0)
    scores = jnp.einsum("qd,kd->qk", query, keys, preferred_element_type=fp32) * score_scale
    scores = jnp.where(causal, scores, -1e30)
    top_score = jnp.max(scores, axis=-1, keepdims=True)
    expo = jnp.exp(scores - top_score)
    probs = expo / jnp.sum(expo, axis=-1, keepdims=True)
    probs_low = probs.astype(bf16)
    heads = jnp.einsum("qk,kd->qd", probs_low, values, preferred_element_type=fp32).astype(bf16)

    heads, active_grad = lax.optimization_barrier((heads, active_grad))

    heads_line = exchange(heads.reshape(SIDE, line_rows, local), GROUPS_A)
    heads_line = heads_line.transpose(1, 0, 2).reshape(line_rows, SIDE * local)
    partial_out = jnp.dot(heads_line, out_lines, preferred_element_type=fp32).astype(bf16)
    partial_out = exchange(partial_out.reshape(SIDE, own_rows, width), GROUPS_B)
    middle = own_tokens + jnp.sum(partial_out.astype(fp32), axis=0) + out_bias.astype(fp32)
    normed_two_own = layer_norm(middle, gain_two, bias_two).astype(bf16)
    normed_two = spread(normed_two_own, GROUPS_B).reshape(line_rows, width)

    hidden = jnp.einsum("rd,adf->arf", normed_two, up_lines, preferred_element_type=fp32)
    hidden = hidden + active_grad[:, line_rows : line_rows + 1].astype(fp32)
    active, gelu_pull = jax.vjp(gelu_tanh, hidden)
    active = active.astype(bf16)
    hidden_grad = gelu_pull(active_grad[:, :line_rows].astype(fp32))[0].astype(bf16)
    normed_two_grad = jnp.einsum(
        "arf,adf->rd", hidden_grad, up_lines, preferred_element_type=fp32
    ).astype(bf16)
    normed_two_grad, active, normed_two = lax.optimization_barrier(
        (normed_two_grad, active, normed_two)
    )

    normed_two_rows = gather_lines(normed_two, GROUPS_A)

    def norm_stage(normed_two_grad, active, middle, own_cot_share):
        normed_two_grad = exchange(normed_two_grad.reshape(SIDE, own_rows, width), GROUPS_B)
        active_own = swap_pieces(active, a_at, GROUPS_A).reshape(rows, hidden_local)
        normed_two_grad = jnp.sum(normed_two_grad.astype(fp32), axis=0)
        norm_value, norm_pull = jax.vjp(layer_norm, middle, gain_two, bias_two)
        middle_part, ln2_gain_part, ln2_bias_part = norm_pull(normed_two_grad)
        middle_grad = own_cot_share + middle_part
        middle_low = spread(middle_grad.astype(bf16), GROUPS_B).reshape(line_rows, width)
        partial_mlp = jnp.dot(active_own, down_weight, preferred_element_type=fp32).astype(bf16)
        vector_two = jnp.stack([ln2_gain_part, ln2_bias_part, jnp.sum(middle_grad, axis=0)])
        return middle_grad, middle_low, vector_two, active_own, partial_mlp

    middle_grad, middle_low, vector_two, active_own, partial_mlp = stage(
        norm_stage, normed_two_grad, active, middle, own_cot * my_share
    )
    normed_two_rows, qkv_turned = lax.optimization_barrier(
        (normed_two_rows, qkv_turned, middle_low)
    )[:2]
    normed_two_rows = normed_two_rows.reshape(rows, width)
    qkv_lines = gather_lines(qkv_turned, GROUPS_A).reshape(SIDE * 3 * local, width)
    partial_mlp = lax.psum_scatter(
        partial_mlp, EVERY, scatter_dimension=0, tiled=True, axis_index_groups=GROUPS_A
    )

    def attention_stage(
        middle_low, hidden_grad, heads_line, active_own, grad_low, normed_two_rows
    ):
        head_grad = jnp.einsum("rd,fd->rf", middle_low, out_lines, preferred_element_type=fp32)
        head_grad = head_grad.astype(bf16).reshape(line_rows, SIDE, local).transpose(1, 0, 2)
        head_grad = exchange(head_grad, GROUPS_A).reshape(rows, local)
        head_grad, hidden_grad, heads_line = lax.optimization_barrier(
            (head_grad, hidden_grad, heads_line)
        )
        hidden_grad_own = exchange(hidden_grad, GROUPS_A).reshape(rows, hidden_local)
        out_weight_grad = jnp.einsum(
            "rf,rd->fd", heads_line, middle_low, preferred_element_type=fp32
        ).astype(bf16)
        out_weight_grad = sum_pieces(out_weight_grad, a_at, GROUPS_A)
        prob_grad = jnp.einsum("qd,kd->qk", head_grad, values, preferred_element_type=fp32)
        values_grad = jnp.einsum("qk,qd->kd", probs_low, head_grad, preferred_element_type=fp32)
        score_grad = (
            probs * (prob_grad - jnp.sum(probs * prob_grad, axis=-1, keepdims=True))
        ).astype(bf16)
        keys_grad = (
            jnp.einsum("qk,qd->kd", score_grad, query, preferred_element_type=fp32) * score_scale
        )
        pair_grad = jnp.stack([keys_grad, values_grad])
        pair_from = lax.ppermute(pair_grad[:, rows:].astype(bf16), "ctx", swap_ctx)
        score_grad, active_own, hidden_grad_own = lax.optimization_barrier(
            (score_grad, active_own, hidden_grad_own, keys_grad)
        )[:3]
        query_grad = (
            jnp.einsum("qk,kd->qd", score_grad, keys, preferred_element_type=fp32) * score_scale
        ).astype(bf16)
        down_weight_grad = jnp.einsum(
            "rf,rd->fd", active_own, grad_low, preferred_element_type=fp32
        ).astype(bf16)
        up_weight_grad = jnp.einsum(
            "rf,rd->fd", hidden_grad_own, normed_two_rows, preferred_element_type=fp32
        ).astype(bf16)
        up_bias_grad = jnp.sum(hidden_grad_own.astype(fp32), axis=0)
        pair_from, down_weight_grad, up_weight_grad, up_bias_grad = lax.optimization_barrier(
            (pair_from, down_weight_grad, up_weight_grad, up_bias_grad)
        )
        pair_grad = (pair_grad[:, :rows] + pair_from.astype(fp32)).astype(bf16)
        qkv_grad = jnp.concatenate([query_grad, pair_grad[0], pair_grad[1]], axis=1)
        return qkv_grad, down_weight_grad, up_weight_grad, out_weight_grad, up_bias_grad

    qkv_grad, down_weight_grad, up_weight_grad, out_weight_grad, up_bias_grad = stage(
        attention_stage, middle_low, hidden_grad, heads_line, active_own, grad_low, normed_two_rows
    )
    qkv_weight_grad = jnp.einsum(
        "rd,rc->dc", normed, qkv_grad, preferred_element_type=fp32
    ).astype(bf16)
    qkv_weight_grad = jnp.stack([qkv_weight_grad[:, j * local : (j + 1) * local] for j in range(3)])
    qkv_bias_grad = jnp.sum(qkv_grad.astype(fp32), axis=0)
    small_rows = jnp.concatenate(
        [
            down_bias_grad[None],
            jnp.concatenate(
                [up_bias_grad, qkv_bias_grad, jnp.zeros((width - hidden_local - 3 * local,), fp32)]
            )[None],
            jnp.zeros((14, width), fp32),
        ]
    )
    out_and_small = jnp.concatenate([out_weight_grad, small_rows], axis=0).astype(bf16)
    weight_grads = (down_weight_grad, up_weight_grad, out_and_small, qkv_weight_grad)
    qkv_grad, partial_mlp, *weight_grads = lax.optimization_barrier(
        (qkv_grad, partial_mlp) + weight_grads
    )
    weight_grads = lax.psum(tuple(weight_grads), ("grp", "ctx"))

    def finish(qkv_grad, partial_mlp, qkv_lines, middle, middle_grad, own_tokens, vector_two):
        qkv_grad_line = exchange(qkv_grad.reshape(SIDE, line_rows, 3 * local), GROUPS_A)
        output_own = middle + sum_pieces(partial_mlp, b_at, GROUPS_B)
        output_own = (output_own + down_bias.astype(fp32)).astype(bf16)
        output_line = join_pieces(output_own, b_at, GROUPS_B)
        qkv_grad_line = qkv_grad_line.transpose(1, 0, 2).reshape(line_rows, SIDE * 3 * local)
        normed_grad = jnp.dot(qkv_grad_line, qkv_lines, preferred_element_type=fp32).astype(bf16)
        normed_grad = exchange(normed_grad.reshape(SIDE, own_rows, width), GROUPS_B)
        normed_grad, output_line = lax.optimization_barrier((normed_grad, output_line))
        layer_output = join_pieces(output_line, a_at, GROUPS_A).reshape(1, rows, width)
        normed_grad = jnp.sum(normed_grad.astype(fp32), axis=0)
        first_value, first_pull = jax.vjp(layer_norm, own_tokens, gain_one, bias_one)
        input_part, ln1_gain_part, ln1_bias_part = first_pull(normed_grad)
        input_grad_own = (middle_grad + input_part).astype(bf16)
        vector_part = jnp.concatenate(
            [
                ln1_gain_part[None],
                ln1_bias_part[None],
                vector_two,
                jnp.zeros((11, width), fp32),
            ]
        ).astype(bf16)
        line = spread(jnp.concatenate([input_grad_own, vector_part]), GROUPS_B)
        line, layer_output = lax.optimization_barrier((line, layer_output))
        vectors = jnp.sum(line[:, own_rows:].astype(fp32), axis=0).astype(bf16)
        line = jnp.concatenate([line[:, :own_rows].reshape(line_rows, width), vectors])
        whole = spread(line, GROUPS_A)
        vectors = jnp.sum(whole[:, line_rows : line_rows + 8].astype(fp32), axis=0)
        for pairs in (swap_all(1, 0), swap_all(2, 0), swap_all(0, 1)):
            vectors = vectors + lax.ppermute(vectors, EVERY, pairs)
        return layer_output, whole, vectors

    layer_output, whole, vectors = stage(
        finish, qkv_grad, partial_mlp, qkv_lines, middle, middle_grad, own_tokens, vector_two
    )
    down_weight_grad, up_weight_grad, qkv_weight_grad, input_grad, out_weight_grad, small_rows = widen(
        *weight_grads, whole
    )
    return (
        layer_output,
        input_grad.reshape(1, rows, width),
        vectors[0],
        vectors[1],
        qkv_weight_grad.transpose(1, 0, 2),
        small_rows[1, hidden_local : hidden_local + 3 * local].reshape(3, local)[::2],
        out_weight_grad,
        vectors[4],
        vectors[2],
        vectors[3],
        up_weight_grad,
        small_rows[1, :hidden_local],
        down_weight_grad,
        small_rows[0],
    )


def solution(mesh):
    placed = (
        P("grp", "ctx", None),
        P(),
        P(),
        P(None, None, "tp"),
        P(None, "tp"),
        P("tp", None),
        P(),
        P(),
        P(),
        P(None, "tp"),
        P("tp"),
        P("tp", None),
        P(),
        P("grp", "ctx", None),
        P(),
        P(),
        P(),
    )
    return jax.shard_map(
        per_device,
        mesh=mesh,
        in_specs=placed,
        out_specs=(
            P("grp", "ctx", None),
            P("grp", "ctx", None),
            P(),
            P(),
            P(None, None, "tp"),
            P(None, "tp"),
            P("tp", None),
            P(),
            P(),
            P(),
            P(None, "tp"),
            P("tp"),
            P("tp", None),
            P(),
        ),
        check_vma=False,
    )
```

```python
import math

import jax
import jax.numpy as jnp
from jax import lax
from jax.experimental import pallas as pl
from jax.experimental.pallas import tpu as pltpu
from jax.sharding import PartitionSpec as P

HD = 128
GROUPS = 3
TILE = 256
SCALE = 1.0 / math.sqrt(HD)
SCALE_TWO = SCALE * math.log2(math.e)
EVERY = ("grp", "tp", "ctx")
N_GRP, N_TP, N_CTX, SIDE = 4, 16, 2, 4
fp32 = jnp.float32
bf16 = jnp.bfloat16


def device_id(grp, tx, tz, ctx):
    return (grp * N_TP + tx * SIDE + tz) * N_CTX + ctx


def line_groups(first_axis):
    groups = []
    for grp in range(N_GRP):
        for ctx in range(N_CTX):
            for fixed in range(SIDE):
                along_z = (grp % 2 == 0) == first_axis
                groups.append(
                    [
                        device_id(grp, fixed, i, ctx) if along_z else device_id(grp, i, fixed, ctx)
                        for i in range(SIDE)
                    ]
                )
    return groups


GROUPS_A = line_groups(True)
GROUPS_B = line_groups(False)


def swap_lines(groups, bit):
    return [(line[i], line[i ^ bit]) for line in groups for i in range(SIDE)]


def swap_all(grp_bit, ctx_bit):
    return [
        (device_id(g, x, z, c), device_id(g ^ grp_bit, x, z, c ^ ctx_bit))
        for g in range(N_GRP)
        for x in range(SIDE)
        for z in range(SIDE)
        for c in range(N_CTX)
    ]


def exchange(pieces, groups):
    return lax.all_to_all(pieces, EVERY, 0, 0, axis_index_groups=groups)


def spread(piece, groups):
    return exchange(jnp.broadcast_to(piece[None], (SIDE,) + piece.shape), groups)


def turn(groups, step):
    return [(line[i], line[(i + step) % SIDE]) for line in groups for i in range(SIDE)]


def sum_pieces(partial, place, groups):
    piece_rows = partial.shape[0] // SIDE
    total = lax.dynamic_slice_in_dim(partial, place * piece_rows, piece_rows, 0).astype(fp32)
    for step in (1, 3, 2):
        goes = (place + step) % SIDE
        piece = lax.dynamic_slice_in_dim(partial, goes * piece_rows, piece_rows, 0)
        total = total + lax.ppermute(piece, EVERY, turn(groups, step)).astype(fp32)
    return total


def join_pieces(piece, place, groups):
    piece_rows, width = piece.shape
    whole = jnp.zeros((SIDE * piece_rows, width), piece.dtype)
    whole = lax.dynamic_update_slice_in_dim(whole, piece, place * piece_rows, 0)
    for step in (1, 3, 2):
        come = lax.ppermute(piece, EVERY, turn(groups, step))
        origin = (place + SIDE - step) % SIDE
        whole = lax.dynamic_update_slice_in_dim(whole, come, origin * piece_rows, 0)
    return whole


def swap_pieces(pieces, place, groups):
    whole = jnp.zeros_like(pieces)
    own = lax.dynamic_index_in_dim(pieces, place, 0)
    whole = lax.dynamic_update_slice_in_dim(whole, own, place, 0)
    for step in (1, 3, 2):
        piece = lax.dynamic_index_in_dim(pieces, (place + step) % SIDE, 0)
        come = lax.ppermute(piece, EVERY, turn(groups, step))
        whole = lax.dynamic_update_slice_in_dim(whole, come, (place + SIDE - step) % SIDE, 0)
    return whole


def arriving(pieces, groups):
    come = {step: lax.ppermute(pieces(step), EVERY, turn(groups, step)) for step in (1, 3, 2)}
    return [pieces(0), come[1], come[2], come[3]]


def after(value, *earlier):
    return lax.optimization_barrier((value,) + earlier)[0]


def gather_lines(piece, groups):
    return lax.all_gather(piece, EVERY, axis=0, axis_index_groups=groups)


def layer_norm(values, gain_vec, bias_vec):
    average = jnp.mean(values, axis=-1, keepdims=True)
    centred = values - average
    variance = jnp.mean(centred * centred, axis=-1, keepdims=True)
    return centred * lax.rsqrt(variance + 1e-05) * gain_vec + bias_vec


def position_shares(group_table, group_counts):
    member = (group_table[:, None] == jnp.arange(GROUPS, dtype=jnp.int32)[None, :]).astype(fp32)
    holders = jnp.sum(member, axis=0)
    counts_float = group_counts.astype(fp32)
    per_group = counts_float / (holders * jnp.sum(counts_float))
    return group_table.shape[0] * jnp.sum(member * per_group[None, :], axis=1)


def turned_product(left, right):
    return lax.dot_general(left, right, (((1,), (1,)), ((), ())), preferred_element_type=fp32)


def plain_product(left, right):
    return lax.dot_general(left, right, (((1,), (0,)), ((), ())), preferred_element_type=fp32)


def attention_call(body, name, scratch, like, places, *operands):
    return pl.pallas_call(
        body,
        in_specs=[pl.BlockSpec(memory_space=pltpu.SMEM)]
        + [pl.BlockSpec(memory_space=pltpu.VMEM)] * len(operands),
        out_specs=[pl.BlockSpec(memory_space=pltpu.VMEM)] * len(like),
        out_shape=[jax.ShapeDtypeStruct(shape, kind) for shape, kind in like],
        scratch_shapes=[pltpu.VMEM(shape, fp32) for shape in scratch],
        compiler_params=pltpu.CompilerParams(vmem_limit_bytes=40 * 2**20),
        name=name,
    )(places, *operands)


def own_keys_forward(places, query, pair):
    rows = query.shape[0]
    block = rows // 2

    def body(places, query, pair, top, total, mixed):
        key, value = pair.at[0], pair.at[1]
        for slot in range(2):
            for start in range(slot * block, (slot + 1) * block, TILE):
                last = start + TILE
                keys = slice(slot * block, last)
                scores = turned_product(query[start:last], key[keys]) * SCALE_TWO
                place_q = lax.broadcasted_iota(jnp.int32, scores.shape, 0) + start
                place_k = lax.broadcasted_iota(jnp.int32, scores.shape, 1) + slot * block
                scores = jnp.where(place_q >= place_k, scores, -1e30)
                peak = jnp.max(scores, axis=1, keepdims=True)
                weights = jnp.exp2(scores - peak)
                top[start:last] = peak
                total[start:last] = jnp.sum(weights, axis=1, keepdims=True)
                mixed[start:last] = plain_product(weights.astype(bf16), value[keys])
        for slot in range(2):
            other = 1 - slot

            @pl.when(places[slot] > places[other])
            def _():
                add_keys(query, key, value, top, total, mixed, slot, other, block)

    like = [((rows, 1), fp32), ((rows, 1), fp32), ((rows, HD), fp32)]
    return attention_call(body, "own_keys_forward", [], like, places, query, pair)


def add_keys(query, key, value, top, total, mixed, slot, key_slot, block):
    keys = slice(key_slot * block, (key_slot + 1) * block)
    for start in range(slot * block, (slot + 1) * block, TILE):
        here = slice(start, start + TILE)
        scores = turned_product(query[here], key[keys]) * SCALE_TWO
        peak = jnp.maximum(top[here], jnp.max(scores, axis=1, keepdims=True))
        fade = jnp.exp2(top[here] - peak)
        weights = jnp.exp2(scores - peak)
        top[here] = peak
        total[here] = total[here] * fade + jnp.sum(weights, axis=1, keepdims=True)
        mixed[here] = mixed[here] * fade + plain_product(weights.astype(bf16), value[keys])


def other_keys_forward(places, query, pair, top, total, mixed):
    rows = query.shape[0]
    block = rows // 2

    def body(places, query, pair, top_in, total_in, mixed_in, heads, level, top, total, mixed):
        key, value = pair.at[0], pair.at[1]
        top[...] = top_in[...]
        total[...] = total_in[...]
        mixed[...] = mixed_in[...]
        for slot in range(2):
            for key_slot in range(2):

                @pl.when(places[slot] > places[2 + key_slot])
                def _():
                    add_keys(query, key, value, top, total, mixed, slot, key_slot, block)

        for start in range(0, rows, TILE):
            here = slice(start, start + TILE)
            heads[here] = (mixed[here] / total[here]).astype(bf16)
            logs = top[here] + jnp.log2(total[here])
            level[:, here] = jnp.broadcast_to(logs, (TILE, HD)).T[:8]

    like = [((rows, HD), bf16), ((8, rows), fp32)]
    scratch = [(rows, 1), (rows, 1), (rows, HD)]
    return attention_call(
        body, "other_keys_forward", scratch, like, places, query, pair, top, total, mixed
    )


def pair_backward(
    query, key, value, head_grad, level, slack, query_grad, key_grad, value_grad, slot, key_slot, block, own
):
    for start in range(key_slot * block, (key_slot + 1) * block, TILE):
        keys = slice(start, start + TILE)
        first = start if own else slot * block
        rows = slice(first, (slot + 1) * block)
        scores = turned_product(key[keys], query[rows]) * SCALE_TWO - level[:1, rows]
        if own:
            place_k = lax.broadcasted_iota(jnp.int32, scores.shape, 0)
            place_q = lax.broadcasted_iota(jnp.int32, scores.shape, 1)
            scores = jnp.where(place_q >= place_k, scores, -1e30)
        probs = jnp.exp2(scores)
        value_grad[keys] += plain_product(probs.astype(bf16), head_grad[rows])
        prob_grad = turned_product(value[keys], head_grad[rows]) - slack[:1, rows]
        score_grad = (probs * prob_grad).astype(bf16)
        key_grad[keys] += plain_product(score_grad, query[rows])
        query_grad[rows] += lax.dot_general(
            score_grad, key[keys], (((0,), (0,)), ((), ())), preferred_element_type=fp32
        )


def other_keys_backward(places, query, pair, head_grad, heads, level):
    rows = query.shape[0]
    block = rows // 2

    def body(
        places, query, pair, head_grad, heads, level, query_grad, pair_grad, slack, key_sum, value_sum
    ):
        key, value = pair.at[0], pair.at[1]
        query_grad[...] = jnp.zeros(query_grad.shape, fp32)
        key_sum[...] = jnp.zeros(key_sum.shape, fp32)
        value_sum[...] = jnp.zeros(value_sum.shape, fp32)
        for start in range(0, rows, TILE):
            here = slice(start, start + TILE)
            both = head_grad[here].astype(fp32) * heads[here].astype(fp32)
            both = jnp.sum(both, axis=1, keepdims=True)
            slack[:, here] = jnp.broadcast_to(both, (TILE, HD)).T[:8]
        for slot in range(2):
            for key_slot in range(2):

                @pl.when(places[slot] > places[2 + key_slot])
                def _():
                    pair_backward(
                        query, key, value, head_grad, level, slack,
                        query_grad, key_sum, value_sum, slot, key_slot, block, False,
                    )

        pair_grad[0] = (key_sum[...] * SCALE).astype(bf16)
        pair_grad[1] = value_sum[...].astype(bf16)

    like = [((rows, HD), fp32), ((2, rows, HD), bf16), ((8, rows), fp32)]
    return attention_call(
        body, "other_keys_backward", [(rows, HD)] * 2, like,
        places, query, pair, head_grad, heads, level,
    )


def own_keys_backward(places, query, pair, head_grad, level, slack, query_grad):
    rows = query.shape[0]
    block = rows // 2

    def body(
        places, query, pair, head_grad, level, slack, query_in, query_grad, pair_grad, query_sum
    ):
        key, value = pair.at[0], pair.at[1]
        query_sum[...] = query_in[...]
        pair_grad[...] = jnp.zeros(pair_grad.shape, fp32)
        key_sum = pair_grad.at[0]
        value_sum = pair_grad.at[1]
        for slot in range(2):
            pair_backward(
                query, key, value, head_grad, level, slack,
                query_sum, key_sum, value_sum, slot, slot, block, True,
            )
        for slot in range(2):

            @pl.when(places[slot] > places[1 - slot])
            def _():
                pair_backward(
                    query, key, value, head_grad, level, slack,
                    query_sum, key_sum, value_sum, slot, 1 - slot, block, False,
                )

        pair_grad[0] = pair_grad[0] * SCALE
        query_grad[...] = (query_sum[...] * SCALE).astype(bf16)

    like = [((rows, HD), bf16), ((2, rows, HD), fp32)]
    return attention_call(
        body, "own_keys_backward", [(rows, HD)], like,
        places, query, pair, head_grad, level, slack, query_grad,
    )


def feed_forward(line_place, normed_two, up_lines, active_grad):
    rows, width = normed_two.shape
    units = up_lines.shape[2]
    bend = math.sqrt(2.0 / math.pi)

    def body(place, normed_two, up, grad, active, hidden_grad, back, total):
        step = pl.program_id(0)
        hidden = plain_product(normed_two[...], up[0])
        hidden = hidden + grad[0, rows : rows + 1].astype(fp32)
        square = hidden * hidden
        bent = jnp.tanh(bend * hidden * (1.0 + 0.044715 * square))
        half = 0.5 * (1.0 + bent)
        active[0] = (hidden * half).astype(bf16)
        slope = half + (0.5 * bend) * hidden * (1.0 - bent * bent) * (1.0 + 0.134145 * square)
        low = (slope * grad[0, :rows].astype(fp32)).astype(bf16)
        hidden_grad[0] = low
        product = turned_product(low, up[0])

        @pl.when(step == 0)
        def _():
            total[...] = product

        @pl.when(step > 0)
        def _():
            total[...] += product

        @pl.when(step == SIDE - 1)
        def _():
            back[...] = total[...].astype(bf16)

    def origin(step, place):
        return ((place[0] + SIDE - step) % SIDE, 0, 0)

    return pl.pallas_call(
        body,
        grid_spec=pltpu.PrefetchScalarGridSpec(
            num_scalar_prefetch=1,
            grid=(SIDE,),
            in_specs=[
                pl.BlockSpec((rows, width), lambda step, place: (0, 0)),
                pl.BlockSpec((1, width, units), origin),
                pl.BlockSpec((1, rows + 16, units), lambda step, place: (step, 0, 0)),
            ],
            out_specs=[
                pl.BlockSpec((1, rows, units), origin),
                pl.BlockSpec((1, rows, units), origin),
                pl.BlockSpec((rows, width), lambda step, place: (0, 0)),
            ],
            scratch_shapes=[pltpu.VMEM((rows, width), fp32)],
        ),
        out_shape=[
            jax.ShapeDtypeStruct((SIDE, rows, units), bf16),
            jax.ShapeDtypeStruct((SIDE, rows, units), bf16),
            jax.ShapeDtypeStruct((rows, width), bf16),
        ],
        compiler_params=pltpu.CompilerParams(vmem_limit_bytes=58 * 2**20),
        name="feed_forward",
    )(line_place, normed_two, up_lines, active_grad)


def line_product(pieces, weights):
    rows, depth = pieces.shape[1:]
    width = weights.shape[2]

    def body(piece, weight, out, total):
        step = pl.program_id(0)
        product = plain_product(piece[0], weight[0])

        @pl.when(step == 0)
        def _():
            total[...] = product

        @pl.when(step > 0)
        def _():
            total[...] += product

        @pl.when(step == SIDE - 1)
        def _():
            out[...] = total[...].astype(bf16)

    return pl.pallas_call(
        body,
        grid=(SIDE,),
        in_specs=[
            pl.BlockSpec((1, rows, depth), lambda step: (step, 0, 0)),
            pl.BlockSpec((1, depth, width), lambda step: (step, 0, 0)),
        ],
        out_specs=pl.BlockSpec((rows, width), lambda step: (0, 0)),
        out_shape=jax.ShapeDtypeStruct((rows, width), bf16),
        scratch_shapes=[pltpu.VMEM((rows, width), fp32)],
        compiler_params=pltpu.CompilerParams(vmem_limit_bytes=58 * 2**20),
        name="line_product",
    )(pieces, weights)


def in_weight_grads(normed, qkv_grad, normed_two, hidden_grad):
    rows, width = normed.shape
    units = hidden_grad.shape[1]
    steps = 8

    def body(normed, qkv_grad, normed_two, hidden_grad, qkv_out, up_out):
        def summed(left, right):
            return lax.dot_general(left, right, (((0,), (0,)), ((), ())), preferred_element_type=fp32)

        qkv = summed(normed[...], qkv_grad[...])
        for plane in range(3):
            qkv_out[plane] = qkv[:, plane * HD : (plane + 1) * HD].astype(bf16)
        up_out[...] = summed(normed_two[...], hidden_grad[...]).astype(bf16)

    columns = pl.BlockSpec((rows, width // steps), lambda step: (0, step))
    return pl.pallas_call(
        body,
        grid=(steps,),
        in_specs=[
            columns,
            pl.BlockSpec((rows, 3 * HD), lambda step: (0, 0)),
            columns,
            pl.BlockSpec((rows, units), lambda step: (0, 0)),
        ],
        out_specs=[
            pl.BlockSpec((3, width // steps, HD), lambda step: (0, step, 0)),
            pl.BlockSpec((width // steps, units), lambda step: (step, 0)),
        ],
        out_shape=[
            jax.ShapeDtypeStruct((3, width, HD), bf16),
            jax.ShapeDtypeStruct((width, units), bf16),
        ],
        compiler_params=pltpu.CompilerParams(vmem_limit_bytes=58 * 2**20),
        name="in_weight_grads",
    )(normed, qkv_grad, normed_two, hidden_grad)


def widen_weights(down, up, qkv, out, small):
    steps = 8

    def body(down_in, up_in, qkv_in, out_in, small_in, down_to, up_to, qkv_to, out_to, small_to):
        def block(down_in, up_in, qkv_in, down_to, up_to, qkv_to):
            down_to[...] = down_in[...].astype(fp32)
            up_to[...] = up_in[...].astype(fp32)
            qkv_to[...] = qkv_in[...].astype(fp32)

        def rows(ref):
            return pl.BlockSpec((ref.shape[0] // steps, ref.shape[1]), lambda i: (i, 0))

        def planes(ref):
            return pl.BlockSpec(
                (ref.shape[0], ref.shape[1] // steps, ref.shape[2]), lambda i: (0, i, 0)
            )

        pltpu.emit_pipeline(
            block,
            grid=(steps,),
            in_specs=[rows(down_in), rows(up_in), planes(qkv_in)],
            out_specs=[rows(down_to), rows(up_to), planes(qkv_to)],
        )(down_in, up_in, qkv_in, down_to, up_to, qkv_to)
        out_to[...] = out_in[...].astype(fp32)
        small_to[...] = small_in[...].astype(fp32)

    hbm = pl.BlockSpec(memory_space=pltpu.HBM)
    vmem = pl.BlockSpec(memory_space=pltpu.VMEM)
    like = [down.shape, up.shape, qkv.shape, out.shape, small.shape]
    return pl.pallas_call(
        body,
        in_specs=[hbm] * 3 + [vmem] * 2,
        out_specs=[hbm] * 3 + [vmem] * 2,
        out_shape=[jax.ShapeDtypeStruct(shape, fp32) for shape in like],
        compiler_params=pltpu.CompilerParams(vmem_limit_bytes=58 * 2**20),
        name="widen_weights",
    )(down, up, qkv, out, small)


def widen_lines(whole):
    lines, rows, width = whole.shape
    rows -= 16
    part = 2

    def body(whole_in, whole_to):
        def block(whole_in, whole_to):
            whole_to[...] = whole_in[0].astype(fp32)

        pltpu.emit_pipeline(
            block,
            grid=(lines * part,),
            in_specs=[
                pl.BlockSpec((1, rows // part, width), lambda i: (i // part, i % part, 0))
            ],
            out_specs=[pl.BlockSpec((rows // part, width), lambda i: (i, 0))],
        )(whole_in, whole_to)

    hbm = pl.BlockSpec(memory_space=pltpu.HBM)
    return pl.pallas_call(
        body,
        in_specs=[hbm],
        out_specs=hbm,
        out_shape=jax.ShapeDtypeStruct((lines * rows, width), fp32),
        compiler_params=pltpu.CompilerParams(vmem_limit_bytes=58 * 2**20),
        name="widen_lines",
    )(whole)


def per_device(
    layer_input,
    ln1_gain,
    ln1_bias,
    qkv_weight,
    qv_bias,
    out_weight,
    out_bias,
    ln2_gain,
    ln2_bias,
    up_weight,
    up_bias,
    down_weight,
    down_bias,
    cotangent,
    group_table,
    group_counts,
    block_order,
):
    width = layer_input.shape[-1]
    rows = layer_input.shape[1]
    local = qkv_weight.shape[2]
    hidden_local = up_weight.shape[1]
    block_rows = rows // 2
    line_rows = rows // SIDE
    own_rows = line_rows // SIDE
    grp_at = lax.axis_index("grp")
    tp_at = lax.axis_index("tp")
    ctx_at = lax.axis_index("ctx")
    even = grp_at % 2 == 0
    a_at = jnp.where(even, tp_at % SIDE, tp_at // SIDE)
    b_at = jnp.where(even, tp_at // SIDE, tp_at % SIDE)
    line_start = a_at * line_rows
    own_start = line_start + b_at * own_rows

    always = ctx_at < N_CTX

    def stage(work, *operands):
        shapes = jax.eval_shape(work, *operands)

        def empty(*operands):
            return jax.tree.map(lambda like: jnp.zeros(like.shape, like.dtype), shapes)

        return lax.cond(always, work, empty, *operands)

    gain_one = ln1_gain.astype(fp32)
    bias_one = ln1_bias.astype(fp32)
    gain_two = ln2_gain.astype(fp32)
    bias_two = ln2_bias.astype(fp32)
    tokens = layer_input.reshape(rows, width)
    cot = cotangent.reshape(rows, width)
    own_tokens = lax.dynamic_slice_in_dim(tokens, own_start, own_rows, 0).astype(fp32)
    own_cot = lax.dynamic_slice_in_dim(cot, own_start, own_rows, 0).astype(fp32)

    shares = position_shares(group_table, group_counts)
    grp_slots = jnp.arange(shares.shape[0], dtype=jnp.int32)
    my_share = jnp.sum(jnp.where(grp_slots == grp_at, shares, jnp.zeros_like(shares)))
    column = jnp.arange(block_order.shape[0], dtype=jnp.int32)
    slots = jnp.arange(4, dtype=jnp.int32)
    slots = jnp.where(slots < 2, ctx_at * 2 + slots, (1 - ctx_at) * 2 + slots - 2)
    places = jnp.sum(
        jnp.where(slots[:, None] == column[None, :], block_order[None, :], 0), axis=1
    )
    out_lines = join_pieces(out_weight, a_at, GROUPS_A)
    up_lines = gather_lines(up_weight, GROUPS_A)
    qkv_turned = qkv_weight.transpose(1, 2, 0).reshape(3 * local, width)
    qkv_lines = gather_lines(qkv_turned, GROUPS_A)
    first_normed = layer_norm(tokens.astype(fp32), gain_one, bias_one).astype(bf16)
    mixed = jnp.einsum("rd,cd->rc", first_normed, qkv_turned, preferred_element_type=fp32)
    query = (mixed[:, :local] + qv_bias[0].astype(fp32)).astype(bf16)
    pair = jnp.stack(
        [mixed[:, local : 2 * local], mixed[:, 2 * local :] + qv_bias[1].astype(fp32)]
    ).astype(bf16)
    swap_ctx = [(0, 1), (1, 0)]
    pair_other = lax.ppermute(pair, "ctx", swap_ctx)

    own_part = own_keys_forward(places, query, pair)
    pair_other, out_lines, *own_part = lax.optimization_barrier(
        (pair_other, out_lines, *own_part)
    )
    heads, level = other_keys_forward(places, query, pair_other, *own_part)

    heads_line = exchange(heads.reshape(SIDE, line_rows, local), GROUPS_A)

    cot = after(cot, heads)
    grad_out = cot.astype(fp32) * my_share
    grad_low = grad_out.astype(bf16)
    down_bias_grad = jnp.sum(grad_out, axis=0)
    active_grad = jnp.einsum("rd,fd->rf", grad_low, down_weight, preferred_element_type=fp32)
    bias_rows = jnp.broadcast_to(up_bias[None, None], (SIDE, 16, hidden_local))
    active_grad = jnp.concatenate(
        [active_grad.astype(bf16).reshape(SIDE, line_rows, hidden_local), bias_rows], axis=1
    )
    heads_line, active_grad, down_bias_grad = lax.optimization_barrier(
        (heads_line, active_grad, down_bias_grad)
    )
    active_grad = jnp.stack(
        arriving(
            lambda step: lax.dynamic_index_in_dim(
                active_grad, (a_at + step) % SIDE, 0, keepdims=False
            ),
            GROUPS_A,
        )
    )

    heads_line = heads_line.transpose(1, 0, 2).reshape(line_rows, SIDE * local)
    partial_out = jnp.dot(heads_line, out_lines, preferred_element_type=fp32).astype(bf16)
    partial_out = exchange(partial_out.reshape(SIDE, own_rows, width), GROUPS_B)
    normed = layer_norm(after(tokens, heads_line).astype(fp32), gain_one, bias_one).astype(bf16)
    partial_out, active_grad, normed = lax.optimization_barrier((partial_out, active_grad, normed))
    middle = own_tokens + jnp.sum(partial_out.astype(fp32), axis=0) + out_bias.astype(fp32)
    normed_two_own = layer_norm(middle, gain_two, bias_two).astype(bf16)
    normed_two = spread(normed_two_own, GROUPS_B).reshape(line_rows, width)

    active, hidden_grad, normed_two_grad = feed_forward(
        a_at.astype(jnp.int32)[None], normed_two, up_lines, active_grad
    )
    normed_two_grad, active, normed_two = lax.optimization_barrier(
        (normed_two_grad, active, normed_two)
    )

    normed_two_rows = gather_lines(normed_two, GROUPS_A)

    def norm_stage(normed_two_grad, active, middle, own_cot_share):
        normed_two_grad = exchange(normed_two_grad.reshape(SIDE, own_rows, width), GROUPS_B)
        active_own = swap_pieces(active, a_at, GROUPS_A).reshape(rows, hidden_local)
        normed_two_grad = jnp.sum(normed_two_grad.astype(fp32), axis=0)
        norm_value, norm_pull = jax.vjp(layer_norm, middle, gain_two, bias_two)
        middle_part, ln2_gain_part, ln2_bias_part = norm_pull(normed_two_grad)
        middle_grad = own_cot_share + middle_part
        middle_low = spread(middle_grad.astype(bf16), GROUPS_B).reshape(line_rows, width)
        partial_mlp = jnp.dot(active_own, down_weight, preferred_element_type=fp32).astype(bf16)
        vector_two = jnp.stack([ln2_gain_part, ln2_bias_part, jnp.sum(middle_grad, axis=0)])
        return middle_grad, middle_low, vector_two, active_own, partial_mlp

    middle_grad, middle_low, vector_two, active_own, partial_mlp = stage(
        norm_stage, normed_two_grad, active, middle, own_cot * my_share
    )
    middle_low, qkv_lines, normed_two_rows = lax.optimization_barrier(
        (middle_low, qkv_lines, normed_two_rows)
    )
    partial_mlp = lax.psum_scatter(
        partial_mlp, EVERY, scatter_dimension=0, tiled=True, axis_index_groups=GROUPS_A
    )

    def attention_stage(middle_low, hidden_grad, heads_line, active_own, grad_low):
        head_grad = jnp.einsum("rd,fd->rf", middle_low, out_lines, preferred_element_type=fp32)
        head_grad = head_grad.astype(bf16).reshape(line_rows, SIDE, local).transpose(1, 0, 2)
        head_grad = exchange(head_grad, GROUPS_A).reshape(rows, local)
        head_grad, hidden_grad, heads_line = lax.optimization_barrier(
            (head_grad, hidden_grad, heads_line)
        )
        hidden_grad_own = exchange(hidden_grad, GROUPS_A).reshape(rows, hidden_local)
        query_grad, pair_other_grad, slack = other_keys_backward(
            places, query, pair_other, head_grad, heads, level
        )
        pair_from = lax.ppermute(pair_other_grad, "ctx", swap_ctx)
        active_own = after(active_own, pair_other_grad)
        out_weight_grad = jnp.einsum(
            "rf,rd->fd", heads_line, middle_low, preferred_element_type=fp32
        ).astype(bf16)
        out_weight_grad = sum_pieces(out_weight_grad, a_at, GROUPS_A)
        query_grad, pair_grad = own_keys_backward(
            places, query, pair, head_grad, level, slack, query_grad
        )
        down_weight_grad = jnp.einsum(
            "rf,rd->fd", active_own, grad_low, preferred_element_type=fp32
        ).astype(bf16)
        up_bias_grad = jnp.sum(hidden_grad_own.astype(fp32), axis=0)
        pair_from, pair_grad, query_grad, down_weight_grad, up_bias_grad = (
            lax.optimization_barrier(
                (pair_from, pair_grad, query_grad, down_weight_grad, up_bias_grad)
            )
        )
        pair_grad = (pair_grad + pair_from.astype(fp32)).astype(bf16)
        qkv_grad = jnp.concatenate([query_grad, pair_grad[0], pair_grad[1]], axis=1)
        return qkv_grad, down_weight_grad, hidden_grad_own, out_weight_grad, up_bias_grad

    qkv_grad, down_weight_grad, hidden_grad_own, out_weight_grad, up_bias_grad = stage(
        attention_stage, middle_low, hidden_grad, heads_line, active_own, grad_low
    )
    qkv_grad_line = exchange(qkv_grad.reshape(SIDE, line_rows, 3 * local), GROUPS_A)
    qkv_weight_grad, up_weight_grad = in_weight_grads(
        normed, qkv_grad, normed_two_rows.reshape(rows, width), hidden_grad_own
    )
    qkv_bias_grad = jnp.sum(qkv_grad.astype(fp32), axis=0)
    small_rows = jnp.concatenate(
        [
            down_bias_grad[None],
            jnp.concatenate(
                [up_bias_grad, qkv_bias_grad, jnp.zeros((width - hidden_local - 3 * local,), fp32)]
            )[None],
            jnp.zeros((14, width), fp32),
        ]
    ).astype(bf16)
    out_weight_grad = out_weight_grad.astype(bf16)
    weight_grads = (down_weight_grad, up_weight_grad, qkv_weight_grad, out_weight_grad, small_rows)
    output_own = middle + sum_pieces(partial_mlp, b_at, GROUPS_B)
    output_own = (output_own + down_bias.astype(fp32)).astype(bf16)
    qkv_grad_line, output_own, *weight_grads = lax.optimization_barrier(
        (qkv_grad_line, output_own) + weight_grads
    )
    weight_grads = lax.psum(tuple(weight_grads), ("grp", "ctx"))

    def finish(qkv_grad_line, output_own, qkv_lines, middle_grad, own_tokens, vector_two):
        output_line = join_pieces(output_own, b_at, GROUPS_B)
        normed_grad = line_product(qkv_grad_line, qkv_lines)
        normed_grad, output_line = lax.optimization_barrier((normed_grad, output_line))
        normed_grad = exchange(normed_grad.reshape(SIDE, own_rows, width), GROUPS_B)
        layer_output = join_pieces(output_line, a_at, GROUPS_A).reshape(1, rows, width)
        normed_grad = jnp.sum(normed_grad.astype(fp32), axis=0)
        first_value, first_pull = jax.vjp(layer_norm, own_tokens, gain_one, bias_one)
        input_part, ln1_gain_part, ln1_bias_part = first_pull(normed_grad)
        input_grad_own = (middle_grad + input_part).astype(bf16)
        vector_part = jnp.concatenate(
            [
                ln1_gain_part[None],
                ln1_bias_part[None],
                vector_two,
                jnp.zeros((11, width), fp32),
            ]
        ).astype(bf16)
        line = spread(jnp.concatenate([input_grad_own, vector_part]), GROUPS_B)
        line, layer_output = lax.optimization_barrier((line, layer_output))
        vectors = jnp.sum(line[:, own_rows:].astype(fp32), axis=0).astype(bf16)
        line = jnp.concatenate([line[:, :own_rows].reshape(line_rows, width), vectors])
        return layer_output, spread(line, GROUPS_A)

    layer_output, whole = stage(
        finish, qkv_grad_line, output_own, qkv_lines, middle_grad, own_tokens, vector_two
    )
    vectors = jnp.sum(whole[:, line_rows : line_rows + 8].astype(fp32), axis=0)
    vectors = vectors + lax.ppermute(vectors, EVERY, swap_all(1, 0))
    come = lax.ppermute(vectors, EVERY, swap_all(2, 0))
    come, input_grad = lax.optimization_barrier((come, widen_lines(after(whole, vectors))))
    vectors = vectors + come
    come = lax.ppermute(vectors, EVERY, swap_all(0, 1))
    weight_grads = lax.optimization_barrier((vectors, *weight_grads))[1:]
    come, *widened = lax.optimization_barrier((come, *widen_weights(*weight_grads)))
    vectors = vectors + come
    down_weight_grad, up_weight_grad, qkv_weight_grad, out_weight_grad, small_rows = widened
    return (
        layer_output,
        input_grad.reshape(1, rows, width),
        vectors[0],
        vectors[1],
        qkv_weight_grad.transpose(1, 0, 2),
        small_rows[1, hidden_local : hidden_local + 3 * local].reshape(3, local)[::2],
        out_weight_grad,
        vectors[4],
        vectors[2],
        vectors[3],
        up_weight_grad,
        small_rows[1, :hidden_local],
        down_weight_grad,
        small_rows[0],
    )


def solution(mesh):
    placed = (
        P("grp", "ctx", None),
        P(),
        P(),
        P(None, None, "tp"),
        P(None, "tp"),
        P("tp", None),
        P(),
        P(),
        P(),
        P(None, "tp"),
        P("tp"),
        P("tp", None),
        P(),
        P("grp", "ctx", None),
        P(),
        P(),
        P(),
    )
    return jax.shard_map(
        per_device,
        mesh=mesh,
        in_specs=placed,
        out_specs=(
            P("grp", "ctx", None),
            P("grp", "ctx", None),
            P(),
            P(),
            P(None, None, "tp"),
            P(None, "tp"),
            P("tp", None),
            P(),
            P(),
            P(),
            P(None, "tp"),
            P("tp"),
            P("tp", None),
            P(),
        ),
        check_vma=False,
    )
```

```python
import math

import jax
import jax.numpy as jnp
from jax import lax
from jax.experimental import pallas as pl
from jax.experimental.pallas import tpu as pltpu
from jax.sharding import PartitionSpec as P

HD = 128
GROUPS = 3
TILE = 256
SCALE = 1.0 / math.sqrt(HD)
SCALE_TWO = SCALE * math.log2(math.e)
EVERY = ("grp", "tp", "ctx")
N_GRP, N_TP, N_CTX, SIDE = 4, 16, 2, 4
fp32 = jnp.float32
bf16 = jnp.bfloat16


def device_id(grp, tx, tz, ctx):
    return (grp * N_TP + tx * SIDE + tz) * N_CTX + ctx


def line_groups(first_axis):
    groups = []
    for grp in range(N_GRP):
        for ctx in range(N_CTX):
            for fixed in range(SIDE):
                along_z = (grp % 2 == 0) == first_axis
                groups.append(
                    [
                        device_id(grp, fixed, i, ctx) if along_z else device_id(grp, i, fixed, ctx)
                        for i in range(SIDE)
                    ]
                )
    return groups


GROUPS_A = line_groups(True)
GROUPS_B = line_groups(False)


def swap_lines(groups, bit):
    return [(line[i], line[i ^ bit]) for line in groups for i in range(SIDE)]


def swap_all(grp_bit, ctx_bit):
    return [
        (device_id(g, x, z, c), device_id(g ^ grp_bit, x, z, c ^ ctx_bit))
        for g in range(N_GRP)
        for x in range(SIDE)
        for z in range(SIDE)
        for c in range(N_CTX)
    ]


def exchange(pieces, groups):
    return lax.all_to_all(pieces, EVERY, 0, 0, axis_index_groups=groups)


def spread(piece, groups):
    return exchange(jnp.broadcast_to(piece[None], (SIDE,) + piece.shape), groups)


def turn(groups, step):
    return [(line[i], line[(i + step) % SIDE]) for line in groups for i in range(SIDE)]


def sum_pieces(partial, place, groups):
    piece_rows = partial.shape[0] // SIDE
    total = lax.dynamic_slice_in_dim(partial, place * piece_rows, piece_rows, 0).astype(fp32)
    for step in (1, 3, 2):
        goes = (place + step) % SIDE
        piece = lax.dynamic_slice_in_dim(partial, goes * piece_rows, piece_rows, 0)
        total = total + lax.ppermute(piece, EVERY, turn(groups, step)).astype(fp32)
    return total


def ring(piece, split, groups):
    before = lax.ppermute(piece, EVERY, turn(groups, 1))
    behind = lax.ppermute(piece, EVERY, turn(groups, 3))
    top = lax.ppermute(before[:split], EVERY, turn(groups, 1))
    bottom = lax.ppermute(behind[split:], EVERY, turn(groups, 3))
    return piece, before, behind, top, bottom


def join_pieces(piece, place, groups):
    piece_rows, width = piece.shape
    whole = jnp.zeros((SIDE * piece_rows, width), piece.dtype)
    whole = lax.dynamic_update_slice_in_dim(whole, piece, place * piece_rows, 0)
    for step in (1, 3, 2):
        come = lax.ppermute(piece, EVERY, turn(groups, step))
        origin = (place + SIDE - step) % SIDE
        whole = lax.dynamic_update_slice_in_dim(whole, come, origin * piece_rows, 0)
    return whole


def arriving(pieces, groups):
    come = {step: lax.ppermute(pieces(step), EVERY, turn(groups, step)) for step in (1, 3, 2)}
    return [pieces(0), come[1], come[2], come[3]]


def after(value, *earlier):
    return lax.optimization_barrier((value,) + earlier)[0]


def gather_lines(piece, groups):
    return lax.all_gather(piece, EVERY, axis=0, axis_index_groups=groups)


def layer_norm(values, gain_vec, bias_vec):
    average = jnp.mean(values, axis=-1, keepdims=True)
    centred = values - average
    variance = jnp.mean(centred * centred, axis=-1, keepdims=True)
    return centred * lax.rsqrt(variance + 1e-05) * gain_vec + bias_vec


def position_shares(group_table, group_counts):
    member = (group_table[:, None] == jnp.arange(GROUPS, dtype=jnp.int32)[None, :]).astype(fp32)
    holders = jnp.sum(member, axis=0)
    counts_float = group_counts.astype(fp32)
    per_group = counts_float / (holders * jnp.sum(counts_float))
    return group_table.shape[0] * jnp.sum(member * per_group[None, :], axis=1)


def turned_product(left, right):
    return lax.dot_general(left, right, (((1,), (1,)), ((), ())), preferred_element_type=fp32)


def plain_product(left, right):
    return lax.dot_general(left, right, (((1,), (0,)), ((), ())), preferred_element_type=fp32)


def attention_call(body, name, scratch, like, places, *operands):
    return pl.pallas_call(
        body,
        in_specs=[pl.BlockSpec(memory_space=pltpu.SMEM)]
        + [pl.BlockSpec(memory_space=pltpu.VMEM)] * len(operands),
        out_specs=[pl.BlockSpec(memory_space=pltpu.VMEM)] * len(like),
        out_shape=[jax.ShapeDtypeStruct(shape, kind) for shape, kind in like],
        scratch_shapes=[pltpu.VMEM(shape, fp32) for shape in scratch],
        compiler_params=pltpu.CompilerParams(vmem_limit_bytes=40 * 2**20),
        name=name,
    )(places, *operands)


def own_keys_forward(places, query, pair):
    rows = query.shape[0]
    block = rows // 2

    def body(places, query, pair, top, total, mixed):
        key, value = pair.at[0], pair.at[1]
        for slot in range(2):
            for start in range(slot * block, (slot + 1) * block, TILE):
                last = start + TILE
                keys = slice(slot * block, last)
                scores = turned_product(query[start:last], key[keys]) * SCALE_TWO
                place_q = lax.broadcasted_iota(jnp.int32, scores.shape, 0) + start
                place_k = lax.broadcasted_iota(jnp.int32, scores.shape, 1) + slot * block
                scores = jnp.where(place_q >= place_k, scores, -1e30)
                peak = jnp.max(scores, axis=1, keepdims=True)
                weights = jnp.exp2(scores - peak)
                top[start:last] = peak
                total[start:last] = jnp.sum(weights, axis=1, keepdims=True)
                mixed[start:last] = plain_product(weights.astype(bf16), value[keys])
        for slot in range(2):
            other = 1 - slot

            @pl.when(places[slot] > places[other])
            def _():
                add_keys(query, key, value, top, total, mixed, slot, other, block)

    like = [((rows, 1), fp32), ((rows, 1), fp32), ((rows, HD), fp32)]
    return attention_call(body, "own_keys_forward", [], like, places, query, pair)


def add_keys(query, key, value, top, total, mixed, slot, key_slot, block):
    keys = slice(key_slot * block, (key_slot + 1) * block)
    for start in range(slot * block, (slot + 1) * block, TILE):
        here = slice(start, start + TILE)
        scores = turned_product(query[here], key[keys]) * SCALE_TWO
        peak = jnp.maximum(top[here], jnp.max(scores, axis=1, keepdims=True))
        fade = jnp.exp2(top[here] - peak)
        weights = jnp.exp2(scores - peak)
        top[here] = peak
        total[here] = total[here] * fade + jnp.sum(weights, axis=1, keepdims=True)
        mixed[here] = mixed[here] * fade + plain_product(weights.astype(bf16), value[keys])


def other_keys_forward(places, query, pair, top, total, mixed):
    rows = query.shape[0]
    block = rows // 2

    def body(places, query, pair, top_in, total_in, mixed_in, heads, level, top, total, mixed):
        key, value = pair.at[0], pair.at[1]
        top[...] = top_in[...]
        total[...] = total_in[...]
        mixed[...] = mixed_in[...]
        for slot in range(2):
            for key_slot in range(2):

                @pl.when(places[slot] > places[2 + key_slot])
                def _():
                    add_keys(query, key, value, top, total, mixed, slot, key_slot, block)

        for start in range(0, rows, TILE):
            here = slice(start, start + TILE)
            heads[here] = (mixed[here] / total[here]).astype(bf16)
            logs = top[here] + jnp.log2(total[here])
            level[:, here] = jnp.broadcast_to(logs, (TILE, HD)).T[:8]

    like = [((rows, HD), bf16), ((8, rows), fp32)]
    scratch = [(rows, 1), (rows, 1), (rows, HD)]
    return attention_call(
        body, "other_keys_forward", scratch, like, places, query, pair, top, total, mixed
    )


def pair_backward(
    query, key, value, head_grad, level, slack, query_grad, key_grad, value_grad, slot, key_slot, block, own
):
    for start in range(key_slot * block, (key_slot + 1) * block, TILE):
        keys = slice(start, start + TILE)
        first = start if own else slot * block
        rows = slice(first, (slot + 1) * block)
        scores = turned_product(key[keys], query[rows]) * SCALE_TWO - level[:1, rows]
        if own:
            place_k = lax.broadcasted_iota(jnp.int32, scores.shape, 0)
            place_q = lax.broadcasted_iota(jnp.int32, scores.shape, 1)
            scores = jnp.where(place_q >= place_k, scores, -1e30)
        probs = jnp.exp2(scores)
        value_grad[keys] += plain_product(probs.astype(bf16), head_grad[rows])
        prob_grad = turned_product(value[keys], head_grad[rows]) - slack[:1, rows]
        score_grad = (probs * prob_grad).astype(bf16)
        key_grad[keys] += plain_product(score_grad, query[rows])
        query_grad[rows] += lax.dot_general(
            score_grad, key[keys], (((0,), (0,)), ((), ())), preferred_element_type=fp32
        )


def other_keys_backward(places, query, pair, head_grad, heads, level):
    rows = query.shape[0]
    block = rows // 2

    def body(
        places, query, pair, head_grad, heads, level, query_grad, pair_grad, slack, key_sum, value_sum
    ):
        key, value = pair.at[0], pair.at[1]
        query_grad[...] = jnp.zeros(query_grad.shape, fp32)
        key_sum[...] = jnp.zeros(key_sum.shape, fp32)
        value_sum[...] = jnp.zeros(value_sum.shape, fp32)
        for start in range(0, rows, TILE):
            here = slice(start, start + TILE)
            both = head_grad[here].astype(fp32) * heads[here].astype(fp32)
            both = jnp.sum(both, axis=1, keepdims=True)
            slack[:, here] = jnp.broadcast_to(both, (TILE, HD)).T[:8]
        for slot in range(2):
            for key_slot in range(2):

                @pl.when(places[slot] > places[2 + key_slot])
                def _():
                    pair_backward(
                        query, key, value, head_grad, level, slack,
                        query_grad, key_sum, value_sum, slot, key_slot, block, False,
                    )

        pair_grad[0] = (key_sum[...] * SCALE).astype(bf16)
        pair_grad[1] = value_sum[...].astype(bf16)

    like = [((rows, HD), fp32), ((2, rows, HD), bf16), ((8, rows), fp32)]
    return attention_call(
        body, "other_keys_backward", [(rows, HD)] * 2, like,
        places, query, pair, head_grad, heads, level,
    )


def own_keys_backward(places, query, pair, head_grad, level, slack, query_grad):
    rows = query.shape[0]
    block = rows // 2

    def body(
        places, query, pair, head_grad, level, slack, query_in, query_grad, pair_grad, query_sum
    ):
        key, value = pair.at[0], pair.at[1]
        query_sum[...] = query_in[...]
        pair_grad[...] = jnp.zeros(pair_grad.shape, fp32)
        key_sum = pair_grad.at[0]
        value_sum = pair_grad.at[1]
        for slot in range(2):
            pair_backward(
                query, key, value, head_grad, level, slack,
                query_sum, key_sum, value_sum, slot, slot, block, True,
            )
        for slot in range(2):

            @pl.when(places[slot] > places[1 - slot])
            def _():
                pair_backward(
                    query, key, value, head_grad, level, slack,
                    query_sum, key_sum, value_sum, slot, 1 - slot, block, False,
                )

        pair_grad[0] = pair_grad[0] * SCALE
        query_grad[...] = (query_sum[...] * SCALE).astype(bf16)

    like = [((rows, HD), bf16), ((2, rows, HD), fp32)]
    return attention_call(
        body, "own_keys_backward", [(rows, HD)], like,
        places, query, pair, head_grad, level, slack, query_grad,
    )


def feed_forward(line_place, normed_two, up_lines, active_grad):
    rows, width = normed_two.shape
    units = up_lines.shape[2]
    bend = math.sqrt(2.0 / math.pi)

    def body(place, normed_two, up, grad, both, back, total):
        step = pl.program_id(0)
        hidden = plain_product(normed_two[...], up[0])
        hidden = hidden + grad[0, rows : rows + 1].astype(fp32)
        square = hidden * hidden
        bent = jnp.tanh(bend * hidden * (1.0 + 0.044715 * square))
        half = 0.5 * (1.0 + bent)
        both[0, :, :units] = (hidden * half).astype(bf16)
        slope = half + (0.5 * bend) * hidden * (1.0 - bent * bent) * (1.0 + 0.134145 * square)
        low = (slope * grad[0, :rows].astype(fp32)).astype(bf16)
        both[0, :, units:] = low
        product = turned_product(low, up[0])

        @pl.when(step == 0)
        def _():
            total[...] = product

        @pl.when(step > 0)
        def _():
            total[...] += product

        @pl.when(step == SIDE - 1)
        def _():
            back[...] = total[...].astype(bf16)

    def origin(step, place):
        return ((place[0] + SIDE - step) % SIDE, 0, 0)

    return pl.pallas_call(
        body,
        grid_spec=pltpu.PrefetchScalarGridSpec(
            num_scalar_prefetch=1,
            grid=(SIDE,),
            in_specs=[
                pl.BlockSpec((rows, width), lambda step, place: (0, 0)),
                pl.BlockSpec((1, width, units), origin),
                pl.BlockSpec((1, rows + 16, units), lambda step, place: (step, 0, 0)),
            ],
            out_specs=[
                pl.BlockSpec((1, rows, 2 * units), origin),
                pl.BlockSpec((rows, width), lambda step, place: (0, 0)),
            ],
            scratch_shapes=[pltpu.VMEM((rows, width), fp32)],
        ),
        out_shape=[
            jax.ShapeDtypeStruct((SIDE, rows, 2 * units), bf16),
            jax.ShapeDtypeStruct((rows, width), bf16),
        ],
        compiler_params=pltpu.CompilerParams(vmem_limit_bytes=58 * 2**20),
        name="feed_forward",
    )(line_place, normed_two, up_lines, active_grad)


def line_product(pieces, weights):
    rows, depth = pieces.shape[1:]
    width = weights.shape[2]

    def body(piece, weight, out, total):
        step = pl.program_id(0)
        product = plain_product(piece[0], weight[0])

        @pl.when(step == 0)
        def _():
            total[...] = product

        @pl.when(step > 0)
        def _():
            total[...] += product

        @pl.when(step == SIDE - 1)
        def _():
            out[...] = total[...].astype(bf16)

    return pl.pallas_call(
        body,
        grid=(SIDE,),
        in_specs=[
            pl.BlockSpec((1, rows, depth), lambda step: (step, 0, 0)),
            pl.BlockSpec((1, depth, width), lambda step: (step, 0, 0)),
        ],
        out_specs=pl.BlockSpec((rows, width), lambda step: (0, 0)),
        out_shape=jax.ShapeDtypeStruct((rows, width), bf16),
        scratch_shapes=[pltpu.VMEM((rows, width), fp32)],
        compiler_params=pltpu.CompilerParams(vmem_limit_bytes=58 * 2**20),
        name="line_product",
    )(pieces, weights)


def down_product(line_place, pieces, down_weight):
    part = pieces[0].shape[0]
    units, width = down_weight.shape

    def body(place, *refs):
        pieces, (weight, out) = refs[:SIDE], refs[SIDE:]
        for index in range(SIDE):

            @pl.when(pl.program_id(0) == index)
            def _():
                out[...] = plain_product(pieces[index][...], weight[...]).astype(bf16)

    return pl.pallas_call(
        body,
        grid_spec=pltpu.PrefetchScalarGridSpec(
            num_scalar_prefetch=1,
            grid=(SIDE,),
            in_specs=[pl.BlockSpec((part, units), lambda step, place: (0, 0))] * SIDE
            + [pl.BlockSpec((units, width), lambda step, place: (0, 0))],
            out_specs=pl.BlockSpec(
                (part, width), lambda step, place: ((place[0] + SIDE - step) % SIDE, 0)
            ),
        ),
        out_shape=jax.ShapeDtypeStruct((SIDE * part, width), bf16),
        compiler_params=pltpu.CompilerParams(vmem_limit_bytes=40 * 2**20),
        name="down_product",
    )(line_place, *pieces, down_weight)


def turned_grad(line_place, matrix, pieces, half):
    rows, width = matrix.shape
    part = rows // SIDE
    units = pieces[0].shape[1] // 2
    steps = 8

    def body(place, matrix, *refs):
        pieces, (out, sums) = refs[:SIDE], refs[SIDE:]
        total = None
        for index in range(SIDE):
            start = pl.multiple_of((place[0] + SIDE - index) % SIDE * part, part)
            product = lax.dot_general(
                matrix[pl.ds(start, part)],
                pieces[index][...],
                (((0,), (0,)), ((), ())),
                preferred_element_type=fp32,
            )
            total = product if total is None else total + product
        out[...] = total.astype(bf16)

        @pl.when(pl.program_id(0) == 0)
        def _():
            added = [jnp.sum(piece[...].astype(fp32), axis=0, keepdims=True) for piece in pieces]
            sums[...] = added[0] + added[1] + added[2] + added[3]

    return pl.pallas_call(
        body,
        grid_spec=pltpu.PrefetchScalarGridSpec(
            num_scalar_prefetch=1,
            grid=(steps,),
            in_specs=[pl.BlockSpec((rows, width // steps), lambda step, place: (0, step))]
            + [pl.BlockSpec((part, units), lambda step, place: (0, half))] * SIDE,
            out_specs=[
                pl.BlockSpec((width // steps, units), lambda step, place: (step, 0)),
                pl.BlockSpec((1, units), lambda step, place: (0, 0)),
            ],
        ),
        out_shape=[
            jax.ShapeDtypeStruct((width, units), bf16),
            jax.ShapeDtypeStruct((1, units), fp32),
        ],
        compiler_params=pltpu.CompilerParams(vmem_limit_bytes=58 * 2**20),
        name="turned_grad",
    )(line_place, matrix, *pieces)


def projection_grad(normed, qkv_grad):
    rows, width = normed.shape
    steps = 8

    def body(normed, qkv_grad, out, sums):
        total = lax.dot_general(
            normed[...], qkv_grad[...], (((0,), (0,)), ((), ())), preferred_element_type=fp32
        )
        for plane in range(3):
            out[plane] = total[:, plane * HD : (plane + 1) * HD].astype(bf16)

        @pl.when(pl.program_id(0) == 0)
        def _():
            sums[...] = jnp.sum(qkv_grad[...].astype(fp32), axis=0, keepdims=True)

    return pl.pallas_call(
        body,
        grid=(steps,),
        in_specs=[
            pl.BlockSpec((rows, width // steps), lambda step: (0, step)),
            pl.BlockSpec((rows, 3 * HD), lambda step: (0, 0)),
        ],
        out_specs=[
            pl.BlockSpec((3, width // steps, HD), lambda step: (0, step, 0)),
            pl.BlockSpec((1, 3 * HD), lambda step: (0, 0)),
        ],
        out_shape=[
            jax.ShapeDtypeStruct((3, width, HD), bf16),
            jax.ShapeDtypeStruct((1, 3 * HD), fp32),
        ],
        compiler_params=pltpu.CompilerParams(vmem_limit_bytes=58 * 2**20),
        name="projection_grad",
    )(normed, qkv_grad)


def norm_call(body, name, parts, rows_in, vectors_in, outs, scratch=(), scalars=()):
    tile = 16
    rows, width = parts.shape[1:]

    def by_rows(shape):
        if len(shape) == 3:
            return pl.BlockSpec((shape[0], tile, shape[2]), lambda step: (0, step, 0))
        return pl.BlockSpec((tile, shape[1]), lambda step: (step, 0))

    def whole(shape):
        return pl.BlockSpec(shape, lambda step: (0,) * len(shape))

    return pl.pallas_call(
        body,
        grid=(rows // tile,),
        in_specs=[pl.BlockSpec(memory_space=pltpu.SMEM)] * len(scalars)
        + [by_rows(parts.shape)]
        + [by_rows(operand.shape) for operand in rows_in]
        + [whole(operand.shape) for operand in vectors_in],
        out_specs=[by_rows(shape) if tiled else whole(shape) for shape, _, tiled in outs],
        out_shape=[jax.ShapeDtypeStruct(shape, kind) for shape, kind, _ in outs],
        scratch_shapes=[pltpu.VMEM(shape, fp32) for shape in scratch],
        compiler_params=pltpu.CompilerParams(vmem_limit_bytes=24 * 2**20),
        name=name,
    )(*scalars, parts, *rows_in, *vectors_in)


def summed_parts(parts):
    return (parts[0].astype(fp32) + parts[1].astype(fp32)) + (
        parts[2].astype(fp32) + parts[3].astype(fp32)
    )


def normalised(values):
    centred = values - jnp.mean(values, axis=1, keepdims=True)
    scale = lax.rsqrt(jnp.mean(centred * centred, axis=1, keepdims=True) + 1e-05)
    return centred * scale, scale


def norm_backward(values, grad, gain):
    unit, scale = normalised(values)
    scaled = grad * gain
    along = jnp.mean(scaled * unit, axis=1, keepdims=True)
    inner = scale * (scaled - jnp.mean(scaled, axis=1, keepdims=True) - unit * along)
    return inner, jnp.sum(grad * unit, axis=0, keepdims=True), jnp.sum(grad, axis=0, keepdims=True)


def second_norm(parts, tokens, out_bias, gain, bias):
    rows, width = tokens.shape

    def body(parts, tokens, out_bias, gain, bias, middle, normed):
        values = tokens[...].astype(fp32) + summed_parts(parts) + out_bias[...]
        middle[...] = values
        low = (normalised(values)[0] * gain[...] + bias[...]).astype(bf16)
        for line in range(SIDE):
            normed[line] = low

    outs = [((rows, width), fp32, True), ((SIDE, rows, width), bf16, True)]
    return norm_call(body, "second_norm", parts, [tokens], [out_bias, gain, bias], outs)


def second_norm_backward(share, parts, middle, cot, gain):
    rows, width = middle.shape

    def body(share, parts, middle, cot, gain, middle_grad, low, vectors):
        inner, gain_part, bias_part = norm_backward(middle[...], summed_parts(parts), gain[...])
        grad = cot[...].astype(fp32) * share[0] + inner
        middle_grad[...] = grad
        for line in range(SIDE):
            low[line] = grad.astype(bf16)

        @pl.when(pl.program_id(0) == 0)
        def _():
            vectors[...] = jnp.zeros(vectors.shape, fp32)

        vectors[0:1] += gain_part
        vectors[1:2] += bias_part
        vectors[2:3] += jnp.sum(grad, axis=0, keepdims=True)

    outs = [
        ((rows, width), fp32, True),
        ((SIDE, rows, width), bf16, True),
        ((8, width), fp32, False),
    ]
    return norm_call(
        body, "second_norm_backward", parts, [middle, cot], [gain], outs, scalars=[share]
    )


def first_norm_backward(parts, tokens, middle_grad, gain, vector_two):
    rows, width = tokens.shape

    def body(parts, tokens, middle_grad, gain, vector_two, line, vectors):
        step = pl.program_id(0)
        values = tokens[...].astype(fp32)
        inner, gain_part, bias_part = norm_backward(values, summed_parts(parts), gain[...])
        low = (middle_grad[...] + inner).astype(bf16)
        tile = low.shape[0]
        here = pl.ds(pl.multiple_of(step * tile, tile), tile)
        for copy in range(SIDE):
            line[copy, here] = low

        @pl.when(step == 0)
        def _():
            vectors[...] = jnp.zeros(vectors.shape, fp32)
            vectors[2:5] = vector_two[:3]

        vectors[0:1] += gain_part
        vectors[1:2] += bias_part

        @pl.when(step == rows // tile - 1)
        def _():
            for copy in range(SIDE):
                line[copy, rows:] = vectors[...].astype(bf16)

    outs = [((SIDE, rows + 16, width), bf16, False)]
    return norm_call(
        body,
        "first_norm_backward",
        parts,
        [tokens, middle_grad],
        [gain, vector_two],
        outs,
        scratch=[(16, width)],
    )[0]


def widen_weights(down, up, qkv, out, small):
    steps = 8
    width, units = up.shape

    def body(
        down_in, up_in, qkv_in, out_in, small_in, down_to, up_to, qkv_to, out_to, down_bias, up_bias, qv_bias
    ):
        def block(down_in, up_in, qkv_in, down_to, up_to, qkv_to):
            down_to[...] = down_in[...].astype(fp32).T
            up_to[...] = up_in[...].astype(fp32)
            qkv_to[...] = qkv_in[...].astype(fp32)

        rows = pl.BlockSpec((width // steps, units), lambda i: (i, 0))
        columns = pl.BlockSpec((units, width // steps), lambda i: (0, i))
        planes = pl.BlockSpec((3, width // steps, HD), lambda i: (0, i, 0))
        pltpu.emit_pipeline(
            block,
            grid=(steps,),
            in_specs=[rows, rows, planes],
            out_specs=[columns, rows, planes],
        )(down_in, up_in, qkv_in, down_to, up_to, qkv_to)
        out_to[...] = out_in[...].astype(fp32)
        values = small_in[...].astype(fp32)
        down_bias[...] = values[:1]
        up_bias[...] = values[1:2, :units]
        qv_bias[:1] = values[1:2, units : units + HD]
        qv_bias[1:] = values[1:2, units + 2 * HD : units + 3 * HD]

    hbm = pl.BlockSpec(memory_space=pltpu.HBM)
    vmem = pl.BlockSpec(memory_space=pltpu.VMEM)
    like = [(units, width), up.shape, qkv.shape, out.shape, (1, width), (1, units), (2, HD)]
    return pl.pallas_call(
        body,
        in_specs=[hbm] * 3 + [vmem] * 2,
        out_specs=[hbm] * 3 + [vmem] * 4,
        out_shape=[jax.ShapeDtypeStruct(shape, fp32) for shape in like],
        compiler_params=pltpu.CompilerParams(vmem_limit_bytes=58 * 2**20),
        name="widen_weights",
    )(down, up, qkv, out, small)


def widen_lines(whole):
    lines, rows, width = whole.shape
    rows -= 16
    part = 2

    def body(whole_in, whole_to):
        def block(whole_in, whole_to):
            whole_to[...] = whole_in[0].astype(fp32)

        pltpu.emit_pipeline(
            block,
            grid=(lines * part,),
            in_specs=[
                pl.BlockSpec((1, rows // part, width), lambda i: (i // part, i % part, 0))
            ],
            out_specs=[pl.BlockSpec((rows // part, width), lambda i: (i, 0))],
        )(whole_in, whole_to)

    hbm = pl.BlockSpec(memory_space=pltpu.HBM)
    return pl.pallas_call(
        body,
        in_specs=[hbm],
        out_specs=hbm,
        out_shape=jax.ShapeDtypeStruct((lines * rows, width), fp32),
        compiler_params=pltpu.CompilerParams(vmem_limit_bytes=24 * 2**20),
        name="widen_lines",
    )(whole)


def lay_lines(line_place, pieces, kind):
    tile = pieces[3].shape[0]
    width = pieces[0].shape[1]

    def body(place, own, before, behind, top, bottom, out):
        step = pl.program_id(0)
        sources = [own, own, before, before, behind, behind, top, bottom]
        for index in range(2 * SIDE):

            @pl.when(step == index)
            def _():
                out[...] = sources[index][:tile].astype(kind)

    def piece(first, last):
        return pl.BlockSpec((tile, width), lambda step, place: (jnp.clip(step - first, 0, last), 0))

    def target(step, place):
        kinds = step // 2
        away = jnp.where(kinds == 1, SIDE - 1, jnp.where(kinds == 2, 1, jnp.where(kinds == 3, 2, 0)))
        return ((place[0] + away) % SIDE * 2 + step % 2, 0)

    return pl.pallas_call(
        body,
        grid_spec=pltpu.PrefetchScalarGridSpec(
            num_scalar_prefetch=1,
            grid=(2 * SIDE,),
            in_specs=[piece(0, 1), piece(2, 1), piece(4, 1), piece(6, 0), piece(7, 0)],
            out_specs=pl.BlockSpec((tile, width), target),
        ),
        out_shape=jax.ShapeDtypeStruct((2 * SIDE * tile, width), kind),
        compiler_params=pltpu.CompilerParams(vmem_limit_bytes=24 * 2**20),
        name="lay_lines",
    )(line_place, *pieces)


def per_device(
    layer_input,
    ln1_gain,
    ln1_bias,
    qkv_weight,
    qv_bias,
    out_weight,
    out_bias,
    ln2_gain,
    ln2_bias,
    up_weight,
    up_bias,
    down_weight,
    down_bias,
    cotangent,
    group_table,
    group_counts,
    block_order,
):
    width = layer_input.shape[-1]
    rows = layer_input.shape[1]
    local = qkv_weight.shape[2]
    hidden_local = up_weight.shape[1]
    block_rows = rows // 2
    line_rows = rows // SIDE
    own_rows = line_rows // SIDE
    grp_at = lax.axis_index("grp")
    tp_at = lax.axis_index("tp")
    ctx_at = lax.axis_index("ctx")
    even = grp_at % 2 == 0
    a_at = jnp.where(even, tp_at % SIDE, tp_at // SIDE)
    b_at = jnp.where(even, tp_at // SIDE, tp_at % SIDE)
    line_start = a_at * line_rows
    own_start = line_start + b_at * own_rows

    always = ctx_at < N_CTX

    def stage(work, *operands):
        shapes = jax.eval_shape(work, *operands)

        def empty(*operands):
            return jax.tree.map(lambda like: jnp.zeros(like.shape, like.dtype), shapes)

        return lax.cond(always, work, empty, *operands)

    gain_one = ln1_gain.astype(fp32)
    bias_one = ln1_bias.astype(fp32)
    gain_two = ln2_gain.astype(fp32)
    bias_two = ln2_bias.astype(fp32)
    tokens = layer_input.reshape(rows, width)
    cot = cotangent.reshape(rows, width)
    own_tokens = lax.dynamic_slice_in_dim(tokens, own_start, own_rows, 0)
    own_cot = lax.dynamic_slice_in_dim(cot, own_start, own_rows, 0)

    shares = position_shares(group_table, group_counts)
    grp_slots = jnp.arange(shares.shape[0], dtype=jnp.int32)
    my_share = jnp.sum(jnp.where(grp_slots == grp_at, shares, jnp.zeros_like(shares)))
    column = jnp.arange(block_order.shape[0], dtype=jnp.int32)
    slots = jnp.arange(4, dtype=jnp.int32)
    slots = jnp.where(slots < 2, ctx_at * 2 + slots, (1 - ctx_at) * 2 + slots - 2)
    places = jnp.sum(
        jnp.where(slots[:, None] == column[None, :], block_order[None, :], 0), axis=1
    )
    out_lines = join_pieces(out_weight, a_at, GROUPS_A)
    up_lines = gather_lines(up_weight, GROUPS_A)
    qkv_turned = qkv_weight.transpose(1, 2, 0).reshape(3 * local, width)
    qkv_lines = gather_lines(qkv_turned, GROUPS_A)
    first_normed = layer_norm(tokens.astype(fp32), gain_one, bias_one).astype(bf16)
    mixed = jnp.einsum("rd,cd->rc", first_normed, qkv_turned, preferred_element_type=fp32)
    query = (mixed[:, :local] + qv_bias[0].astype(fp32)).astype(bf16)
    pair = jnp.stack(
        [mixed[:, local : 2 * local], mixed[:, 2 * local :] + qv_bias[1].astype(fp32)]
    ).astype(bf16)
    swap_ctx = [(0, 1), (1, 0)]
    pair_other = lax.ppermute(pair, "ctx", swap_ctx)

    own_part = own_keys_forward(places, query, pair)
    pair_other, out_lines, *own_part = lax.optimization_barrier(
        (pair_other, out_lines, *own_part)
    )
    heads, level = other_keys_forward(places, query, pair_other, *own_part)

    heads_line = exchange(heads.reshape(SIDE, line_rows, local), GROUPS_A)

    cot = after(cot, heads)
    grad_out = cot.astype(fp32) * my_share
    grad_low = grad_out.astype(bf16)
    down_bias_grad = jnp.sum(grad_out, axis=0)
    active_grad = jnp.einsum("rd,fd->rf", grad_low, down_weight, preferred_element_type=fp32)
    bias_rows = jnp.broadcast_to(up_bias[None, None], (SIDE, 16, hidden_local))
    active_grad = jnp.concatenate(
        [active_grad.astype(bf16).reshape(SIDE, line_rows, hidden_local), bias_rows], axis=1
    )
    heads_line, active_grad, down_bias_grad = lax.optimization_barrier(
        (heads_line, active_grad, down_bias_grad)
    )
    active_grad = jnp.stack(
        arriving(
            lambda step: lax.dynamic_index_in_dim(
                active_grad, (a_at + step) % SIDE, 0, keepdims=False
            ),
            GROUPS_A,
        )
    )

    heads_line = heads_line.transpose(1, 0, 2).reshape(line_rows, SIDE * local)
    partial_out = jnp.dot(heads_line, out_lines, preferred_element_type=fp32).astype(bf16)
    partial_out = exchange(partial_out.reshape(SIDE, own_rows, width), GROUPS_B)
    normed = layer_norm(after(tokens, heads_line).astype(fp32), gain_one, bias_one).astype(bf16)
    partial_out, active_grad, normed = lax.optimization_barrier((partial_out, active_grad, normed))
    middle, normed_two = second_norm(
        partial_out, own_tokens, out_bias.astype(fp32)[None], gain_two[None], bias_two[None]
    )
    normed_two = exchange(normed_two, GROUPS_B).reshape(line_rows, width)

    line_place = a_at.astype(jnp.int32)[None]
    both, normed_two_grad = feed_forward(line_place, normed_two, up_lines, active_grad)
    normed_two_grad, both, normed_two = lax.optimization_barrier(
        (normed_two_grad, both, normed_two)
    )

    normed_two_rows = gather_lines(normed_two, GROUPS_A)

    def norm_stage(normed_two_grad, both, middle, own_cot, my_share):
        normed_two_grad = exchange(normed_two_grad.reshape(SIDE, own_rows, width), GROUPS_B)
        pieces = arriving(
            lambda step: lax.dynamic_index_in_dim(both, (a_at + step) % SIDE, 0, keepdims=False),
            GROUPS_A,
        )
        middle_grad, middle_low, vector_two = second_norm_backward(
            my_share[None], normed_two_grad, middle, own_cot, gain_two[None]
        )
        middle_low, *pieces = lax.optimization_barrier((middle_low, *pieces))
        middle_low = exchange(middle_low, GROUPS_B).reshape(line_rows, width)
        partial_mlp = down_product(line_place, pieces, down_weight)
        return middle_grad, middle_low, vector_two, pieces, partial_mlp

    middle_grad, middle_low, vector_two, pieces, partial_mlp = stage(
        norm_stage, normed_two_grad, both, middle, own_cot, my_share
    )
    middle_low, qkv_lines, normed_two_rows = lax.optimization_barrier(
        (middle_low, qkv_lines, normed_two_rows)
    )
    partial_mlp = lax.psum_scatter(
        partial_mlp, EVERY, scatter_dimension=0, tiled=True, axis_index_groups=GROUPS_A
    )

    def attention_stage(middle_low, heads_line, pieces, normed_two_rows):
        head_grad = jnp.einsum("rd,fd->rf", middle_low, out_lines, preferred_element_type=fp32)
        head_grad = head_grad.astype(bf16).reshape(line_rows, SIDE, local).transpose(1, 0, 2)
        head_grad = exchange(head_grad, GROUPS_A).reshape(rows, local)
        up_weight_grad, up_bias_grad = turned_grad(line_place, normed_two_rows, pieces, 1)
        head_grad, up_weight_grad = lax.optimization_barrier((head_grad, up_weight_grad))
        query_grad, pair_other_grad, slack = other_keys_backward(
            places, query, pair_other, head_grad, heads, level
        )
        pair_from = lax.ppermute(pair_other_grad, "ctx", swap_ctx)
        query_grad, pair_grad = own_keys_backward(
            places, query, pair, head_grad, level, slack, query_grad
        )
        out_weight_grad = jnp.einsum(
            "rf,rd->fd",
            after(heads_line, pair_other_grad),
            middle_low,
            preferred_element_type=fp32,
        ).astype(bf16)
        out_weight_grad = sum_pieces(out_weight_grad, a_at, GROUPS_A).astype(bf16)
        pair_from, pair_grad, query_grad = lax.optimization_barrier(
            (pair_from, pair_grad, query_grad)
        )
        pair_grad = (pair_grad + pair_from.astype(fp32)).astype(bf16)
        qkv_grad = jnp.concatenate([query_grad, pair_grad[0], pair_grad[1]], axis=1)
        return qkv_grad, up_weight_grad, up_bias_grad, out_weight_grad

    qkv_grad, up_weight_grad, up_bias_grad, out_weight_grad = stage(
        attention_stage, middle_low, heads_line, pieces, normed_two_rows.reshape(rows, width)
    )
    qkv_grad_line = exchange(qkv_grad.reshape(SIDE, line_rows, 3 * local), GROUPS_A)
    output_sum = sum_pieces(after(partial_mlp, qkv_grad), b_at, GROUPS_B)
    down_weight_grad, _ = turned_grad(line_place, after(grad_low, qkv_grad), pieces, 0)
    qkv_grad_line, output_sum, down_weight_grad, qkv_grad = lax.optimization_barrier(
        (qkv_grad_line, output_sum, down_weight_grad, qkv_grad)
    )
    output_own = (middle + output_sum + down_bias.astype(fp32)).astype(bf16)
    output_line = join_pieces(output_own, b_at, GROUPS_B)
    qkv_weight_grad, qkv_bias_grad = projection_grad(normed, qkv_grad)
    small_rows = jnp.concatenate(
        [
            down_bias_grad[None],
            jnp.concatenate(
                [
                    up_bias_grad,
                    qkv_bias_grad,
                    jnp.zeros((1, width - hidden_local - 3 * local), fp32),
                ],
                axis=1,
            ),
            jnp.zeros((14, width), fp32),
        ]
    ).astype(bf16)
    out_weight_grad = out_weight_grad.astype(bf16)
    weight_grads = (down_weight_grad, up_weight_grad, qkv_weight_grad, out_weight_grad, small_rows)
    qkv_grad_line, output_line, *weight_grads = lax.optimization_barrier(
        (qkv_grad_line, output_line) + weight_grads
    )
    weight_grads = lax.psum(tuple(weight_grads), ("grp", "ctx"))

    def finish(qkv_grad_line, output_line, qkv_lines, middle_grad, own_tokens, vector_two):
        output_pieces = ring(output_line, line_rows // 2, GROUPS_A)
        normed_grad = line_product(qkv_grad_line, qkv_lines)
        normed_grad = exchange(normed_grad.reshape(SIDE, own_rows, width), GROUPS_B)
        normed_grad, *first_pieces = lax.optimization_barrier((normed_grad, *output_pieces[:3]))
        output_pieces = (*first_pieces, *output_pieces[3:])
        line = first_norm_backward(
            normed_grad, own_tokens, middle_grad, gain_one[None], vector_two
        )
        line = exchange(line, GROUPS_B)
        line, *output_pieces = lax.optimization_barrier((line, *output_pieces))
        vectors = jnp.sum(line[:, own_rows:].astype(fp32), axis=0).astype(bf16)
        line = jnp.concatenate([line[:, :own_rows].reshape(line_rows, width), vectors])
        return lay_lines(line_place, output_pieces, bf16), spread(line, GROUPS_A)

    layer_output, whole = stage(
        finish, qkv_grad_line, output_line, qkv_lines, middle_grad, own_tokens, vector_two
    )
    vectors = jnp.sum(whole[:, line_rows : line_rows + 8].astype(fp32), axis=0)
    vectors = vectors + lax.ppermute(vectors, EVERY, swap_all(1, 0))
    come = lax.ppermute(vectors, EVERY, swap_all(2, 0))
    come, input_grad = lax.optimization_barrier((come, widen_lines(after(whole, vectors))))
    vectors = vectors + come
    come = lax.ppermute(vectors, EVERY, swap_all(0, 1))
    weight_grads = lax.optimization_barrier((vectors, *weight_grads))[1:]
    come, *widened = lax.optimization_barrier((come, *widen_weights(*weight_grads)))
    vectors = vectors + come
    down_weight_grad, up_weight_grad, qkv_weight_grad, out_weight_grad = widened[:4]
    down_bias_grad, up_bias_grad, qv_bias_grad = widened[4:]
    return (
        layer_output.reshape(1, rows, width),
        input_grad.reshape(1, rows, width),
        vectors[0],
        vectors[1],
        qkv_weight_grad.transpose(1, 0, 2),
        qv_bias_grad,
        out_weight_grad,
        vectors[4],
        vectors[2],
        vectors[3],
        up_weight_grad,
        up_bias_grad.reshape(hidden_local),
        down_weight_grad,
        down_bias_grad.reshape(width),
    )


def solution(mesh):
    placed = (
        P("grp", "ctx", None),
        P(),
        P(),
        P(None, None, "tp"),
        P(None, "tp"),
        P("tp", None),
        P(),
        P(),
        P(),
        P(None, "tp"),
        P("tp"),
        P("tp", None),
        P(),
        P("grp", "ctx", None),
        P(),
        P(),
        P(),
    )
    return jax.shard_map(
        per_device,
        mesh=mesh,
        in_specs=placed,
        out_specs=(
            P("grp", "ctx", None),
            P("grp", "ctx", None),
            P(),
            P(),
            P(None, None, "tp"),
            P(None, "tp"),
            P("tp", None),
            P(),
            P(),
            P(),
            P(None, "tp"),
            P("tp"),
            P("tp", None),
            P(),
        ),
        check_vma=False,
    )
```

```python
import math

import jax
import jax.numpy as jnp
from jax import lax
from jax.experimental import pallas as pl
from jax.experimental.pallas import tpu as pltpu
from jax.sharding import PartitionSpec as P

HD = 128
GROUPS = 3
TILE = 256
SCALE = 1.0 / math.sqrt(HD)
SCALE_TWO = SCALE * math.log2(math.e)
EVERY = ("grp", "tp", "ctx")
N_GRP, N_TP, N_CTX, SIDE = 4, 16, 2, 4
fp32 = jnp.float32
bf16 = jnp.bfloat16


def device_id(grp, tx, tz, ctx):
    return (grp * N_TP + tx * SIDE + tz) * N_CTX + ctx


def line_groups(first_axis):
    groups = []
    for grp in range(N_GRP):
        for ctx in range(N_CTX):
            for fixed in range(SIDE):
                along_z = (grp % 2 == 0) == first_axis
                groups.append(
                    [
                        device_id(grp, fixed, i, ctx) if along_z else device_id(grp, i, fixed, ctx)
                        for i in range(SIDE)
                    ]
                )
    return groups


GROUPS_A = line_groups(True)
GROUPS_B = line_groups(False)


def swap_lines(groups, bit):
    return [(line[i], line[i ^ bit]) for line in groups for i in range(SIDE)]


def swap_all(grp_bit, ctx_bit):
    return [
        (device_id(g, x, z, c), device_id(g ^ grp_bit, x, z, c ^ ctx_bit))
        for g in range(N_GRP)
        for x in range(SIDE)
        for z in range(SIDE)
        for c in range(N_CTX)
    ]


def exchange(pieces, groups):
    return lax.all_to_all(pieces, EVERY, 0, 0, axis_index_groups=groups)


def spread(piece, groups):
    return exchange(jnp.broadcast_to(piece[None], (SIDE,) + piece.shape), groups)


def turn(groups, step):
    return [(line[i], line[(i + step) % SIDE]) for line in groups for i in range(SIDE)]


def sum_pieces(partial, place, groups):
    piece_rows = partial.shape[0] // SIDE
    total = lax.dynamic_slice_in_dim(partial, place * piece_rows, piece_rows, 0).astype(fp32)
    for step in (1, 3, 2):
        goes = (place + step) % SIDE
        piece = lax.dynamic_slice_in_dim(partial, goes * piece_rows, piece_rows, 0)
        total = total + lax.ppermute(piece, EVERY, turn(groups, step)).astype(fp32)
    return total


def ring(piece, split, groups):
    before = lax.ppermute(piece, EVERY, turn(groups, 1))
    behind = lax.ppermute(piece, EVERY, turn(groups, 3))
    top = lax.ppermute(before[:split], EVERY, turn(groups, 1))
    bottom = lax.ppermute(behind[split:], EVERY, turn(groups, 3))
    return piece, before, behind, top, bottom


def join_pieces(piece, place, groups):
    piece_rows, width = piece.shape
    whole = jnp.zeros((SIDE * piece_rows, width), piece.dtype)
    whole = lax.dynamic_update_slice_in_dim(whole, piece, place * piece_rows, 0)
    for step in (1, 3, 2):
        come = lax.ppermute(piece, EVERY, turn(groups, step))
        origin = (place + SIDE - step) % SIDE
        whole = lax.dynamic_update_slice_in_dim(whole, come, origin * piece_rows, 0)
    return whole


def arriving(pieces, groups):
    come = {step: lax.ppermute(pieces(step), EVERY, turn(groups, step)) for step in (1, 3, 2)}
    return [pieces(0), come[1], come[2], come[3]]


def after(value, *earlier):
    return lax.optimization_barrier((value,) + earlier)[0]


def gather_lines(piece, groups):
    return lax.all_gather(piece, EVERY, axis=0, axis_index_groups=groups)


def layer_norm(values, gain_vec, bias_vec):
    average = jnp.mean(values, axis=-1, keepdims=True)
    centred = values - average
    variance = jnp.mean(centred * centred, axis=-1, keepdims=True)
    return centred * lax.rsqrt(variance + 1e-05) * gain_vec + bias_vec


def position_shares(group_table, group_counts):
    member = (group_table[:, None] == jnp.arange(GROUPS, dtype=jnp.int32)[None, :]).astype(fp32)
    holders = jnp.sum(member, axis=0)
    counts_float = group_counts.astype(fp32)
    per_group = counts_float / (holders * jnp.sum(counts_float))
    return group_table.shape[0] * jnp.sum(member * per_group[None, :], axis=1)


def turned_product(left, right):
    return lax.dot_general(left, right, (((1,), (1,)), ((), ())), preferred_element_type=fp32)


def plain_product(left, right):
    return lax.dot_general(left, right, (((1,), (0,)), ((), ())), preferred_element_type=fp32)


def attention_call(body, name, scratch, like, places, *operands):
    return pl.pallas_call(
        body,
        in_specs=[pl.BlockSpec(memory_space=pltpu.SMEM)]
        + [pl.BlockSpec(memory_space=pltpu.VMEM)] * len(operands),
        out_specs=[pl.BlockSpec(memory_space=pltpu.VMEM)] * len(like),
        out_shape=[jax.ShapeDtypeStruct(shape, kind) for shape, kind in like],
        scratch_shapes=[pltpu.VMEM(shape, fp32) for shape in scratch],
        compiler_params=pltpu.CompilerParams(vmem_limit_bytes=40 * 2**20),
        name=name,
    )(places, *operands)


def own_keys_forward(places, query, pair):
    rows = query.shape[0]
    block = rows // 2

    def body(places, query, pair, top, total, mixed):
        key, value = pair.at[0], pair.at[1]
        for slot in range(2):
            for start in range(slot * block, (slot + 1) * block, TILE):
                last = start + TILE
                keys = slice(slot * block, last)
                scores = turned_product(query[start:last], key[keys]) * SCALE_TWO
                place_q = lax.broadcasted_iota(jnp.int32, scores.shape, 0) + start
                place_k = lax.broadcasted_iota(jnp.int32, scores.shape, 1) + slot * block
                scores = jnp.where(place_q >= place_k, scores, -1e30)
                peak = jnp.max(scores, axis=1, keepdims=True)
                weights = jnp.exp2(scores - peak)
                top[start:last] = peak
                total[start:last] = jnp.sum(weights, axis=1, keepdims=True)
                mixed[start:last] = plain_product(weights.astype(bf16), value[keys])
        for slot in range(2):
            other = 1 - slot

            @pl.when(places[slot] > places[other])
            def _():
                add_keys(query, key, value, top, total, mixed, slot, other, block)

    like = [((rows, 1), fp32), ((rows, 1), fp32), ((rows, HD), fp32)]
    return attention_call(body, "own_keys_forward", [], like, places, query, pair)


def add_keys(query, key, value, top, total, mixed, slot, key_slot, block):
    keys = slice(key_slot * block, (key_slot + 1) * block)
    for start in range(slot * block, (slot + 1) * block, TILE):
        here = slice(start, start + TILE)
        scores = turned_product(query[here], key[keys]) * SCALE_TWO
        peak = jnp.maximum(top[here], jnp.max(scores, axis=1, keepdims=True))
        fade = jnp.exp2(top[here] - peak)
        weights = jnp.exp2(scores - peak)
        top[here] = peak
        total[here] = total[here] * fade + jnp.sum(weights, axis=1, keepdims=True)
        mixed[here] = mixed[here] * fade + plain_product(weights.astype(bf16), value[keys])


def other_keys_forward(places, query, pair, top, total, mixed):
    rows = query.shape[0]
    block = rows // 2

    def body(places, query, pair, top_in, total_in, mixed_in, heads, level, top, total, mixed):
        key, value = pair.at[0], pair.at[1]
        top[...] = top_in[...]
        total[...] = total_in[...]
        mixed[...] = mixed_in[...]
        for slot in range(2):
            for key_slot in range(2):

                @pl.when(places[slot] > places[2 + key_slot])
                def _():
                    add_keys(query, key, value, top, total, mixed, slot, key_slot, block)

        for start in range(0, rows, TILE):
            here = slice(start, start + TILE)
            heads[here] = (mixed[here] / total[here]).astype(bf16)
            logs = top[here] + jnp.log2(total[here])
            level[:, here] = jnp.broadcast_to(logs, (TILE, HD)).T[:8]

    like = [((rows, HD), bf16), ((8, rows), fp32)]
    scratch = [(rows, 1), (rows, 1), (rows, HD)]
    return attention_call(
        body, "other_keys_forward", scratch, like, places, query, pair, top, total, mixed
    )


def pair_backward(
    query, key, value, head_grad, level, slack, query_grad, key_grad, value_grad, slot, key_slot, block, own
):
    for start in range(key_slot * block, (key_slot + 1) * block, TILE):
        keys = slice(start, start + TILE)
        first = start if own else slot * block
        rows = slice(first, (slot + 1) * block)
        scores = turned_product(key[keys], query[rows]) * SCALE_TWO - level[:1, rows]
        if own:
            place_k = lax.broadcasted_iota(jnp.int32, scores.shape, 0)
            place_q = lax.broadcasted_iota(jnp.int32, scores.shape, 1)
            scores = jnp.where(place_q >= place_k, scores, -1e30)
        probs = jnp.exp2(scores)
        value_grad[keys] += plain_product(probs.astype(bf16), head_grad[rows])
        prob_grad = turned_product(value[keys], head_grad[rows]) - slack[:1, rows]
        score_grad = (probs * prob_grad).astype(bf16)
        key_grad[keys] += plain_product(score_grad, query[rows])
        query_grad[rows] += lax.dot_general(
            score_grad, key[keys], (((0,), (0,)), ((), ())), preferred_element_type=fp32
        )


def other_keys_backward(places, query, pair, head_grad, heads, level):
    rows = query.shape[0]
    block = rows // 2

    def body(
        places, query, pair, head_grad, heads, level, query_grad, pair_grad, slack, key_sum, value_sum
    ):
        key, value = pair.at[0], pair.at[1]
        query_grad[...] = jnp.zeros(query_grad.shape, fp32)
        key_sum[...] = jnp.zeros(key_sum.shape, fp32)
        value_sum[...] = jnp.zeros(value_sum.shape, fp32)
        for start in range(0, rows, TILE):
            here = slice(start, start + TILE)
            both = head_grad[here].astype(fp32) * heads[here].astype(fp32)
            both = jnp.sum(both, axis=1, keepdims=True)
            slack[:, here] = jnp.broadcast_to(both, (TILE, HD)).T[:8]
        for slot in range(2):
            for key_slot in range(2):

                @pl.when(places[slot] > places[2 + key_slot])
                def _():
                    pair_backward(
                        query, key, value, head_grad, level, slack,
                        query_grad, key_sum, value_sum, slot, key_slot, block, False,
                    )

        pair_grad[0] = (key_sum[...] * SCALE).astype(bf16)
        pair_grad[1] = value_sum[...].astype(bf16)

    like = [((rows, HD), fp32), ((2, rows, HD), bf16), ((8, rows), fp32)]
    return attention_call(
        body, "other_keys_backward", [(rows, HD)] * 2, like,
        places, query, pair, head_grad, heads, level,
    )


def own_keys_backward(places, query, pair, head_grad, level, slack, query_grad):
    rows = query.shape[0]
    block = rows // 2

    def body(
        places, query, pair, head_grad, level, slack, query_in, query_grad, pair_grad, query_sum
    ):
        key, value = pair.at[0], pair.at[1]
        query_sum[...] = query_in[...]
        pair_grad[...] = jnp.zeros(pair_grad.shape, fp32)
        key_sum = pair_grad.at[0]
        value_sum = pair_grad.at[1]
        for slot in range(2):
            pair_backward(
                query, key, value, head_grad, level, slack,
                query_sum, key_sum, value_sum, slot, slot, block, True,
            )
        for slot in range(2):

            @pl.when(places[slot] > places[1 - slot])
            def _():
                pair_backward(
                    query, key, value, head_grad, level, slack,
                    query_sum, key_sum, value_sum, slot, 1 - slot, block, False,
                )

        pair_grad[0] = pair_grad[0] * SCALE
        query_grad[...] = (query_sum[...] * SCALE).astype(bf16)

    like = [((rows, HD), bf16), ((2, rows, HD), fp32)]
    return attention_call(
        body, "own_keys_backward", [(rows, HD)], like,
        places, query, pair, head_grad, level, slack, query_grad,
    )


def feed_forward(line_place, normed_two, up_lines, active_grad):
    rows, width = normed_two.shape
    units = up_lines.shape[2]
    bend = math.sqrt(2.0 / math.pi)

    def body(place, normed_two, up, grad, *refs):
        pieces, (back, total) = refs[:SIDE], refs[SIDE:]
        step = pl.program_id(0)
        hidden = plain_product(normed_two[...], up[0])
        hidden = hidden + grad[0, rows : rows + 1].astype(fp32)
        square = hidden * hidden
        bent = jnp.tanh(bend * hidden * (1.0 + 0.044715 * square))
        half = 0.5 * (1.0 + bent)
        active = (hidden * half).astype(bf16)
        slope = half + (0.5 * bend) * hidden * (1.0 - bent * bent) * (1.0 + 0.134145 * square)
        low = (slope * grad[0, :rows].astype(fp32)).astype(bf16)

        for index in range(SIDE):

            @pl.when(step == index)
            def _():
                pieces[index][:, :units] = active
                pieces[index][:, units:] = low

        product = turned_product(low, up[0])

        @pl.when(step == 0)
        def _():
            total[...] = product

        @pl.when(step > 0)
        def _():
            total[...] += product

        @pl.when(step == SIDE - 1)
        def _():
            back[...] = total[...].astype(bf16)

    def origin(step, place):
        return ((place[0] + SIDE - step) % SIDE, 0, 0)

    return pl.pallas_call(
        body,
        grid_spec=pltpu.PrefetchScalarGridSpec(
            num_scalar_prefetch=1,
            grid=(SIDE,),
            in_specs=[
                pl.BlockSpec((rows, width), lambda step, place: (0, 0)),
                pl.BlockSpec((1, width, units), origin),
                pl.BlockSpec((1, rows + 16, units), lambda step, place: (step, 0, 0)),
            ],
            out_specs=[
                pl.BlockSpec((rows, 2 * units), lambda step, place: (0, 0)),
            ]
            * SIDE
            + [pl.BlockSpec((rows, width), lambda step, place: (0, 0))],
            scratch_shapes=[pltpu.VMEM((rows, width), fp32)],
        ),
        out_shape=[
            jax.ShapeDtypeStruct((rows, 2 * units), bf16),
        ]
        * SIDE
        + [
            jax.ShapeDtypeStruct((rows, width), bf16),
        ],
        compiler_params=pltpu.CompilerParams(vmem_limit_bytes=58 * 2**20),
        name="feed_forward",
    )(line_place, normed_two, up_lines, active_grad)


def line_product(pieces, weights):
    rows, depth = pieces.shape[1:]
    width = weights.shape[2]

    def body(piece, weight, out, total):
        step = pl.program_id(0)
        product = plain_product(piece[0], weight[0])

        @pl.when(step == 0)
        def _():
            total[...] = product

        @pl.when(step > 0)
        def _():
            total[...] += product

        @pl.when(step == SIDE - 1)
        def _():
            out[...] = total[...].astype(bf16)

    return pl.pallas_call(
        body,
        grid=(SIDE,),
        in_specs=[
            pl.BlockSpec((1, rows, depth), lambda step: (step, 0, 0)),
            pl.BlockSpec((1, depth, width), lambda step: (step, 0, 0)),
        ],
        out_specs=pl.BlockSpec((rows, width), lambda step: (0, 0)),
        out_shape=jax.ShapeDtypeStruct((rows, width), bf16),
        scratch_shapes=[pltpu.VMEM((rows, width), fp32)],
        compiler_params=pltpu.CompilerParams(vmem_limit_bytes=58 * 2**20),
        name="line_product",
    )(pieces, weights)


def down_product(line_place, pieces, down_weight):
    part = pieces[0].shape[0]
    units, width = down_weight.shape

    def body(place, *refs):
        pieces, (weight, out) = refs[:SIDE], refs[SIDE:]
        for index in range(SIDE):

            @pl.when(pl.program_id(0) == index)
            def _():
                out[...] = plain_product(pieces[index][...], weight[...]).astype(bf16)

    return pl.pallas_call(
        body,
        grid_spec=pltpu.PrefetchScalarGridSpec(
            num_scalar_prefetch=1,
            grid=(SIDE,),
            in_specs=[pl.BlockSpec((part, units), lambda step, place: (0, 0))] * SIDE
            + [pl.BlockSpec((units, width), lambda step, place: (0, 0))],
            out_specs=pl.BlockSpec(
                (part, width), lambda step, place: ((place[0] + SIDE - step) % SIDE, 0)
            ),
        ),
        out_shape=jax.ShapeDtypeStruct((SIDE * part, width), bf16),
        compiler_params=pltpu.CompilerParams(vmem_limit_bytes=40 * 2**20),
        name="down_product",
    )(line_place, *pieces, down_weight)


def turned_grad(line_place, matrix, pieces, half):
    rows, width = matrix.shape
    part = rows // SIDE
    units = pieces[0].shape[1] // 2
    steps = 2

    def body(place, matrix, *refs):
        pieces, (out, sums, turned) = refs[:SIDE], refs[SIDE:]

        @pl.when(pl.program_id(0) == 0)
        def _():
            added = None
            for index in range(SIDE):
                start = pl.multiple_of((place[0] + SIDE - index) % SIDE * part, part)
                values = pieces[index][...]
                turned[:, pl.ds(start, part)] = values.T
                piece_sum = jnp.sum(values.astype(fp32), axis=0, keepdims=True)
                added = piece_sum if added is None else added + piece_sum
            sums[...] = added

        out[...] = plain_product(turned[...], matrix[...]).astype(bf16)

    return pl.pallas_call(
        body,
        grid_spec=pltpu.PrefetchScalarGridSpec(
            num_scalar_prefetch=1,
            grid=(steps,),
            in_specs=[pl.BlockSpec((rows, width // steps), lambda step, place: (0, step))]
            + [pl.BlockSpec((part, units), lambda step, place: (0, half))] * SIDE,
            out_specs=[
                pl.BlockSpec((units, width // steps), lambda step, place: (0, step)),
                pl.BlockSpec((1, units), lambda step, place: (0, 0)),
            ],
            scratch_shapes=[pltpu.VMEM((units, rows), bf16)],
        ),
        out_shape=[
            jax.ShapeDtypeStruct((units, width), bf16),
            jax.ShapeDtypeStruct((1, units), fp32),
        ],
        compiler_params=pltpu.CompilerParams(vmem_limit_bytes=58 * 2**20),
        name="turned_grad",
    )(line_place, matrix, *pieces)


def projection_grad(normed, qkv_grad):
    rows, width = normed.shape
    columns = qkv_grad.shape[1]
    steps = 2

    def body(normed, qkv_grad, out, sums, turned):
        @pl.when(pl.program_id(0) == 0)
        def _():
            turned[...] = qkv_grad[...].T
            sums[...] = jnp.sum(qkv_grad[...].astype(fp32), axis=0, keepdims=True)

        out[...] = plain_product(turned[...], normed[...]).astype(bf16)

    return pl.pallas_call(
        body,
        grid=(steps,),
        in_specs=[
            pl.BlockSpec((rows, width // steps), lambda step: (0, step)),
            pl.BlockSpec((rows, columns), lambda step: (0, 0)),
        ],
        out_specs=[
            pl.BlockSpec((columns, width // steps), lambda step: (0, step)),
            pl.BlockSpec((1, columns), lambda step: (0, 0)),
        ],
        out_shape=[
            jax.ShapeDtypeStruct((columns, width), bf16),
            jax.ShapeDtypeStruct((1, columns), fp32),
        ],
        scratch_shapes=[pltpu.VMEM((columns, rows), bf16)],
        compiler_params=pltpu.CompilerParams(vmem_limit_bytes=58 * 2**20),
        name="projection_grad",
    )(normed, qkv_grad)


def norm_call(body, name, parts, rows_in, vectors_in, outs, scratch=(), scalars=()):
    tile = 16
    rows, width = parts.shape[1:]

    def by_rows(shape):
        if len(shape) == 3:
            return pl.BlockSpec((shape[0], tile, shape[2]), lambda step: (0, step, 0))
        return pl.BlockSpec((tile, shape[1]), lambda step: (step, 0))

    def whole(shape):
        return pl.BlockSpec(shape, lambda step: (0,) * len(shape))

    return pl.pallas_call(
        body,
        grid=(rows // tile,),
        in_specs=[pl.BlockSpec(memory_space=pltpu.SMEM)] * len(scalars)
        + [by_rows(parts.shape)]
        + [by_rows(operand.shape) for operand in rows_in]
        + [whole(operand.shape) for operand in vectors_in],
        out_specs=[by_rows(shape) if tiled else whole(shape) for shape, _, tiled in outs],
        out_shape=[jax.ShapeDtypeStruct(shape, kind) for shape, kind, _ in outs],
        scratch_shapes=[pltpu.VMEM(shape, fp32) for shape in scratch],
        compiler_params=pltpu.CompilerParams(vmem_limit_bytes=24 * 2**20),
        name=name,
    )(*scalars, parts, *rows_in, *vectors_in)


def summed_parts(parts):
    return (parts[0].astype(fp32) + parts[1].astype(fp32)) + (
        parts[2].astype(fp32) + parts[3].astype(fp32)
    )


def normalised(values):
    centred = values - jnp.mean(values, axis=1, keepdims=True)
    scale = lax.rsqrt(jnp.mean(centred * centred, axis=1, keepdims=True) + 1e-05)
    return centred * scale, scale


def norm_backward(values, grad, gain):
    unit, scale = normalised(values)
    scaled = grad * gain
    along = jnp.mean(scaled * unit, axis=1, keepdims=True)
    inner = scale * (scaled - jnp.mean(scaled, axis=1, keepdims=True) - unit * along)
    return inner, jnp.sum(grad * unit, axis=0, keepdims=True), jnp.sum(grad, axis=0, keepdims=True)


def second_norm(parts, tokens, out_bias, gain, bias):
    rows, width = tokens.shape

    def body(parts, tokens, out_bias, gain, bias, middle, normed):
        values = tokens[...].astype(fp32) + summed_parts(parts) + out_bias[...]
        middle[...] = values
        low = (normalised(values)[0] * gain[...] + bias[...]).astype(bf16)
        for line in range(SIDE):
            normed[line] = low

    outs = [((rows, width), fp32, True), ((SIDE, rows, width), bf16, True)]
    return norm_call(body, "second_norm", parts, [tokens], [out_bias, gain, bias], outs)


def second_norm_backward(share, parts, middle, cot, gain):
    rows, width = middle.shape

    def body(share, parts, middle, cot, gain, middle_grad, low, vectors):
        inner, gain_part, bias_part = norm_backward(middle[...], summed_parts(parts), gain[...])
        grad = cot[...].astype(fp32) * share[0] + inner
        middle_grad[...] = grad
        for line in range(SIDE):
            low[line] = grad.astype(bf16)

        @pl.when(pl.program_id(0) == 0)
        def _():
            vectors[...] = jnp.zeros(vectors.shape, fp32)

        vectors[0:1] += gain_part
        vectors[1:2] += bias_part
        vectors[2:3] += jnp.sum(grad, axis=0, keepdims=True)

    outs = [
        ((rows, width), fp32, True),
        ((SIDE, rows, width), bf16, True),
        ((8, width), fp32, False),
    ]
    return norm_call(
        body, "second_norm_backward", parts, [middle, cot], [gain], outs, scalars=[share]
    )


def first_norm_backward(parts, tokens, middle_grad, gain, vector_two):
    rows, width = tokens.shape

    def body(parts, tokens, middle_grad, gain, vector_two, line, vectors):
        step = pl.program_id(0)
        values = tokens[...].astype(fp32)
        inner, gain_part, bias_part = norm_backward(values, summed_parts(parts), gain[...])
        low = (middle_grad[...] + inner).astype(bf16)
        tile = low.shape[0]
        here = pl.ds(pl.multiple_of(step * tile, tile), tile)
        for copy in range(SIDE):
            line[copy, here] = low

        @pl.when(step == 0)
        def _():
            vectors[...] = jnp.zeros(vectors.shape, fp32)
            vectors[2:5] = vector_two[:3]

        vectors[0:1] += gain_part
        vectors[1:2] += bias_part

        @pl.when(step == rows // tile - 1)
        def _():
            for copy in range(SIDE):
                line[copy, rows:] = vectors[...].astype(bf16)

    outs = [((SIDE, rows + 16, width), bf16, False)]
    return norm_call(
        body,
        "first_norm_backward",
        parts,
        [tokens, middle_grad],
        [gain, vector_two],
        outs,
        scratch=[(16, width)],
    )[0]


def widen_weights(down, up, qkv, out, small):
    steps = 2
    units, width = down.shape

    def body(
        down_in, up_in, qkv_in, out_in, small_in, down_to, up_to, qkv_to, out_to, down_bias, up_bias, qv_bias
    ):
        def block(down_in, up_in, qkv_in, down_to, up_to, qkv_to):
            down_to[...] = down_in[...].astype(fp32)
            up_to[...] = up_in[...].astype(fp32).T
            for plane in range(3):
                qkv_to[plane] = qkv_in[plane * HD : (plane + 1) * HD].astype(fp32).T

        def columns(count):
            return pl.BlockSpec((count, width // steps), lambda i: (0, i))

        rows = pl.BlockSpec((units // steps, width), lambda i: (i, 0))
        turned = pl.BlockSpec((width // steps, units), lambda i: (i, 0))
        planes = pl.BlockSpec((3, width // steps, HD), lambda i: (0, i, 0))
        pltpu.emit_pipeline(
            block,
            grid=(steps,),
            in_specs=[rows, columns(units), columns(3 * HD)],
            out_specs=[rows, turned, planes],
        )(down_in, up_in, qkv_in, down_to, up_to, qkv_to)
        out_to[...] = out_in[...].astype(fp32)
        values = small_in[...].astype(fp32)
        down_bias[...] = values[:1]
        up_bias[...] = values[1:2, :units]
        qv_bias[:1] = values[1:2, units : units + HD]
        qv_bias[1:] = values[1:2, units + 2 * HD : units + 3 * HD]

    hbm = pl.BlockSpec(memory_space=pltpu.HBM)
    vmem = pl.BlockSpec(memory_space=pltpu.VMEM)
    like = [down.shape, (width, units), (3, width, HD), out.shape, (1, width), (1, units), (2, HD)]
    return pl.pallas_call(
        body,
        in_specs=[hbm] * 3 + [vmem] * 2,
        out_specs=[hbm] * 3 + [vmem] * 4,
        out_shape=[jax.ShapeDtypeStruct(shape, fp32) for shape in like],
        compiler_params=pltpu.CompilerParams(vmem_limit_bytes=58 * 2**20),
        name="widen_weights",
    )(down, up, qkv, out, small)


def widen_parts(line_place, parts, rows):
    width = parts[0].shape[1]

    def body(place, *refs):
        parts, out = refs[:SIDE], refs[SIDE]
        for index in range(SIDE):

            @pl.when(pl.program_id(0) == index)
            def _():
                out[...] = parts[index][...].astype(fp32)

    def part(index):
        return pl.BlockSpec(
            (rows, width), lambda step, place: (0, 0)
        )

    return pl.pallas_call(
        body,
        grid_spec=pltpu.PrefetchScalarGridSpec(
            num_scalar_prefetch=1,
            grid=(SIDE,),
            in_specs=[part(index) for index in range(SIDE)],
            out_specs=pl.BlockSpec(
                (rows, width), lambda step, place: ((place[0] + SIDE - step) % SIDE, 0)
            ),
        ),
        out_shape=jax.ShapeDtypeStruct((SIDE * rows, width), fp32),
        compiler_params=pltpu.CompilerParams(vmem_limit_bytes=32 * 2**20),
        name="widen_parts",
    )(line_place, *parts)


def lay_lines(line_place, pieces, kind):
    tile = pieces[3].shape[0]
    width = pieces[0].shape[1]

    def body(place, own, before, behind, top, bottom, out):
        step = pl.program_id(0)
        sources = [own, own, before, before, behind, behind, top, bottom]
        for index in range(2 * SIDE):

            @pl.when(step == index)
            def _():
                out[...] = sources[index][:tile].astype(kind)

    def piece(first, last):
        return pl.BlockSpec((tile, width), lambda step, place: (jnp.clip(step - first, 0, last), 0))

    def target(step, place):
        kinds = step // 2
        away = jnp.where(kinds == 1, SIDE - 1, jnp.where(kinds == 2, 1, jnp.where(kinds == 3, 2, 0)))
        return ((place[0] + away) % SIDE * 2 + step % 2, 0)

    return pl.pallas_call(
        body,
        grid_spec=pltpu.PrefetchScalarGridSpec(
            num_scalar_prefetch=1,
            grid=(2 * SIDE,),
            in_specs=[piece(0, 1), piece(2, 1), piece(4, 1), piece(6, 0), piece(7, 0)],
            out_specs=pl.BlockSpec((tile, width), target),
        ),
        out_shape=jax.ShapeDtypeStruct((2 * SIDE * tile, width), kind),
        compiler_params=pltpu.CompilerParams(vmem_limit_bytes=24 * 2**20),
        name="lay_lines",
    )(line_place, *pieces)


def per_device(
    layer_input,
    ln1_gain,
    ln1_bias,
    qkv_weight,
    qv_bias,
    out_weight,
    out_bias,
    ln2_gain,
    ln2_bias,
    up_weight,
    up_bias,
    down_weight,
    down_bias,
    cotangent,
    group_table,
    group_counts,
    block_order,
):
    width = layer_input.shape[-1]
    rows = layer_input.shape[1]
    local = qkv_weight.shape[2]
    hidden_local = up_weight.shape[1]
    block_rows = rows // 2
    line_rows = rows // SIDE
    own_rows = line_rows // SIDE
    grp_at = lax.axis_index("grp")
    tp_at = lax.axis_index("tp")
    ctx_at = lax.axis_index("ctx")
    even = grp_at % 2 == 0
    a_at = jnp.where(even, tp_at % SIDE, tp_at // SIDE)
    b_at = jnp.where(even, tp_at // SIDE, tp_at % SIDE)
    line_start = a_at * line_rows
    own_start = line_start + b_at * own_rows

    always = ctx_at < N_CTX

    def stage(work, *operands):
        shapes = jax.eval_shape(work, *operands)

        def empty(*operands):
            return jax.tree.map(lambda like: jnp.zeros(like.shape, like.dtype), shapes)

        return lax.cond(always, work, empty, *operands)

    gain_one = ln1_gain.astype(fp32)
    bias_one = ln1_bias.astype(fp32)
    gain_two = ln2_gain.astype(fp32)
    bias_two = ln2_bias.astype(fp32)
    tokens = layer_input.reshape(rows, width)
    cot = cotangent.reshape(rows, width)
    own_tokens = lax.dynamic_slice_in_dim(tokens, own_start, own_rows, 0)
    own_cot = lax.dynamic_slice_in_dim(cot, own_start, own_rows, 0)

    shares = position_shares(group_table, group_counts)
    grp_slots = jnp.arange(shares.shape[0], dtype=jnp.int32)
    my_share = jnp.sum(jnp.where(grp_slots == grp_at, shares, jnp.zeros_like(shares)))
    column = jnp.arange(block_order.shape[0], dtype=jnp.int32)
    slots = jnp.arange(4, dtype=jnp.int32)
    slots = jnp.where(slots < 2, ctx_at * 2 + slots, (1 - ctx_at) * 2 + slots - 2)
    places = jnp.sum(
        jnp.where(slots[:, None] == column[None, :], block_order[None, :], 0), axis=1
    )
    out_lines = join_pieces(out_weight, a_at, GROUPS_A)
    up_lines = gather_lines(up_weight, GROUPS_A)
    qkv_turned = qkv_weight.transpose(1, 2, 0).reshape(3 * local, width)
    qkv_lines = gather_lines(qkv_turned, GROUPS_A)
    first_normed = layer_norm(tokens.astype(fp32), gain_one, bias_one).astype(bf16)
    mixed = jnp.einsum("rd,cd->rc", first_normed, qkv_turned, preferred_element_type=fp32)
    query = (mixed[:, :local] + qv_bias[0].astype(fp32)).astype(bf16)
    pair = jnp.stack(
        [mixed[:, local : 2 * local], mixed[:, 2 * local :] + qv_bias[1].astype(fp32)]
    ).astype(bf16)
    swap_ctx = [(0, 1), (1, 0)]
    pair_other = lax.ppermute(pair, "ctx", swap_ctx)

    own_part = own_keys_forward(places, query, pair)
    pair_other, out_lines, *own_part = lax.optimization_barrier(
        (pair_other, out_lines, *own_part)
    )
    heads, level = other_keys_forward(places, query, pair_other, *own_part)

    heads_line = exchange(heads.reshape(SIDE, line_rows, local), GROUPS_A)

    cot = after(cot, heads)
    grad_out = cot.astype(fp32) * my_share
    grad_low = grad_out.astype(bf16)
    down_bias_grad = jnp.sum(grad_out, axis=0)
    active_grad = jnp.einsum("rd,fd->rf", grad_low, down_weight, preferred_element_type=fp32)
    bias_rows = jnp.broadcast_to(up_bias[None, None], (SIDE, 16, hidden_local))
    active_grad = jnp.concatenate(
        [active_grad.astype(bf16).reshape(SIDE, line_rows, hidden_local), bias_rows], axis=1
    )
    heads_line, active_grad, down_bias_grad = lax.optimization_barrier(
        (heads_line, active_grad, down_bias_grad)
    )
    active_grad = jnp.stack(
        arriving(
            lambda step: lax.dynamic_index_in_dim(
                active_grad, (a_at + step) % SIDE, 0, keepdims=False
            ),
            GROUPS_A,
        )
    )

    heads_line = heads_line.transpose(1, 0, 2).reshape(line_rows, SIDE * local)
    partial_out = jnp.dot(heads_line, out_lines, preferred_element_type=fp32).astype(bf16)
    partial_out = exchange(partial_out.reshape(SIDE, own_rows, width), GROUPS_B)
    normed = layer_norm(after(tokens, heads_line).astype(fp32), gain_one, bias_one).astype(bf16)
    partial_out, active_grad, normed = lax.optimization_barrier((partial_out, active_grad, normed))
    middle, normed_two = second_norm(
        partial_out, own_tokens, out_bias.astype(fp32)[None], gain_two[None], bias_two[None]
    )
    normed_two = exchange(normed_two, GROUPS_B).reshape(line_rows, width)

    line_place = a_at.astype(jnp.int32)[None]
    *unit_pieces, normed_two_grad = feed_forward(line_place, normed_two, up_lines, active_grad)
    normed_two_grad, normed_two, *unit_pieces = lax.optimization_barrier(
        (normed_two_grad, normed_two, *unit_pieces)
    )

    normed_two_rows = gather_lines(normed_two, GROUPS_A)

    def norm_stage(normed_two_grad, unit_pieces, middle, own_cot, my_share):
        normed_two_grad = exchange(normed_two_grad.reshape(SIDE, own_rows, width), GROUPS_B)
        pieces = arriving(lambda step: unit_pieces[-step % SIDE], GROUPS_A)
        middle_grad, middle_low, vector_two = second_norm_backward(
            my_share[None], normed_two_grad, middle, own_cot, gain_two[None]
        )
        middle_low, *pieces = lax.optimization_barrier((middle_low, *pieces))
        middle_low = exchange(middle_low, GROUPS_B).reshape(line_rows, width)
        partial_mlp = down_product(line_place, pieces, down_weight)
        return middle_grad, middle_low, vector_two, pieces, partial_mlp

    middle_grad, middle_low, vector_two, pieces, partial_mlp = stage(
        norm_stage, normed_two_grad, unit_pieces, middle, own_cot, my_share
    )
    middle_low, qkv_lines, normed_two_rows = lax.optimization_barrier(
        (middle_low, qkv_lines, normed_two_rows)
    )
    partial_mlp = lax.psum_scatter(
        partial_mlp, EVERY, scatter_dimension=0, tiled=True, axis_index_groups=GROUPS_A
    )

    def attention_stage(middle_low, heads_line, pieces, normed_two_rows):
        head_grad = jnp.einsum("rd,fd->rf", middle_low, out_lines, preferred_element_type=fp32)
        head_grad = head_grad.astype(bf16).reshape(line_rows, SIDE, local).transpose(1, 0, 2)
        head_grad = exchange(head_grad, GROUPS_A).reshape(rows, local)
        up_weight_grad, up_bias_grad = turned_grad(line_place, normed_two_rows, pieces, 1)
        head_grad, up_weight_grad = lax.optimization_barrier((head_grad, up_weight_grad))
        query_grad, pair_other_grad, slack = other_keys_backward(
            places, query, pair_other, head_grad, heads, level
        )
        pair_from = lax.ppermute(pair_other_grad, "ctx", swap_ctx)
        query_grad, pair_grad = own_keys_backward(
            places, query, pair, head_grad, level, slack, query_grad
        )
        out_weight_grad = jnp.einsum(
            "rf,rd->fd",
            after(heads_line, pair_other_grad),
            middle_low,
            preferred_element_type=fp32,
        ).astype(bf16)
        out_weight_grad = sum_pieces(out_weight_grad, a_at, GROUPS_A).astype(bf16)
        pair_from, pair_grad, query_grad = lax.optimization_barrier(
            (pair_from, pair_grad, query_grad)
        )
        pair_grad = (pair_grad + pair_from.astype(fp32)).astype(bf16)
        qkv_grad = jnp.concatenate([query_grad, pair_grad[0], pair_grad[1]], axis=1)
        return qkv_grad, up_weight_grad, up_bias_grad, out_weight_grad

    qkv_grad, up_weight_grad, up_bias_grad, out_weight_grad = stage(
        attention_stage, middle_low, heads_line, pieces, normed_two_rows.reshape(rows, width)
    )
    qkv_grad_line = exchange(qkv_grad.reshape(SIDE, line_rows, 3 * local), GROUPS_A)
    output_sum = sum_pieces(after(partial_mlp, qkv_grad), b_at, GROUPS_B)
    down_weight_grad, _ = turned_grad(line_place, after(grad_low, qkv_grad), pieces, 0)
    qkv_grad_line, output_sum, down_weight_grad, qkv_grad = lax.optimization_barrier(
        (qkv_grad_line, output_sum, down_weight_grad, qkv_grad)
    )
    output_own = (middle + output_sum + down_bias.astype(fp32)).astype(bf16)
    output_line = join_pieces(output_own, b_at, GROUPS_B)
    qkv_weight_grad, qkv_bias_grad = projection_grad(normed, qkv_grad)
    small_rows = jnp.concatenate(
        [
            down_bias_grad[None],
            jnp.concatenate(
                [
                    up_bias_grad,
                    qkv_bias_grad,
                    jnp.zeros((1, width - hidden_local - 3 * local), fp32),
                ],
                axis=1,
            ),
            jnp.zeros((14, width), fp32),
        ]
    ).astype(bf16)
    out_weight_grad = out_weight_grad.astype(bf16)
    weight_grads = (down_weight_grad, up_weight_grad, qkv_weight_grad, out_weight_grad, small_rows)
    qkv_grad_line, output_line, *weight_grads = lax.optimization_barrier(
        (qkv_grad_line, output_line) + weight_grads
    )
    weight_grads = lax.psum(tuple(weight_grads), ("grp", "ctx"))

    def finish(qkv_grad_line, output_line, qkv_lines, middle_grad, own_tokens, vector_two):
        output_pieces = ring(output_line, line_rows // 2, GROUPS_A)
        normed_grad = line_product(qkv_grad_line, qkv_lines)
        normed_grad = exchange(normed_grad.reshape(SIDE, own_rows, width), GROUPS_B)
        normed_grad, *first_pieces = lax.optimization_barrier((normed_grad, *output_pieces[:3]))
        output_pieces = (*first_pieces, *output_pieces[3:])
        line = first_norm_backward(
            normed_grad, own_tokens, middle_grad, gain_one[None], vector_two
        )
        line = exchange(line, GROUPS_B)
        line, *output_pieces = lax.optimization_barrier((line, *output_pieces))
        vectors = jnp.sum(line[:, own_rows:].astype(fp32), axis=0).astype(bf16)
        line = jnp.concatenate([line[:, :own_rows].reshape(line_rows, width), vectors])
        input_parts = arriving(lambda step: line, GROUPS_A)
        return lay_lines(line_place, output_pieces, bf16), input_parts

    layer_output, input_parts = stage(
        finish, qkv_grad_line, output_line, qkv_lines, middle_grad, own_tokens, vector_two
    )
    vectors = jnp.stack([part[line_rows : line_rows + 8] for part in input_parts])
    vectors = jnp.sum(vectors.astype(fp32), axis=0)
    vectors = vectors + lax.ppermute(vectors, EVERY, swap_all(1, 0))
    come = lax.ppermute(vectors, EVERY, swap_all(2, 0))
    input_parts = lax.optimization_barrier((vectors, *input_parts))[1:]
    come, input_grad = lax.optimization_barrier(
        (come, widen_parts(line_place, input_parts, line_rows))
    )
    vectors = vectors + come
    come = lax.ppermute(vectors, EVERY, swap_all(0, 1))
    weight_grads = lax.optimization_barrier((vectors, *weight_grads))[1:]
    come, *widened = lax.optimization_barrier((come, *widen_weights(*weight_grads)))
    vectors = vectors + come
    down_weight_grad, up_weight_grad, qkv_weight_grad, out_weight_grad = widened[:4]
    down_bias_grad, up_bias_grad, qv_bias_grad = widened[4:]
    return (
        layer_output.reshape(1, rows, width),
        input_grad.reshape(1, rows, width),
        vectors[0],
        vectors[1],
        qkv_weight_grad.transpose(1, 0, 2),
        qv_bias_grad,
        out_weight_grad,
        vectors[4],
        vectors[2],
        vectors[3],
        up_weight_grad,
        up_bias_grad.reshape(hidden_local),
        down_weight_grad,
        down_bias_grad.reshape(width),
    )


def solution(mesh):
    placed = (
        P("grp", "ctx", None),
        P(),
        P(),
        P(None, None, "tp"),
        P(None, "tp"),
        P("tp", None),
        P(),
        P(),
        P(),
        P(None, "tp"),
        P("tp"),
        P("tp", None),
        P(),
        P("grp", "ctx", None),
        P(),
        P(),
        P(),
    )
    return jax.shard_map(
        per_device,
        mesh=mesh,
        in_specs=placed,
        out_specs=(
            P("grp", "ctx", None),
            P("grp", "ctx", None),
            P(),
            P(),
            P(None, None, "tp"),
            P(None, "tp"),
            P("tp", None),
            P(),
            P(),
            P(),
            P(None, "tp"),
            P("tp"),
            P("tp", None),
            P(),
        ),
        check_vma=False,
    )
```

```python
import math

import jax
import jax.numpy as jnp
from jax import lax
from jax.experimental import pallas as pl
from jax.experimental.pallas import tpu as pltpu
from jax.sharding import PartitionSpec as P

HD = 128
GROUPS = 3
TILE = 256
SCALE = 1.0 / math.sqrt(HD)
SCALE_TWO = SCALE * math.log2(math.e)
EVERY = ("grp", "tp", "ctx")
N_GRP, N_TP, N_CTX, SIDE = 4, 16, 2, 4
fp32 = jnp.float32
bf16 = jnp.bfloat16


def device_id(grp, tx, tz, ctx):
    return (grp * N_TP + tx * SIDE + tz) * N_CTX + ctx


def line_groups(first_axis):
    groups = []
    for grp in range(N_GRP):
        for ctx in range(N_CTX):
            for fixed in range(SIDE):
                along_z = (grp % 2 == 0) == first_axis
                groups.append(
                    [
                        device_id(grp, fixed, i, ctx) if along_z else device_id(grp, i, fixed, ctx)
                        for i in range(SIDE)
                    ]
                )
    return groups


GROUPS_A = line_groups(True)
GROUPS_B = line_groups(False)


def swap_lines(groups, bit):
    return [(line[i], line[i ^ bit]) for line in groups for i in range(SIDE)]


def swap_all(grp_bit, ctx_bit):
    return [
        (device_id(g, x, z, c), device_id(g ^ grp_bit, x, z, c ^ ctx_bit))
        for g in range(N_GRP)
        for x in range(SIDE)
        for z in range(SIDE)
        for c in range(N_CTX)
    ]


def exchange(pieces, groups):
    return lax.all_to_all(pieces, EVERY, 0, 0, axis_index_groups=groups)


def spread(piece, groups):
    return exchange(jnp.broadcast_to(piece[None], (SIDE,) + piece.shape), groups)


def turn(groups, step):
    return [(line[i], line[(i + step) % SIDE]) for line in groups for i in range(SIDE)]


def sum_pieces(partial, place, groups):
    piece_rows = partial.shape[0] // SIDE
    total = lax.dynamic_slice_in_dim(partial, place * piece_rows, piece_rows, 0).astype(fp32)
    for step in (1, 3, 2):
        goes = (place + step) % SIDE
        piece = lax.dynamic_slice_in_dim(partial, goes * piece_rows, piece_rows, 0)
        total = total + lax.ppermute(piece, EVERY, turn(groups, step)).astype(fp32)
    return total


def ring(piece, split, groups):
    before = lax.ppermute(piece, EVERY, turn(groups, 1))
    behind = lax.ppermute(piece, EVERY, turn(groups, 3))
    top = lax.ppermute(before[:split], EVERY, turn(groups, 1))
    bottom = lax.ppermute(behind[split:], EVERY, turn(groups, 3))
    return piece, before, behind, top, bottom


def join_pieces(piece, place, groups):
    piece_rows, width = piece.shape
    whole = jnp.zeros((SIDE * piece_rows, width), piece.dtype)
    whole = lax.dynamic_update_slice_in_dim(whole, piece, place * piece_rows, 0)
    for step in (1, 3, 2):
        come = lax.ppermute(piece, EVERY, turn(groups, step))
        origin = (place + SIDE - step) % SIDE
        whole = lax.dynamic_update_slice_in_dim(whole, come, origin * piece_rows, 0)
    return whole


def arriving(pieces, groups):
    come = {step: lax.ppermute(pieces(step), EVERY, turn(groups, step)) for step in (1, 3, 2)}
    return [pieces(0), come[1], come[2], come[3]]


def after(value, *earlier):
    return lax.optimization_barrier((value,) + earlier)[0]


def gather_lines(piece, groups):
    return lax.all_gather(piece, EVERY, axis=0, axis_index_groups=groups)


def layer_norm(values, gain_vec, bias_vec):
    average = jnp.mean(values, axis=-1, keepdims=True)
    centred = values - average
    variance = jnp.mean(centred * centred, axis=-1, keepdims=True)
    return centred * lax.rsqrt(variance + 1e-05) * gain_vec + bias_vec


def position_shares(group_table, group_counts):
    member = (group_table[:, None] == jnp.arange(GROUPS, dtype=jnp.int32)[None, :]).astype(fp32)
    holders = jnp.sum(member, axis=0)
    counts_float = group_counts.astype(fp32)
    per_group = counts_float / (holders * jnp.sum(counts_float))
    return group_table.shape[0] * jnp.sum(member * per_group[None, :], axis=1)


def turned_product(left, right):
    return lax.dot_general(left, right, (((1,), (1,)), ((), ())), preferred_element_type=fp32)


def plain_product(left, right):
    return lax.dot_general(left, right, (((1,), (0,)), ((), ())), preferred_element_type=fp32)


def attention_call(body, name, scratch, like, places, *operands):
    return pl.pallas_call(
        body,
        in_specs=[pl.BlockSpec(memory_space=pltpu.SMEM)]
        + [pl.BlockSpec(memory_space=pltpu.VMEM)] * len(operands),
        out_specs=[pl.BlockSpec(memory_space=pltpu.VMEM)] * len(like),
        out_shape=[jax.ShapeDtypeStruct(shape, kind) for shape, kind in like],
        scratch_shapes=[pltpu.VMEM(shape, fp32) for shape in scratch],
        compiler_params=pltpu.CompilerParams(vmem_limit_bytes=40 * 2**20),
        name=name,
    )(places, *operands)


def own_keys_forward(places, query, pair):
    rows = query.shape[0]
    block = rows // 2

    def body(places, query, pair, top, total, mixed):
        key, value = pair.at[0], pair.at[1]
        for slot in range(2):
            for start in range(slot * block, (slot + 1) * block, TILE):
                last = start + TILE
                keys = slice(slot * block, last)
                scores = turned_product(query[start:last], key[keys]) * SCALE_TWO
                place_q = lax.broadcasted_iota(jnp.int32, scores.shape, 0) + start
                place_k = lax.broadcasted_iota(jnp.int32, scores.shape, 1) + slot * block
                scores = jnp.where(place_q >= place_k, scores, -1e30)
                peak = jnp.max(scores, axis=1, keepdims=True)
                weights = jnp.exp2(scores - peak)
                top[start:last] = peak
                total[start:last] = jnp.sum(weights, axis=1, keepdims=True)
                mixed[start:last] = plain_product(weights.astype(bf16), value[keys])
        for slot in range(2):
            other = 1 - slot

            @pl.when(places[slot] > places[other])
            def _():
                add_keys(query, key, value, top, total, mixed, slot, other, block)

    like = [((rows, 1), fp32), ((rows, 1), fp32), ((rows, HD), fp32)]
    return attention_call(body, "own_keys_forward", [], like, places, query, pair)


def add_keys(query, key, value, top, total, mixed, slot, key_slot, block):
    keys = slice(key_slot * block, (key_slot + 1) * block)
    for start in range(slot * block, (slot + 1) * block, TILE):
        here = slice(start, start + TILE)
        scores = turned_product(query[here], key[keys]) * SCALE_TWO
        peak = jnp.maximum(top[here], jnp.max(scores, axis=1, keepdims=True))
        fade = jnp.exp2(top[here] - peak)
        weights = jnp.exp2(scores - peak)
        top[here] = peak
        total[here] = total[here] * fade + jnp.sum(weights, axis=1, keepdims=True)
        mixed[here] = mixed[here] * fade + plain_product(weights.astype(bf16), value[keys])


def other_keys_forward(places, query, pair, top, total, mixed):
    rows = query.shape[0]
    block = rows // 2

    def body(places, query, pair, top_in, total_in, mixed_in, heads, level, top, total, mixed):
        key, value = pair.at[0], pair.at[1]
        top[...] = top_in[...]
        total[...] = total_in[...]
        mixed[...] = mixed_in[...]
        for slot in range(2):
            for key_slot in range(2):

                @pl.when(places[slot] > places[2 + key_slot])
                def _():
                    add_keys(query, key, value, top, total, mixed, slot, key_slot, block)

        for start in range(0, rows, TILE):
            here = slice(start, start + TILE)
            heads[here] = (mixed[here] / total[here]).astype(bf16)
            logs = top[here] + jnp.log2(total[here])
            level[:, here] = jnp.broadcast_to(logs, (TILE, HD)).T[:8]

    like = [((rows, HD), bf16), ((8, rows), fp32)]
    scratch = [(rows, 1), (rows, 1), (rows, HD)]
    return attention_call(
        body, "other_keys_forward", scratch, like, places, query, pair, top, total, mixed
    )


def pair_backward(
    query, key, value, head_grad, level, slack, query_grad, key_grad, value_grad, slot, key_slot, block, own
):
    for start in range(key_slot * block, (key_slot + 1) * block, TILE):
        keys = slice(start, start + TILE)
        first = start if own else slot * block
        rows = slice(first, (slot + 1) * block)
        scores = turned_product(key[keys], query[rows]) * SCALE_TWO - level[:1, rows]
        if own:
            place_k = lax.broadcasted_iota(jnp.int32, scores.shape, 0)
            place_q = lax.broadcasted_iota(jnp.int32, scores.shape, 1)
            scores = jnp.where(place_q >= place_k, scores, -1e30)
        probs = jnp.exp2(scores)
        value_grad[keys] += plain_product(probs.astype(bf16), head_grad[rows])
        prob_grad = turned_product(value[keys], head_grad[rows]) - slack[:1, rows]
        score_grad = (probs * prob_grad).astype(bf16)
        key_grad[keys] += plain_product(score_grad, query[rows])
        query_grad[rows] += lax.dot_general(
            score_grad, key[keys], (((0,), (0,)), ((), ())), preferred_element_type=fp32
        )


def other_keys_backward(places, query, pair, head_grad, heads, level):
    rows = query.shape[0]
    block = rows // 2

    def body(
        places, query, pair, head_grad, heads, level, query_grad, pair_grad, slack, key_sum, value_sum
    ):
        key, value = pair.at[0], pair.at[1]
        query_grad[...] = jnp.zeros(query_grad.shape, fp32)
        key_sum[...] = jnp.zeros(key_sum.shape, fp32)
        value_sum[...] = jnp.zeros(value_sum.shape, fp32)
        for start in range(0, rows, TILE):
            here = slice(start, start + TILE)
            both = head_grad[here].astype(fp32) * heads[here].astype(fp32)
            both = jnp.sum(both, axis=1, keepdims=True)
            slack[:, here] = jnp.broadcast_to(both, (TILE, HD)).T[:8]
        for slot in range(2):
            for key_slot in range(2):

                @pl.when(places[slot] > places[2 + key_slot])
                def _():
                    pair_backward(
                        query, key, value, head_grad, level, slack,
                        query_grad, key_sum, value_sum, slot, key_slot, block, False,
                    )

        pair_grad[0] = (key_sum[...] * SCALE).astype(bf16)
        pair_grad[1] = value_sum[...].astype(bf16)

    like = [((rows, HD), fp32), ((2, rows, HD), bf16), ((8, rows), fp32)]
    return attention_call(
        body, "other_keys_backward", [(rows, HD)] * 2, like,
        places, query, pair, head_grad, heads, level,
    )


def own_keys_backward(places, query, pair, head_grad, level, slack, query_grad):
    rows = query.shape[0]
    block = rows // 2

    def body(
        places, query, pair, head_grad, level, slack, query_in, query_grad, pair_grad, query_sum
    ):
        key, value = pair.at[0], pair.at[1]
        query_sum[...] = query_in[...]
        pair_grad[...] = jnp.zeros(pair_grad.shape, fp32)
        key_sum = pair_grad.at[0]
        value_sum = pair_grad.at[1]
        for slot in range(2):
            pair_backward(
                query, key, value, head_grad, level, slack,
                query_sum, key_sum, value_sum, slot, slot, block, True,
            )
        for slot in range(2):

            @pl.when(places[slot] > places[1 - slot])
            def _():
                pair_backward(
                    query, key, value, head_grad, level, slack,
                    query_sum, key_sum, value_sum, slot, 1 - slot, block, False,
                )

        pair_grad[0] = pair_grad[0] * SCALE
        query_grad[...] = (query_sum[...] * SCALE).astype(bf16)

    like = [((rows, HD), bf16), ((2, rows, HD), fp32)]
    return attention_call(
        body, "own_keys_backward", [(rows, HD)], like,
        places, query, pair, head_grad, level, slack, query_grad,
    )


def feed_forward(line_place, normed_two, up_lines, active_grad):
    rows, width = normed_two.shape
    units = up_lines.shape[2]
    bend = math.sqrt(2.0 / math.pi)

    def body(place, normed_two, up, grad, *refs):
        pieces, (back, total) = refs[:SIDE], refs[SIDE:]
        step = pl.program_id(0)
        hidden = plain_product(normed_two[...], up[0])
        hidden = hidden + grad[0, rows : rows + 1].astype(fp32)
        square = hidden * hidden
        bent = jnp.tanh(bend * hidden * (1.0 + 0.044715 * square))
        half = 0.5 * (1.0 + bent)
        active = (hidden * half).astype(bf16)
        slope = half + (0.5 * bend) * hidden * (1.0 - bent * bent) * (1.0 + 0.134145 * square)
        low = (slope * grad[0, :rows].astype(fp32)).astype(bf16)

        for index in range(SIDE):

            @pl.when(step == index)
            def _():
                pieces[index][:, :units] = active
                pieces[index][:, units:] = low

        product = turned_product(low, up[0])

        @pl.when(step == 0)
        def _():
            total[...] = product

        @pl.when(step > 0)
        def _():
            total[...] += product

        @pl.when(step == SIDE - 1)
        def _():
            back[...] = total[...].astype(bf16)

    def origin(step, place):
        return ((place[0] + SIDE - step) % SIDE, 0, 0)

    return pl.pallas_call(
        body,
        grid_spec=pltpu.PrefetchScalarGridSpec(
            num_scalar_prefetch=1,
            grid=(SIDE,),
            in_specs=[
                pl.BlockSpec((rows, width), lambda step, place: (0, 0)),
                pl.BlockSpec((1, width, units), origin),
                pl.BlockSpec((1, rows + 16, units), lambda step, place: (step, 0, 0)),
            ],
            out_specs=[
                pl.BlockSpec((rows, 2 * units), lambda step, place: (0, 0)),
            ]
            * SIDE
            + [pl.BlockSpec((rows, width), lambda step, place: (0, 0))],
            scratch_shapes=[pltpu.VMEM((rows, width), fp32)],
        ),
        out_shape=[
            jax.ShapeDtypeStruct((rows, 2 * units), bf16),
        ]
        * SIDE
        + [
            jax.ShapeDtypeStruct((rows, width), bf16),
        ],
        compiler_params=pltpu.CompilerParams(vmem_limit_bytes=58 * 2**20),
        name="feed_forward",
    )(line_place, normed_two, up_lines, active_grad)


def line_product(pieces, weights):
    rows, depth = pieces.shape[1:]
    width = weights.shape[2]

    def body(piece, weight, out, total):
        step = pl.program_id(0)
        product = plain_product(piece[0], weight[0])

        @pl.when(step == 0)
        def _():
            total[...] = product

        @pl.when(step > 0)
        def _():
            total[...] += product

        @pl.when(step == SIDE - 1)
        def _():
            out[...] = total[...].astype(bf16)

    return pl.pallas_call(
        body,
        grid=(SIDE,),
        in_specs=[
            pl.BlockSpec((1, rows, depth), lambda step: (step, 0, 0)),
            pl.BlockSpec((1, depth, width), lambda step: (step, 0, 0)),
        ],
        out_specs=pl.BlockSpec((rows, width), lambda step: (0, 0)),
        out_shape=jax.ShapeDtypeStruct((rows, width), bf16),
        scratch_shapes=[pltpu.VMEM((rows, width), fp32)],
        compiler_params=pltpu.CompilerParams(vmem_limit_bytes=58 * 2**20),
        name="line_product",
    )(pieces, weights)


def down_product(line_place, pieces, down_weight):
    part = pieces[0].shape[0]
    units, width = down_weight.shape

    def body(place, *refs):
        pieces, (weight, out) = refs[:SIDE], refs[SIDE:]
        for index in range(SIDE):

            @pl.when(pl.program_id(0) == index)
            def _():
                out[...] = plain_product(pieces[index][...], weight[...]).astype(bf16)

    return pl.pallas_call(
        body,
        grid_spec=pltpu.PrefetchScalarGridSpec(
            num_scalar_prefetch=1,
            grid=(SIDE,),
            in_specs=[pl.BlockSpec((part, units), lambda step, place: (0, 0))] * SIDE
            + [pl.BlockSpec((units, width), lambda step, place: (0, 0))],
            out_specs=pl.BlockSpec(
                (part, width), lambda step, place: ((place[0] + SIDE - step) % SIDE, 0)
            ),
        ),
        out_shape=jax.ShapeDtypeStruct((SIDE * part, width), bf16),
        compiler_params=pltpu.CompilerParams(vmem_limit_bytes=40 * 2**20),
        name="down_product",
    )(line_place, *pieces, down_weight)


def turned_grad(line_place, matrix, pieces, half):
    rows, width = matrix.shape
    part = rows // SIDE
    units = pieces[0].shape[1] // 2
    steps = 2

    def body(place, matrix, *refs):
        pieces, (out, sums, turned) = refs[:SIDE], refs[SIDE:]

        @pl.when(pl.program_id(0) == 0)
        def _():
            added = None
            for index in range(SIDE):
                start = pl.multiple_of((place[0] + SIDE - index) % SIDE * part, part)
                values = pieces[index][...]
                turned[:, pl.ds(start, part)] = values.T
                piece_sum = jnp.sum(values.astype(fp32), axis=0, keepdims=True)
                added = piece_sum if added is None else added + piece_sum
            sums[...] = added

        out[...] = plain_product(turned[...], matrix[...]).astype(bf16)

    return pl.pallas_call(
        body,
        grid_spec=pltpu.PrefetchScalarGridSpec(
            num_scalar_prefetch=1,
            grid=(steps,),
            in_specs=[pl.BlockSpec((rows, width // steps), lambda step, place: (0, step))]
            + [pl.BlockSpec((part, units), lambda step, place: (0, half))] * SIDE,
            out_specs=[
                pl.BlockSpec((units, width // steps), lambda step, place: (0, step)),
                pl.BlockSpec((1, units), lambda step, place: (0, 0)),
            ],
            scratch_shapes=[pltpu.VMEM((units, rows), bf16)],
        ),
        out_shape=[
            jax.ShapeDtypeStruct((units, width), bf16),
            jax.ShapeDtypeStruct((1, units), fp32),
        ],
        compiler_params=pltpu.CompilerParams(vmem_limit_bytes=58 * 2**20),
        name="turned_grad",
    )(line_place, matrix, *pieces)


def projection_grad(normed, qkv_grad):
    rows, width = normed.shape
    columns = qkv_grad.shape[1]
    steps = 2

    def body(normed, qkv_grad, out, sums, turned):
        @pl.when(pl.program_id(0) == 0)
        def _():
            turned[...] = qkv_grad[...].T
            sums[...] = jnp.sum(qkv_grad[...].astype(fp32), axis=0, keepdims=True)

        out[...] = plain_product(turned[...], normed[...]).astype(bf16)

    return pl.pallas_call(
        body,
        grid=(steps,),
        in_specs=[
            pl.BlockSpec((rows, width // steps), lambda step: (0, step)),
            pl.BlockSpec((rows, columns), lambda step: (0, 0)),
        ],
        out_specs=[
            pl.BlockSpec((columns, width // steps), lambda step: (0, step)),
            pl.BlockSpec((1, columns), lambda step: (0, 0)),
        ],
        out_shape=[
            jax.ShapeDtypeStruct((columns, width), bf16),
            jax.ShapeDtypeStruct((1, columns), fp32),
        ],
        scratch_shapes=[pltpu.VMEM((columns, rows), bf16)],
        compiler_params=pltpu.CompilerParams(vmem_limit_bytes=58 * 2**20),
        name="projection_grad",
    )(normed, qkv_grad)


def norm_call(body, name, parts, rows_in, vectors_in, outs, scratch=(), scalars=()):
    tile = 16
    rows, width = parts.shape[1:]

    def by_rows(shape):
        if len(shape) == 3:
            return pl.BlockSpec((shape[0], tile, shape[2]), lambda step: (0, step, 0))
        return pl.BlockSpec((tile, shape[1]), lambda step: (step, 0))

    def whole(shape):
        return pl.BlockSpec(shape, lambda step: (0,) * len(shape))

    return pl.pallas_call(
        body,
        grid=(rows // tile,),
        in_specs=[pl.BlockSpec(memory_space=pltpu.SMEM)] * len(scalars)
        + [by_rows(parts.shape)]
        + [by_rows(operand.shape) for operand in rows_in]
        + [whole(operand.shape) for operand in vectors_in],
        out_specs=[by_rows(shape) if tiled else whole(shape) for shape, _, tiled in outs],
        out_shape=[jax.ShapeDtypeStruct(shape, kind) for shape, kind, _ in outs],
        scratch_shapes=[pltpu.VMEM(shape, fp32) for shape in scratch],
        compiler_params=pltpu.CompilerParams(vmem_limit_bytes=24 * 2**20),
        name=name,
    )(*scalars, parts, *rows_in, *vectors_in)


def summed_parts(parts):
    return (parts[0].astype(fp32) + parts[1].astype(fp32)) + (
        parts[2].astype(fp32) + parts[3].astype(fp32)
    )


def normalised(values):
    centred = values - jnp.mean(values, axis=1, keepdims=True)
    scale = lax.rsqrt(jnp.mean(centred * centred, axis=1, keepdims=True) + 1e-05)
    return centred * scale, scale


def norm_backward(values, grad, gain):
    unit, scale = normalised(values)
    scaled = grad * gain
    along = jnp.mean(scaled * unit, axis=1, keepdims=True)
    inner = scale * (scaled - jnp.mean(scaled, axis=1, keepdims=True) - unit * along)
    return inner, jnp.sum(grad * unit, axis=0, keepdims=True), jnp.sum(grad, axis=0, keepdims=True)


def second_norm(parts, tokens, out_bias, gain, bias):
    rows, width = tokens.shape

    def body(parts, tokens, out_bias, gain, bias, middle, normed):
        values = tokens[...].astype(fp32) + summed_parts(parts) + out_bias[...]
        middle[...] = values
        low = (normalised(values)[0] * gain[...] + bias[...]).astype(bf16)
        for line in range(SIDE):
            normed[line] = low

    outs = [((rows, width), fp32, True), ((SIDE, rows, width), bf16, True)]
    return norm_call(body, "second_norm", parts, [tokens], [out_bias, gain, bias], outs)


def second_norm_backward(share, parts, middle, cot, gain):
    rows, width = middle.shape

    def body(share, parts, middle, cot, gain, middle_grad, low, vectors):
        inner, gain_part, bias_part = norm_backward(middle[...], summed_parts(parts), gain[...])
        grad = cot[...].astype(fp32) * share[0] + inner
        middle_grad[...] = grad
        for line in range(SIDE):
            low[line] = grad.astype(bf16)

        @pl.when(pl.program_id(0) == 0)
        def _():
            vectors[...] = jnp.zeros(vectors.shape, fp32)

        vectors[0:1] += gain_part
        vectors[1:2] += bias_part
        vectors[2:3] += jnp.sum(grad, axis=0, keepdims=True)

    outs = [
        ((rows, width), fp32, True),
        ((SIDE, rows, width), bf16, True),
        ((8, width), fp32, False),
    ]
    return norm_call(
        body, "second_norm_backward", parts, [middle, cot], [gain], outs, scalars=[share]
    )


def first_norm_backward(parts, tokens, middle_grad, gain, vector_two):
    rows, width = tokens.shape

    def body(parts, tokens, middle_grad, gain, vector_two, line, vectors):
        step = pl.program_id(0)
        values = tokens[...].astype(fp32)
        inner, gain_part, bias_part = norm_backward(values, summed_parts(parts), gain[...])
        low = (middle_grad[...] + inner).astype(bf16)
        tile = low.shape[0]
        here = pl.ds(pl.multiple_of(step * tile, tile), tile)
        for copy in range(SIDE):
            line[copy, here] = low

        @pl.when(step == 0)
        def _():
            vectors[...] = jnp.zeros(vectors.shape, fp32)
            vectors[2:5] = vector_two[:3]

        vectors[0:1] += gain_part
        vectors[1:2] += bias_part

        @pl.when(step == rows // tile - 1)
        def _():
            for copy in range(SIDE):
                line[copy, rows:] = vectors[...].astype(bf16)

    outs = [((SIDE, rows + 16, width), bf16, False)]
    return norm_call(
        body,
        "first_norm_backward",
        parts,
        [tokens, middle_grad],
        [gain, vector_two],
        outs,
        scratch=[(16, width)],
    )[0]


def widen_weights(down, up, qkv, out, small):
    steps = 2
    units, width = down.shape

    def body(
        down_in, up_in, qkv_in, out_in, small_in, down_to, up_to, qkv_to, out_to, down_bias, up_bias, qv_bias
    ):
        def block(down_in, up_in, qkv_in, down_to, up_to, qkv_to):
            down_to[...] = down_in[...].astype(fp32)
            up_to[...] = up_in[...].astype(fp32).T
            for plane in range(3):
                qkv_to[plane] = qkv_in[plane * HD : (plane + 1) * HD].astype(fp32).T

        def columns(count):
            return pl.BlockSpec((count, width // steps), lambda i: (0, i))

        rows = pl.BlockSpec((units // steps, width), lambda i: (i, 0))
        turned = pl.BlockSpec((width // steps, units), lambda i: (i, 0))
        planes = pl.BlockSpec((3, width // steps, HD), lambda i: (0, i, 0))
        pltpu.emit_pipeline(
            block,
            grid=(steps,),
            in_specs=[rows, columns(units), columns(3 * HD)],
            out_specs=[rows, turned, planes],
        )(down_in, up_in, qkv_in, down_to, up_to, qkv_to)
        out_to[...] = out_in[...].astype(fp32)
        values = small_in[...].astype(fp32)
        down_bias[...] = values[:1]
        up_bias[...] = values[1:2, :units]
        qv_bias[:1] = values[1:2, units : units + HD]
        qv_bias[1:] = values[1:2, units + 2 * HD : units + 3 * HD]

    hbm = pl.BlockSpec(memory_space=pltpu.HBM)
    vmem = pl.BlockSpec(memory_space=pltpu.VMEM)
    like = [down.shape, (width, units), (3, width, HD), out.shape, (1, width), (1, units), (2, HD)]
    return pl.pallas_call(
        body,
        in_specs=[hbm] * 3 + [vmem] * 2,
        out_specs=[hbm] * 3 + [vmem] * 4,
        out_shape=[jax.ShapeDtypeStruct(shape, fp32) for shape in like],
        compiler_params=pltpu.CompilerParams(vmem_limit_bytes=58 * 2**20),
        name="widen_weights",
    )(down, up, qkv, out, small)


def widen_parts(line_place, parts, rows):
    width = parts[0].shape[1]

    def body(place, *refs):
        parts, out = refs[:SIDE], refs[SIDE]
        for index in range(SIDE):

            @pl.when(pl.program_id(0) == index)
            def _():
                out[...] = parts[index][...].astype(fp32)

    def part(index):
        return pl.BlockSpec(
            (rows, width), lambda step, place: (0, 0)
        )

    return pl.pallas_call(
        body,
        grid_spec=pltpu.PrefetchScalarGridSpec(
            num_scalar_prefetch=1,
            grid=(SIDE,),
            in_specs=[part(index) for index in range(SIDE)],
            out_specs=pl.BlockSpec(
                (rows, width), lambda step, place: ((place[0] + SIDE - step) % SIDE, 0)
            ),
        ),
        out_shape=jax.ShapeDtypeStruct((SIDE * rows, width), fp32),
        compiler_params=pltpu.CompilerParams(vmem_limit_bytes=32 * 2**20),
        name="widen_parts",
    )(line_place, *parts)


def lay_lines(line_place, pieces, kind):
    tile = pieces[3].shape[0]
    width = pieces[0].shape[1]

    def body(place, own, before, behind, top, bottom, out):
        step = pl.program_id(0)
        sources = [own, own, before, before, behind, behind, top, bottom]
        for index in range(2 * SIDE):

            @pl.when(step == index)
            def _():
                out[...] = sources[index][:tile].astype(kind)

    def piece(first, last):
        return pl.BlockSpec((tile, width), lambda step, place: (jnp.clip(step - first, 0, last), 0))

    def target(step, place):
        kinds = step // 2
        away = jnp.where(kinds == 1, SIDE - 1, jnp.where(kinds == 2, 1, jnp.where(kinds == 3, 2, 0)))
        return ((place[0] + away) % SIDE * 2 + step % 2, 0)

    return pl.pallas_call(
        body,
        grid_spec=pltpu.PrefetchScalarGridSpec(
            num_scalar_prefetch=1,
            grid=(2 * SIDE,),
            in_specs=[piece(0, 1), piece(2, 1), piece(4, 1), piece(6, 0), piece(7, 0)],
            out_specs=pl.BlockSpec((tile, width), target),
        ),
        out_shape=jax.ShapeDtypeStruct((2 * SIDE * tile, width), kind),
        compiler_params=pltpu.CompilerParams(vmem_limit_bytes=24 * 2**20),
        name="lay_lines",
    )(line_place, *pieces)


def per_device(
    layer_input,
    ln1_gain,
    ln1_bias,
    qkv_weight,
    qv_bias,
    out_weight,
    out_bias,
    ln2_gain,
    ln2_bias,
    up_weight,
    up_bias,
    down_weight,
    down_bias,
    cotangent,
    group_table,
    group_counts,
    block_order,
):
    width = layer_input.shape[-1]
    rows = layer_input.shape[1]
    local = qkv_weight.shape[2]
    hidden_local = up_weight.shape[1]
    block_rows = rows // 2
    line_rows = rows // SIDE
    own_rows = line_rows // SIDE
    grp_at = lax.axis_index("grp")
    tp_at = lax.axis_index("tp")
    ctx_at = lax.axis_index("ctx")
    even = grp_at % 2 == 0
    a_at = jnp.where(even, tp_at % SIDE, tp_at // SIDE)
    b_at = jnp.where(even, tp_at // SIDE, tp_at % SIDE)
    line_start = a_at * line_rows
    own_start = line_start + b_at * own_rows

    always = ctx_at < N_CTX

    def stage(work, *operands):
        shapes = jax.eval_shape(work, *operands)

        def empty(*operands):
            return jax.tree.map(lambda like: jnp.zeros(like.shape, like.dtype), shapes)

        return lax.cond(always, work, empty, *operands)

    gain_one = ln1_gain.astype(fp32)
    bias_one = ln1_bias.astype(fp32)
    gain_two = ln2_gain.astype(fp32)
    bias_two = ln2_bias.astype(fp32)
    tokens = layer_input.reshape(rows, width)
    cot = cotangent.reshape(rows, width)
    own_tokens = lax.dynamic_slice_in_dim(tokens, own_start, own_rows, 0)
    own_cot = lax.dynamic_slice_in_dim(cot, own_start, own_rows, 0)

    shares = position_shares(group_table, group_counts)
    grp_slots = jnp.arange(shares.shape[0], dtype=jnp.int32)
    my_share = jnp.sum(jnp.where(grp_slots == grp_at, shares, jnp.zeros_like(shares)))
    column = jnp.arange(block_order.shape[0], dtype=jnp.int32)
    slots = jnp.arange(4, dtype=jnp.int32)
    slots = jnp.where(slots < 2, ctx_at * 2 + slots, (1 - ctx_at) * 2 + slots - 2)
    places = jnp.sum(
        jnp.where(slots[:, None] == column[None, :], block_order[None, :], 0), axis=1
    )
    out_lines = join_pieces(out_weight, a_at, GROUPS_A)
    up_lines = gather_lines(up_weight, GROUPS_A)
    qkv_turned = qkv_weight.transpose(1, 2, 0).reshape(3 * local, width)
    qkv_lines = gather_lines(qkv_turned, GROUPS_A)
    first_normed = layer_norm(tokens.astype(fp32), gain_one, bias_one).astype(bf16)
    mixed = jnp.einsum("rd,cd->rc", first_normed, qkv_turned, preferred_element_type=fp32)
    query = (mixed[:, :local] + qv_bias[0].astype(fp32)).astype(bf16)
    pair = jnp.stack(
        [mixed[:, local : 2 * local], mixed[:, 2 * local :] + qv_bias[1].astype(fp32)]
    ).astype(bf16)
    swap_ctx = [(0, 1), (1, 0)]
    pair_other = lax.ppermute(pair, "ctx", swap_ctx)

    own_part = own_keys_forward(places, query, pair)
    pair_other, out_lines, *own_part = lax.optimization_barrier(
        (pair_other, out_lines, *own_part)
    )
    heads, level = other_keys_forward(places, query, pair_other, *own_part)

    heads_line = exchange(heads.reshape(SIDE, line_rows, local), GROUPS_A)

    cot = after(cot, heads)
    grad_out = cot.astype(fp32) * my_share
    grad_low = grad_out.astype(bf16)
    down_bias_grad = jnp.sum(grad_out, axis=0)
    active_grad = jnp.einsum("rd,fd->rf", grad_low, down_weight, preferred_element_type=fp32)
    bias_rows = jnp.broadcast_to(up_bias[None, None], (SIDE, 16, hidden_local))
    active_grad = jnp.concatenate(
        [active_grad.astype(bf16).reshape(SIDE, line_rows, hidden_local), bias_rows], axis=1
    )
    heads_line, active_grad, down_bias_grad = lax.optimization_barrier(
        (heads_line, active_grad, down_bias_grad)
    )
    active_grad = jnp.stack(
        arriving(
            lambda step: lax.dynamic_index_in_dim(
                active_grad, (a_at + step) % SIDE, 0, keepdims=False
            ),
            GROUPS_A,
        )
    )

    heads_line = heads_line.transpose(1, 0, 2).reshape(line_rows, SIDE * local)
    partial_out = jnp.dot(heads_line, out_lines, preferred_element_type=fp32).astype(bf16)
    partial_out = exchange(partial_out.reshape(SIDE, own_rows, width), GROUPS_B)
    normed = layer_norm(after(tokens, heads_line).astype(fp32), gain_one, bias_one).astype(bf16)
    partial_out, active_grad, normed = lax.optimization_barrier((partial_out, active_grad, normed))
    middle, normed_two = second_norm(
        partial_out, own_tokens, out_bias.astype(fp32)[None], gain_two[None], bias_two[None]
    )
    normed_two = exchange(normed_two, GROUPS_B).reshape(line_rows, width)

    line_place = a_at.astype(jnp.int32)[None]
    *unit_pieces, normed_two_grad = feed_forward(line_place, normed_two, up_lines, active_grad)
    normed_two_grad, normed_two, *unit_pieces = lax.optimization_barrier(
        (normed_two_grad, normed_two, *unit_pieces)
    )

    normed_two_rows = gather_lines(normed_two, GROUPS_A)

    def norm_stage(normed_two_grad, unit_pieces, middle, own_cot, my_share):
        normed_two_grad = exchange(normed_two_grad.reshape(SIDE, own_rows, width), GROUPS_B)
        pieces = arriving(lambda step: unit_pieces[-step % SIDE], GROUPS_A)
        middle_grad, middle_low, vector_two = second_norm_backward(
            my_share[None], normed_two_grad, middle, own_cot, gain_two[None]
        )
        middle_low, *pieces = lax.optimization_barrier((middle_low, *pieces))
        middle_low = exchange(middle_low, GROUPS_B).reshape(line_rows, width)
        partial_mlp = down_product(line_place, pieces, down_weight)
        return middle_grad, middle_low, vector_two, pieces, partial_mlp

    middle_grad, middle_low, vector_two, pieces, partial_mlp = stage(
        norm_stage, normed_two_grad, unit_pieces, middle, own_cot, my_share
    )
    middle_low, qkv_lines, normed_two_rows = lax.optimization_barrier(
        (middle_low, qkv_lines, normed_two_rows)
    )
    partial_mlp = lax.psum_scatter(
        partial_mlp, EVERY, scatter_dimension=0, tiled=True, axis_index_groups=GROUPS_A
    )

    def attention_stage(middle_low, heads_line, pieces, normed_two_rows, grad_low):
        head_grad = jnp.einsum("rd,fd->rf", middle_low, out_lines, preferred_element_type=fp32)
        head_grad = head_grad.astype(bf16).reshape(line_rows, SIDE, local).transpose(1, 0, 2)
        head_grad = exchange(head_grad, GROUPS_A).reshape(rows, local)
        up_weight_grad, up_bias_grad = turned_grad(line_place, normed_two_rows, pieces, 1)
        head_grad, up_weight_grad = lax.optimization_barrier((head_grad, up_weight_grad))
        query_grad, pair_other_grad, slack = other_keys_backward(
            places, query, pair_other, head_grad, heads, level
        )
        pair_from = lax.ppermute(pair_other_grad, "ctx", swap_ctx)
        query_grad, pair_grad = own_keys_backward(
            places, query, pair, head_grad, level, slack, query_grad
        )
        out_weight_grad = jnp.einsum(
            "rf,rd->fd",
            after(heads_line, pair_other_grad),
            middle_low,
            preferred_element_type=fp32,
        ).astype(bf16)
        out_weight_grad = sum_pieces(out_weight_grad, a_at, GROUPS_A).astype(bf16)
        down_weight_grad, _ = turned_grad(line_place, after(grad_low, pair_other_grad), pieces, 0)
        pair_from, pair_grad, query_grad, down_weight_grad = lax.optimization_barrier(
            (pair_from, pair_grad, query_grad, down_weight_grad)
        )
        pair_grad = (pair_grad + pair_from.astype(fp32)).astype(bf16)
        qkv_grad = jnp.concatenate([query_grad, pair_grad[0], pair_grad[1]], axis=1)
        return qkv_grad, up_weight_grad, up_bias_grad, out_weight_grad, down_weight_grad

    qkv_grad, up_weight_grad, up_bias_grad, out_weight_grad, down_weight_grad = stage(
        attention_stage,
        middle_low,
        heads_line,
        pieces,
        normed_two_rows.reshape(rows, width),
        grad_low,
    )
    qkv_grad_line = exchange(qkv_grad.reshape(SIDE, line_rows, 3 * local), GROUPS_A)
    output_sum = sum_pieces(after(partial_mlp, qkv_grad), b_at, GROUPS_B)
    qkv_weight_grad, qkv_bias_grad = projection_grad(normed, qkv_grad)
    qkv_grad_line, output_sum, qkv_weight_grad, qkv_bias_grad = lax.optimization_barrier(
        (qkv_grad_line, output_sum, qkv_weight_grad, qkv_bias_grad)
    )
    output_own = (middle + output_sum + down_bias.astype(fp32)).astype(bf16)
    small_rows = jnp.concatenate(
        [
            down_bias_grad[None],
            jnp.concatenate(
                [
                    up_bias_grad,
                    qkv_bias_grad,
                    jnp.zeros((1, width - hidden_local - 3 * local), fp32),
                ],
                axis=1,
            ),
            jnp.zeros((14, width), fp32),
        ]
    ).astype(bf16)
    out_weight_grad = out_weight_grad.astype(bf16)
    weight_grads = (down_weight_grad, up_weight_grad, qkv_weight_grad, out_weight_grad, small_rows)
    qkv_grad_line, output_own, *weight_grads = lax.optimization_barrier(
        (qkv_grad_line, output_own) + weight_grads
    )
    weight_grads = lax.psum(tuple(weight_grads), ("grp", "ctx"))

    def finish(qkv_grad_line, output_own, qkv_lines, middle_grad, own_tokens, vector_two):
        output_line = join_pieces(output_own, b_at, GROUPS_B)
        normed_grad = line_product(qkv_grad_line, qkv_lines)
        normed_grad, output_line = lax.optimization_barrier((normed_grad, output_line))
        output_pieces = ring(output_line, line_rows // 2, GROUPS_A)
        normed_grad = exchange(normed_grad.reshape(SIDE, own_rows, width), GROUPS_B)
        normed_grad, *first_pieces = lax.optimization_barrier((normed_grad, *output_pieces[:3]))
        output_pieces = (*first_pieces, *output_pieces[3:])
        line = first_norm_backward(
            normed_grad, own_tokens, middle_grad, gain_one[None], vector_two
        )
        line = exchange(line, GROUPS_B)
        line, *output_pieces = lax.optimization_barrier((line, *output_pieces))
        vectors = jnp.sum(line[:, own_rows:].astype(fp32), axis=0).astype(bf16)
        line = jnp.concatenate([line[:, :own_rows].reshape(line_rows, width), vectors])
        input_parts = arriving(lambda step: line, GROUPS_A)
        return lay_lines(line_place, output_pieces, bf16), input_parts

    layer_output, input_parts = stage(
        finish, qkv_grad_line, output_own, qkv_lines, middle_grad, own_tokens, vector_two
    )
    vectors = jnp.stack([part[line_rows : line_rows + 8] for part in input_parts])
    vectors = jnp.sum(vectors.astype(fp32), axis=0)
    vectors = vectors + lax.ppermute(vectors, EVERY, swap_all(1, 0))
    come = lax.ppermute(vectors, EVERY, swap_all(2, 0))
    input_parts = lax.optimization_barrier((vectors, *input_parts))[1:]
    come, input_grad = lax.optimization_barrier(
        (come, widen_parts(line_place, input_parts, line_rows))
    )
    vectors = vectors + come
    come = lax.ppermute(vectors, EVERY, swap_all(0, 1))
    weight_grads = lax.optimization_barrier((vectors, *weight_grads))[1:]
    come, *widened = lax.optimization_barrier((come, *widen_weights(*weight_grads)))
    vectors = vectors + come
    down_weight_grad, up_weight_grad, qkv_weight_grad, out_weight_grad = widened[:4]
    down_bias_grad, up_bias_grad, qv_bias_grad = widened[4:]
    return (
        layer_output.reshape(1, rows, width),
        input_grad.reshape(1, rows, width),
        vectors[0],
        vectors[1],
        qkv_weight_grad.transpose(1, 0, 2),
        qv_bias_grad,
        out_weight_grad,
        vectors[4],
        vectors[2],
        vectors[3],
        up_weight_grad,
        up_bias_grad.reshape(hidden_local),
        down_weight_grad,
        down_bias_grad.reshape(width),
    )


def solution(mesh):
    placed = (
        P("grp", "ctx", None),
        P(),
        P(),
        P(None, None, "tp"),
        P(None, "tp"),
        P("tp", None),
        P(),
        P(),
        P(),
        P(None, "tp"),
        P("tp"),
        P("tp", None),
        P(),
        P("grp", "ctx", None),
        P(),
        P(),
        P(),
    )
    return jax.shard_map(
        per_device,
        mesh=mesh,
        in_specs=placed,
        out_specs=(
            P("grp", "ctx", None),
            P("grp", "ctx", None),
            P(),
            P(),
            P(None, None, "tp"),
            P(None, "tp"),
            P("tp", None),
            P(),
            P(),
            P(),
            P(None, "tp"),
            P("tp"),
            P("tp", None),
            P(),
        ),
        check_vma=False,
    )
```

```python
import math

import jax
import jax.numpy as jnp
from jax import lax
from jax.experimental import pallas as pl
from jax.experimental.pallas import tpu as pltpu
from jax.sharding import PartitionSpec as P

HD = 128
GROUPS = 3
TILE = 256
SCALE = 1.0 / math.sqrt(HD)
SCALE_TWO = SCALE * math.log2(math.e)
EVERY = ("grp", "tp", "ctx")
N_GRP, N_TP, N_CTX, SIDE = 4, 16, 2, 4
fp32 = jnp.float32
bf16 = jnp.bfloat16


def device_id(grp, tx, tz, ctx):
    return (grp * N_TP + tx * SIDE + tz) * N_CTX + ctx


def line_groups(first_axis):
    groups = []
    for grp in range(N_GRP):
        for ctx in range(N_CTX):
            for fixed in range(SIDE):
                along_z = (grp % 2 == 0) == first_axis
                groups.append(
                    [
                        device_id(grp, fixed, i, ctx) if along_z else device_id(grp, i, fixed, ctx)
                        for i in range(SIDE)
                    ]
                )
    return groups


GROUPS_A = line_groups(True)
GROUPS_B = line_groups(False)


def swap_lines(groups, bit):
    return [(line[i], line[i ^ bit]) for line in groups for i in range(SIDE)]


def swap_all(grp_bit, ctx_bit):
    return [
        (device_id(g, x, z, c), device_id(g ^ grp_bit, x, z, c ^ ctx_bit))
        for g in range(N_GRP)
        for x in range(SIDE)
        for z in range(SIDE)
        for c in range(N_CTX)
    ]


def exchange(pieces, groups):
    return lax.all_to_all(pieces, EVERY, 0, 0, axis_index_groups=groups)


def spread(piece, groups):
    return exchange(jnp.broadcast_to(piece[None], (SIDE,) + piece.shape), groups)


def turn(groups, step):
    return [(line[i], line[(i + step) % SIDE]) for line in groups for i in range(SIDE)]


def sum_pieces(partial, place, groups):
    piece_rows = partial.shape[0] // SIDE
    total = lax.dynamic_slice_in_dim(partial, place * piece_rows, piece_rows, 0).astype(fp32)
    for step in (1, 3, 2):
        goes = (place + step) % SIDE
        piece = lax.dynamic_slice_in_dim(partial, goes * piece_rows, piece_rows, 0)
        total = total + lax.ppermute(piece, EVERY, turn(groups, step)).astype(fp32)
    return total


def ring(piece, split, groups):
    before = lax.ppermute(piece, EVERY, turn(groups, 1))
    behind = lax.ppermute(piece, EVERY, turn(groups, 3))
    top = lax.ppermute(before[:split], EVERY, turn(groups, 1))
    bottom = lax.ppermute(behind[split:], EVERY, turn(groups, 3))
    return piece, before, behind, top, bottom


def join_pieces(piece, place, groups):
    piece_rows, width = piece.shape
    whole = jnp.zeros((SIDE * piece_rows, width), piece.dtype)
    whole = lax.dynamic_update_slice_in_dim(whole, piece, place * piece_rows, 0)
    for step in (1, 3, 2):
        come = lax.ppermute(piece, EVERY, turn(groups, step))
        origin = (place + SIDE - step) % SIDE
        whole = lax.dynamic_update_slice_in_dim(whole, come, origin * piece_rows, 0)
    return whole


def arriving(pieces, groups):
    come = {step: lax.ppermute(pieces(step), EVERY, turn(groups, step)) for step in (1, 3, 2)}
    return [pieces(0), come[1], come[2], come[3]]


def after(value, *earlier):
    return lax.optimization_barrier((value,) + earlier)[0]


def gather_lines(piece, groups):
    return lax.all_gather(piece, EVERY, axis=0, axis_index_groups=groups)


def layer_norm(values, gain_vec, bias_vec):
    average = jnp.mean(values, axis=-1, keepdims=True)
    centred = values - average
    variance = jnp.mean(centred * centred, axis=-1, keepdims=True)
    return centred * lax.rsqrt(variance + 1e-05) * gain_vec + bias_vec


def position_shares(group_table, group_counts):
    member = (group_table[:, None] == jnp.arange(GROUPS, dtype=jnp.int32)[None, :]).astype(fp32)
    holders = jnp.sum(member, axis=0)
    counts_float = group_counts.astype(fp32)
    per_group = counts_float / (holders * jnp.sum(counts_float))
    return group_table.shape[0] * jnp.sum(member * per_group[None, :], axis=1)


def turned_product(left, right):
    return lax.dot_general(left, right, (((1,), (1,)), ((), ())), preferred_element_type=fp32)


def plain_product(left, right):
    return lax.dot_general(left, right, (((1,), (0,)), ((), ())), preferred_element_type=fp32)


def attention_call(body, name, scratch, like, places, *operands):
    return pl.pallas_call(
        body,
        in_specs=[pl.BlockSpec(memory_space=pltpu.SMEM)]
        + [pl.BlockSpec(memory_space=pltpu.VMEM)] * len(operands),
        out_specs=[pl.BlockSpec(memory_space=pltpu.VMEM)] * len(like),
        out_shape=[jax.ShapeDtypeStruct(shape, kind) for shape, kind in like],
        scratch_shapes=[pltpu.VMEM(shape, fp32) for shape in scratch],
        compiler_params=pltpu.CompilerParams(vmem_limit_bytes=40 * 2**20),
        name=name,
    )(places, *operands)


def own_keys_forward(places, query, pair):
    rows = query.shape[0]
    block = rows // 2

    def body(places, query, pair, top, total, mixed):
        key, value = pair.at[0], pair.at[1]
        for slot in range(2):
            for start in range(slot * block, (slot + 1) * block, TILE):
                last = start + TILE
                keys = slice(slot * block, last)
                scores = turned_product(query[start:last], key[keys]) * SCALE_TWO
                place_q = lax.broadcasted_iota(jnp.int32, scores.shape, 0) + start
                place_k = lax.broadcasted_iota(jnp.int32, scores.shape, 1) + slot * block
                scores = jnp.where(place_q >= place_k, scores, -1e30)
                peak = jnp.max(scores, axis=1, keepdims=True)
                weights = jnp.exp2(scores - peak)
                top[start:last] = peak
                total[start:last] = jnp.sum(weights, axis=1, keepdims=True)
                mixed[start:last] = plain_product(weights.astype(bf16), value[keys])
        for slot in range(2):
            other = 1 - slot

            @pl.when(places[slot] > places[other])
            def _():
                add_keys(query, key, value, top, total, mixed, slot, other, block)

    like = [((rows, 1), fp32), ((rows, 1), fp32), ((rows, HD), fp32)]
    return attention_call(body, "own_keys_forward", [], like, places, query, pair)


def add_keys(query, key, value, top, total, mixed, slot, key_slot, block):
    keys = slice(key_slot * block, (key_slot + 1) * block)
    for start in range(slot * block, (slot + 1) * block, TILE):
        here = slice(start, start + TILE)
        scores = turned_product(query[here], key[keys]) * SCALE_TWO
        peak = jnp.maximum(top[here], jnp.max(scores, axis=1, keepdims=True))
        fade = jnp.exp2(top[here] - peak)
        weights = jnp.exp2(scores - peak)
        top[here] = peak
        total[here] = total[here] * fade + jnp.sum(weights, axis=1, keepdims=True)
        mixed[here] = mixed[here] * fade + plain_product(weights.astype(bf16), value[keys])


def other_keys_forward(places, query, pair, top, total, mixed):
    rows = query.shape[0]
    block = rows // 2

    def body(places, query, pair, top_in, total_in, mixed_in, heads, level, top, total, mixed):
        key, value = pair.at[0], pair.at[1]
        top[...] = top_in[...]
        total[...] = total_in[...]
        mixed[...] = mixed_in[...]
        for slot in range(2):
            for key_slot in range(2):

                @pl.when(places[slot] > places[2 + key_slot])
                def _():
                    add_keys(query, key, value, top, total, mixed, slot, key_slot, block)

        for start in range(0, rows, TILE):
            here = slice(start, start + TILE)
            heads[here] = (mixed[here] / total[here]).astype(bf16)
            logs = top[here] + jnp.log2(total[here])
            level[:, here] = jnp.broadcast_to(logs, (TILE, HD)).T[:8]

    like = [((rows, HD), bf16), ((8, rows), fp32)]
    scratch = [(rows, 1), (rows, 1), (rows, HD)]
    return attention_call(
        body, "other_keys_forward", scratch, like, places, query, pair, top, total, mixed
    )


def pair_backward(
    query, key, value, head_grad, level, slack, query_grad, key_grad, value_grad, slot, key_slot, block, own
):
    for start in range(key_slot * block, (key_slot + 1) * block, TILE):
        keys = slice(start, start + TILE)
        first = start if own else slot * block
        rows = slice(first, (slot + 1) * block)
        scores = turned_product(key[keys], query[rows]) * SCALE_TWO - level[:1, rows]
        if own:
            place_k = lax.broadcasted_iota(jnp.int32, scores.shape, 0)
            place_q = lax.broadcasted_iota(jnp.int32, scores.shape, 1)
            scores = jnp.where(place_q >= place_k, scores, -1e30)
        probs = jnp.exp2(scores)
        value_grad[keys] += plain_product(probs.astype(bf16), head_grad[rows])
        prob_grad = turned_product(value[keys], head_grad[rows]) - slack[:1, rows]
        score_grad = (probs * prob_grad).astype(bf16)
        key_grad[keys] += plain_product(score_grad, query[rows])
        query_grad[rows] += lax.dot_general(
            score_grad, key[keys], (((0,), (0,)), ((), ())), preferred_element_type=fp32
        )


def other_keys_backward(places, query, pair, head_grad, heads, level):
    rows = query.shape[0]
    block = rows // 2

    def body(
        places, query, pair, head_grad, heads, level, query_grad, pair_grad, slack, key_sum, value_sum
    ):
        key, value = pair.at[0], pair.at[1]
        query_grad[...] = jnp.zeros(query_grad.shape, fp32)
        key_sum[...] = jnp.zeros(key_sum.shape, fp32)
        value_sum[...] = jnp.zeros(value_sum.shape, fp32)
        for start in range(0, rows, TILE):
            here = slice(start, start + TILE)
            both = head_grad[here].astype(fp32) * heads[here].astype(fp32)
            both = jnp.sum(both, axis=1, keepdims=True)
            slack[:, here] = jnp.broadcast_to(both, (TILE, HD)).T[:8]
        for slot in range(2):
            for key_slot in range(2):

                @pl.when(places[slot] > places[2 + key_slot])
                def _():
                    pair_backward(
                        query, key, value, head_grad, level, slack,
                        query_grad, key_sum, value_sum, slot, key_slot, block, False,
                    )

        pair_grad[0] = (key_sum[...] * SCALE).astype(bf16)
        pair_grad[1] = value_sum[...].astype(bf16)

    like = [((rows, HD), fp32), ((2, rows, HD), bf16), ((8, rows), fp32)]
    return attention_call(
        body, "other_keys_backward", [(rows, HD)] * 2, like,
        places, query, pair, head_grad, heads, level,
    )


def own_keys_backward(places, query, pair, head_grad, level, slack, query_grad):
    rows = query.shape[0]
    block = rows // 2

    def body(
        places, query, pair, head_grad, level, slack, query_in, query_grad, pair_grad, query_sum
    ):
        key, value = pair.at[0], pair.at[1]
        query_sum[...] = query_in[...]
        pair_grad[...] = jnp.zeros(pair_grad.shape, fp32)
        key_sum = pair_grad.at[0]
        value_sum = pair_grad.at[1]
        for slot in range(2):
            pair_backward(
                query, key, value, head_grad, level, slack,
                query_sum, key_sum, value_sum, slot, slot, block, True,
            )
        for slot in range(2):

            @pl.when(places[slot] > places[1 - slot])
            def _():
                pair_backward(
                    query, key, value, head_grad, level, slack,
                    query_sum, key_sum, value_sum, slot, 1 - slot, block, False,
                )

        pair_grad[0] = pair_grad[0] * SCALE
        query_grad[...] = (query_sum[...] * SCALE).astype(bf16)

    like = [((rows, HD), bf16), ((2, rows, HD), fp32)]
    return attention_call(
        body, "own_keys_backward", [(rows, HD)], like,
        places, query, pair, head_grad, level, slack, query_grad,
    )


def feed_forward(line_place, normed_two, up_lines, active_grad):
    rows, width = normed_two.shape
    units = up_lines.shape[2]
    bend = math.sqrt(2.0 / math.pi)

    def body(place, normed_two, up, grad, *refs):
        pieces, (back, total) = refs[:SIDE], refs[SIDE:]
        step = pl.program_id(0)
        hidden = plain_product(normed_two[...], up[0])
        hidden = hidden + grad[0, rows : rows + 1].astype(fp32)
        square = hidden * hidden
        bent = jnp.tanh(bend * hidden * (1.0 + 0.044715 * square))
        half = 0.5 * (1.0 + bent)
        active = (hidden * half).astype(bf16)
        slope = half + (0.5 * bend) * hidden * (1.0 - bent * bent) * (1.0 + 0.134145 * square)
        low = (slope * grad[0, :rows].astype(fp32)).astype(bf16)

        for index in range(SIDE):

            @pl.when(step == index)
            def _():
                pieces[index][:, :units] = active
                pieces[index][:, units:] = low

        product = turned_product(low, up[0])

        @pl.when(step == 0)
        def _():
            total[...] = product

        @pl.when(step > 0)
        def _():
            total[...] += product

        @pl.when(step == SIDE - 1)
        def _():
            back[...] = total[...].astype(bf16)

    def origin(step, place):
        return ((place[0] + SIDE - step) % SIDE, 0, 0)

    return pl.pallas_call(
        body,
        grid_spec=pltpu.PrefetchScalarGridSpec(
            num_scalar_prefetch=1,
            grid=(SIDE,),
            in_specs=[
                pl.BlockSpec((rows, width), lambda step, place: (0, 0)),
                pl.BlockSpec((1, width, units), origin),
                pl.BlockSpec((1, rows + 16, units), lambda step, place: (step, 0, 0)),
            ],
            out_specs=[
                pl.BlockSpec((rows, 2 * units), lambda step, place: (0, 0)),
            ]
            * SIDE
            + [pl.BlockSpec((rows, width), lambda step, place: (0, 0))],
            scratch_shapes=[pltpu.VMEM((rows, width), fp32)],
        ),
        out_shape=[
            jax.ShapeDtypeStruct((rows, 2 * units), bf16),
        ]
        * SIDE
        + [
            jax.ShapeDtypeStruct((rows, width), bf16),
        ],
        compiler_params=pltpu.CompilerParams(vmem_limit_bytes=58 * 2**20),
        name="feed_forward",
    )(line_place, normed_two, up_lines, active_grad)


def line_product(pieces, weights):
    rows, depth = pieces.shape[1:]
    width = weights.shape[2]

    def body(piece, weight, out, total):
        step = pl.program_id(0)
        product = plain_product(piece[0], weight[0])

        @pl.when(step == 0)
        def _():
            total[...] = product

        @pl.when(step > 0)
        def _():
            total[...] += product

        @pl.when(step == SIDE - 1)
        def _():
            out[...] = total[...].astype(bf16)

    return pl.pallas_call(
        body,
        grid=(SIDE,),
        in_specs=[
            pl.BlockSpec((1, rows, depth), lambda step: (step, 0, 0)),
            pl.BlockSpec((1, depth, width), lambda step: (step, 0, 0)),
        ],
        out_specs=pl.BlockSpec((rows, width), lambda step: (0, 0)),
        out_shape=jax.ShapeDtypeStruct((rows, width), bf16),
        scratch_shapes=[pltpu.VMEM((rows, width), fp32)],
        compiler_params=pltpu.CompilerParams(vmem_limit_bytes=58 * 2**20),
        name="line_product",
    )(pieces, weights)


def down_product(line_place, pieces, down_weight):
    part = pieces[0].shape[0]
    units, width = down_weight.shape

    def body(place, *refs):
        pieces, (weight, out) = refs[:SIDE], refs[SIDE:]
        for index in range(SIDE):

            @pl.when(pl.program_id(0) == index)
            def _():
                out[...] = plain_product(pieces[index][...], weight[...]).astype(bf16)

    return pl.pallas_call(
        body,
        grid_spec=pltpu.PrefetchScalarGridSpec(
            num_scalar_prefetch=1,
            grid=(SIDE,),
            in_specs=[pl.BlockSpec((part, units), lambda step, place: (0, 0))] * SIDE
            + [pl.BlockSpec((units, width), lambda step, place: (0, 0))],
            out_specs=pl.BlockSpec(
                (part, width), lambda step, place: ((place[0] + SIDE - step) % SIDE, 0)
            ),
        ),
        out_shape=jax.ShapeDtypeStruct((SIDE * part, width), bf16),
        compiler_params=pltpu.CompilerParams(vmem_limit_bytes=40 * 2**20),
        name="down_product",
    )(line_place, *pieces, down_weight)


def turned_grad(line_place, matrix, pieces, half):
    rows, width = matrix.shape
    part = rows // SIDE
    units = pieces[0].shape[1] // 2
    steps = 2

    def body(place, matrix, *refs):
        pieces, (out, sums, turned) = refs[:SIDE], refs[SIDE:]

        @pl.when(pl.program_id(0) == 0)
        def _():
            added = None
            for index in range(SIDE):
                start = pl.multiple_of((place[0] + SIDE - index) % SIDE * part, part)
                values = pieces[index][...]
                turned[:, pl.ds(start, part)] = values.T
                piece_sum = jnp.sum(values.astype(fp32), axis=0, keepdims=True)
                added = piece_sum if added is None else added + piece_sum
            sums[...] = added

        out[...] = plain_product(turned[...], matrix[...]).astype(bf16)

    return pl.pallas_call(
        body,
        grid_spec=pltpu.PrefetchScalarGridSpec(
            num_scalar_prefetch=1,
            grid=(steps,),
            in_specs=[pl.BlockSpec((rows, width // steps), lambda step, place: (0, step))]
            + [pl.BlockSpec((part, units), lambda step, place: (0, half))] * SIDE,
            out_specs=[
                pl.BlockSpec((units, width // steps), lambda step, place: (0, step)),
                pl.BlockSpec((1, units), lambda step, place: (0, 0)),
            ],
            scratch_shapes=[pltpu.VMEM((units, rows), bf16)],
        ),
        out_shape=[
            jax.ShapeDtypeStruct((units, width), bf16),
            jax.ShapeDtypeStruct((1, units), fp32),
        ],
        compiler_params=pltpu.CompilerParams(vmem_limit_bytes=58 * 2**20),
        name="turned_grad",
    )(line_place, matrix, *pieces)


def projection_grad(normed, qkv_grad):
    rows, width = normed.shape
    columns = qkv_grad.shape[1]
    steps = 2

    def body(normed, qkv_grad, out, sums, turned):
        @pl.when(pl.program_id(0) == 0)
        def _():
            turned[...] = qkv_grad[...].T
            sums[...] = jnp.sum(qkv_grad[...].astype(fp32), axis=0, keepdims=True)

        out[...] = plain_product(turned[...], normed[...]).astype(bf16)

    return pl.pallas_call(
        body,
        grid=(steps,),
        in_specs=[
            pl.BlockSpec((rows, width // steps), lambda step: (0, step)),
            pl.BlockSpec((rows, columns), lambda step: (0, 0)),
        ],
        out_specs=[
            pl.BlockSpec((columns, width // steps), lambda step: (0, step)),
            pl.BlockSpec((1, columns), lambda step: (0, 0)),
        ],
        out_shape=[
            jax.ShapeDtypeStruct((columns, width), bf16),
            jax.ShapeDtypeStruct((1, columns), fp32),
        ],
        scratch_shapes=[pltpu.VMEM((columns, rows), bf16)],
        compiler_params=pltpu.CompilerParams(vmem_limit_bytes=58 * 2**20),
        name="projection_grad",
    )(normed, qkv_grad)


def norm_call(body, name, parts, rows_in, vectors_in, outs, scratch=(), scalars=()):
    tile = 16
    rows, width = parts.shape[1:]

    def by_rows(shape):
        if len(shape) == 3:
            return pl.BlockSpec((shape[0], tile, shape[2]), lambda step: (0, step, 0))
        return pl.BlockSpec((tile, shape[1]), lambda step: (step, 0))

    def whole(shape):
        return pl.BlockSpec(shape, lambda step: (0,) * len(shape))

    return pl.pallas_call(
        body,
        grid=(rows // tile,),
        in_specs=[pl.BlockSpec(memory_space=pltpu.SMEM)] * len(scalars)
        + [by_rows(parts.shape)]
        + [by_rows(operand.shape) for operand in rows_in]
        + [whole(operand.shape) for operand in vectors_in],
        out_specs=[by_rows(shape) if tiled else whole(shape) for shape, _, tiled in outs],
        out_shape=[jax.ShapeDtypeStruct(shape, kind) for shape, kind, _ in outs],
        scratch_shapes=[pltpu.VMEM(shape, fp32) for shape in scratch],
        compiler_params=pltpu.CompilerParams(vmem_limit_bytes=24 * 2**20),
        name=name,
    )(*scalars, parts, *rows_in, *vectors_in)


def summed_parts(parts):
    return (parts[0].astype(fp32) + parts[1].astype(fp32)) + (
        parts[2].astype(fp32) + parts[3].astype(fp32)
    )


def normalised(values):
    centred = values - jnp.mean(values, axis=1, keepdims=True)
    scale = lax.rsqrt(jnp.mean(centred * centred, axis=1, keepdims=True) + 1e-05)
    return centred * scale, scale


def norm_backward(values, grad, gain):
    unit, scale = normalised(values)
    scaled = grad * gain
    along = jnp.mean(scaled * unit, axis=1, keepdims=True)
    inner = scale * (scaled - jnp.mean(scaled, axis=1, keepdims=True) - unit * along)
    return inner, jnp.sum(grad * unit, axis=0, keepdims=True), jnp.sum(grad, axis=0, keepdims=True)


def second_norm(parts, tokens, out_bias, gain, bias):
    rows, width = tokens.shape

    def body(parts, tokens, out_bias, gain, bias, middle, normed):
        values = tokens[...].astype(fp32) + summed_parts(parts) + out_bias[...]
        middle[...] = values
        low = (normalised(values)[0] * gain[...] + bias[...]).astype(bf16)
        for line in range(SIDE):
            normed[line] = low

    outs = [((rows, width), fp32, True), ((SIDE, rows, width), bf16, True)]
    return norm_call(body, "second_norm", parts, [tokens], [out_bias, gain, bias], outs)


def second_norm_backward(share, parts, middle, cot, gain):
    rows, width = middle.shape

    def body(share, parts, middle, cot, gain, middle_grad, low, vectors):
        inner, gain_part, bias_part = norm_backward(middle[...], summed_parts(parts), gain[...])
        grad = cot[...].astype(fp32) * share[0] + inner
        middle_grad[...] = grad
        for line in range(SIDE):
            low[line] = grad.astype(bf16)

        @pl.when(pl.program_id(0) == 0)
        def _():
            vectors[...] = jnp.zeros(vectors.shape, fp32)

        vectors[0:1] += gain_part
        vectors[1:2] += bias_part
        vectors[2:3] += jnp.sum(grad, axis=0, keepdims=True)

    outs = [
        ((rows, width), fp32, True),
        ((SIDE, rows, width), bf16, True),
        ((8, width), fp32, False),
    ]
    return norm_call(
        body, "second_norm_backward", parts, [middle, cot], [gain], outs, scalars=[share]
    )


def first_norm_backward(parts, tokens, middle_grad, gain, vector_two):
    rows, width = tokens.shape

    def body(parts, tokens, middle_grad, gain, vector_two, line, vectors):
        step = pl.program_id(0)
        values = tokens[...].astype(fp32)
        inner, gain_part, bias_part = norm_backward(values, summed_parts(parts), gain[...])
        low = (middle_grad[...] + inner).astype(bf16)
        tile = low.shape[0]
        here = pl.ds(pl.multiple_of(step * tile, tile), tile)
        for copy in range(SIDE):
            line[copy, here] = low

        @pl.when(step == 0)
        def _():
            vectors[...] = jnp.zeros(vectors.shape, fp32)
            vectors[2:5] = vector_two[:3]

        vectors[0:1] += gain_part
        vectors[1:2] += bias_part

        @pl.when(step == rows // tile - 1)
        def _():
            for copy in range(SIDE):
                line[copy, rows:] = vectors[...].astype(bf16)

    outs = [((SIDE, rows + 16, width), bf16, False)]
    return norm_call(
        body,
        "first_norm_backward",
        parts,
        [tokens, middle_grad],
        [gain, vector_two],
        outs,
        scratch=[(16, width)],
    )[0]


def widen_weights(down, up, qkv, out, small):
    steps = 2
    units, width = down.shape

    def body(
        down_in, up_in, qkv_in, out_in, small_in, down_to, up_to, qkv_to, out_to, down_bias, up_bias, qv_bias
    ):
        def block(down_in, up_in, qkv_in, down_to, up_to, qkv_to):
            down_to[...] = down_in[...].astype(fp32)
            up_to[...] = up_in[...].astype(fp32).T
            for plane in range(3):
                qkv_to[plane] = qkv_in[plane * HD : (plane + 1) * HD].astype(fp32).T

        def columns(count):
            return pl.BlockSpec((count, width // steps), lambda i: (0, i))

        rows = pl.BlockSpec((units // steps, width), lambda i: (i, 0))
        turned = pl.BlockSpec((width // steps, units), lambda i: (i, 0))
        planes = pl.BlockSpec((3, width // steps, HD), lambda i: (0, i, 0))
        pltpu.emit_pipeline(
            block,
            grid=(steps,),
            in_specs=[rows, columns(units), columns(3 * HD)],
            out_specs=[rows, turned, planes],
        )(down_in, up_in, qkv_in, down_to, up_to, qkv_to)
        out_to[...] = out_in[...].astype(fp32)
        values = small_in[...].astype(fp32)
        down_bias[...] = values[:1]
        up_bias[...] = values[1:2, :units]
        qv_bias[:1] = values[1:2, units : units + HD]
        qv_bias[1:] = values[1:2, units + 2 * HD : units + 3 * HD]

    hbm = pl.BlockSpec(memory_space=pltpu.HBM)
    vmem = pl.BlockSpec(memory_space=pltpu.VMEM)
    like = [down.shape, (width, units), (3, width, HD), out.shape, (1, width), (1, units), (2, HD)]
    return pl.pallas_call(
        body,
        in_specs=[hbm] * 3 + [vmem] * 2,
        out_specs=[hbm] * 3 + [vmem] * 4,
        out_shape=[jax.ShapeDtypeStruct(shape, fp32) for shape in like],
        compiler_params=pltpu.CompilerParams(vmem_limit_bytes=58 * 2**20),
        name="widen_weights",
    )(down, up, qkv, out, small)


def widen_parts(line_place, parts, rows):
    width = parts[0].shape[1]

    def body(place, *refs):
        parts, out = refs[:SIDE], refs[SIDE]
        for index in range(SIDE):

            @pl.when(pl.program_id(0) == index)
            def _():
                out[...] = parts[index][...].astype(fp32)

    def part(index):
        return pl.BlockSpec(
            (rows, width), lambda step, place: (0, 0)
        )

    return pl.pallas_call(
        body,
        grid_spec=pltpu.PrefetchScalarGridSpec(
            num_scalar_prefetch=1,
            grid=(SIDE,),
            in_specs=[part(index) for index in range(SIDE)],
            out_specs=pl.BlockSpec(
                (rows, width), lambda step, place: ((place[0] + SIDE - step) % SIDE, 0)
            ),
        ),
        out_shape=jax.ShapeDtypeStruct((SIDE * rows, width), fp32),
        compiler_params=pltpu.CompilerParams(vmem_limit_bytes=32 * 2**20),
        name="widen_parts",
    )(line_place, *parts)


def lay_lines(line_place, pieces, kind):
    tile = pieces[3].shape[0]
    width = pieces[0].shape[1]

    def body(place, own, before, behind, top, bottom, out):
        step = pl.program_id(0)
        sources = [own, own, before, before, behind, behind, top, bottom]
        for index in range(2 * SIDE):

            @pl.when(step == index)
            def _():
                out[...] = sources[index][:tile].astype(kind)

    def piece(first, last):
        return pl.BlockSpec((tile, width), lambda step, place: (jnp.clip(step - first, 0, last), 0))

    def target(step, place):
        kinds = step // 2
        away = jnp.where(kinds == 1, SIDE - 1, jnp.where(kinds == 2, 1, jnp.where(kinds == 3, 2, 0)))
        return ((place[0] + away) % SIDE * 2 + step % 2, 0)

    return pl.pallas_call(
        body,
        grid_spec=pltpu.PrefetchScalarGridSpec(
            num_scalar_prefetch=1,
            grid=(2 * SIDE,),
            in_specs=[piece(0, 1), piece(2, 1), piece(4, 1), piece(6, 0), piece(7, 0)],
            out_specs=pl.BlockSpec((tile, width), target),
        ),
        out_shape=jax.ShapeDtypeStruct((2 * SIDE * tile, width), kind),
        compiler_params=pltpu.CompilerParams(vmem_limit_bytes=24 * 2**20),
        name="lay_lines",
    )(line_place, *pieces)


def per_device(
    layer_input,
    ln1_gain,
    ln1_bias,
    qkv_weight,
    qv_bias,
    out_weight,
    out_bias,
    ln2_gain,
    ln2_bias,
    up_weight,
    up_bias,
    down_weight,
    down_bias,
    cotangent,
    group_table,
    group_counts,
    block_order,
):
    width = layer_input.shape[-1]
    rows = layer_input.shape[1]
    local = qkv_weight.shape[2]
    hidden_local = up_weight.shape[1]
    block_rows = rows // 2
    line_rows = rows // SIDE
    own_rows = line_rows // SIDE
    grp_at = lax.axis_index("grp")
    tp_at = lax.axis_index("tp")
    ctx_at = lax.axis_index("ctx")
    even = grp_at % 2 == 0
    a_at = jnp.where(even, tp_at % SIDE, tp_at // SIDE)
    b_at = jnp.where(even, tp_at // SIDE, tp_at % SIDE)
    line_start = a_at * line_rows
    own_start = line_start + b_at * own_rows

    always = ctx_at < N_CTX

    def stage(work, *operands):
        shapes = jax.eval_shape(work, *operands)

        def empty(*operands):
            return jax.tree.map(lambda like: jnp.zeros(like.shape, like.dtype), shapes)

        return lax.cond(always, work, empty, *operands)

    gain_one = ln1_gain.astype(fp32)
    bias_one = ln1_bias.astype(fp32)
    gain_two = ln2_gain.astype(fp32)
    bias_two = ln2_bias.astype(fp32)
    tokens = layer_input.reshape(rows, width)
    cot = cotangent.reshape(rows, width)
    own_tokens = lax.dynamic_slice_in_dim(tokens, own_start, own_rows, 0)
    own_cot = lax.dynamic_slice_in_dim(cot, own_start, own_rows, 0)

    shares = position_shares(group_table, group_counts)
    grp_slots = jnp.arange(shares.shape[0], dtype=jnp.int32)
    my_share = jnp.sum(jnp.where(grp_slots == grp_at, shares, jnp.zeros_like(shares)))
    column = jnp.arange(block_order.shape[0], dtype=jnp.int32)
    slots = jnp.arange(4, dtype=jnp.int32)
    slots = jnp.where(slots < 2, ctx_at * 2 + slots, (1 - ctx_at) * 2 + slots - 2)
    places = jnp.sum(
        jnp.where(slots[:, None] == column[None, :], block_order[None, :], 0), axis=1
    )
    out_lines = join_pieces(out_weight, a_at, GROUPS_A)
    up_lines = gather_lines(up_weight, GROUPS_A)
    qkv_turned = qkv_weight.transpose(1, 2, 0).reshape(3 * local, width)
    qkv_lines = gather_lines(qkv_turned, GROUPS_A)
    first_normed = layer_norm(tokens.astype(fp32), gain_one, bias_one).astype(bf16)
    mixed = jnp.einsum("rd,cd->rc", first_normed, qkv_turned, preferred_element_type=fp32)
    query = (mixed[:, :local] + qv_bias[0].astype(fp32)).astype(bf16)
    pair = jnp.stack(
        [mixed[:, local : 2 * local], mixed[:, 2 * local :] + qv_bias[1].astype(fp32)]
    ).astype(bf16)
    swap_ctx = [(0, 1), (1, 0)]
    pair_other = lax.ppermute(pair, "ctx", swap_ctx)

    own_part = own_keys_forward(places, query, pair)
    pair_other, out_lines, *own_part = lax.optimization_barrier(
        (pair_other, out_lines, *own_part)
    )
    heads, level = other_keys_forward(places, query, pair_other, *own_part)

    heads_line = exchange(heads.reshape(SIDE, line_rows, local), GROUPS_A)

    cot = after(cot, heads)
    grad_out = cot.astype(fp32) * my_share
    grad_low = grad_out.astype(bf16)
    down_bias_grad = jnp.sum(grad_out, axis=0)
    active_grad = jnp.einsum("rd,fd->rf", grad_low, down_weight, preferred_element_type=fp32)
    bias_rows = jnp.broadcast_to(up_bias[None, None], (SIDE, 16, hidden_local))
    active_grad = jnp.concatenate(
        [active_grad.astype(bf16).reshape(SIDE, line_rows, hidden_local), bias_rows], axis=1
    )
    heads_line, active_grad, down_bias_grad = lax.optimization_barrier(
        (heads_line, active_grad, down_bias_grad)
    )
    active_grad = jnp.stack(
        arriving(
            lambda step: lax.dynamic_index_in_dim(
                active_grad, (a_at + step) % SIDE, 0, keepdims=False
            ),
            GROUPS_A,
        )
    )

    heads_line = heads_line.transpose(1, 0, 2).reshape(line_rows, SIDE * local)
    partial_out = jnp.dot(heads_line, out_lines, preferred_element_type=fp32).astype(bf16)
    partial_out = exchange(partial_out.reshape(SIDE, own_rows, width), GROUPS_B)
    normed = layer_norm(after(tokens, heads_line).astype(fp32), gain_one, bias_one).astype(bf16)
    partial_out, active_grad, normed = lax.optimization_barrier((partial_out, active_grad, normed))
    middle, normed_two = second_norm(
        partial_out, own_tokens, out_bias.astype(fp32)[None], gain_two[None], bias_two[None]
    )
    normed_two = exchange(normed_two, GROUPS_B).reshape(line_rows, width)

    line_place = a_at.astype(jnp.int32)[None]
    *unit_pieces, normed_two_grad = feed_forward(line_place, normed_two, up_lines, active_grad)
    normed_two_grad, normed_two, *unit_pieces = lax.optimization_barrier(
        (normed_two_grad, normed_two, *unit_pieces)
    )

    normed_two_rows = gather_lines(normed_two, GROUPS_A)

    def norm_stage(normed_two_grad, unit_pieces, middle, own_cot, my_share):
        normed_two_grad = exchange(normed_two_grad.reshape(SIDE, own_rows, width), GROUPS_B)
        pieces = arriving(lambda step: unit_pieces[-step % SIDE], GROUPS_A)
        middle_grad, middle_low, vector_two = second_norm_backward(
            my_share[None], normed_two_grad, middle, own_cot, gain_two[None]
        )
        middle_low, *pieces = lax.optimization_barrier((middle_low, *pieces))
        middle_low = exchange(middle_low, GROUPS_B).reshape(line_rows, width)
        partial_mlp = down_product(line_place, pieces, down_weight)
        return middle_grad, middle_low, vector_two, pieces, partial_mlp

    middle_grad, middle_low, vector_two, pieces, partial_mlp = stage(
        norm_stage, normed_two_grad, unit_pieces, middle, own_cot, my_share
    )
    middle_low, qkv_lines, normed_two_rows = lax.optimization_barrier(
        (middle_low, qkv_lines, normed_two_rows)
    )
    partial_mlp = lax.psum_scatter(
        partial_mlp, EVERY, scatter_dimension=0, tiled=True, axis_index_groups=GROUPS_A
    )

    def attention_stage(middle_low, heads_line, pieces, normed_two_rows, grad_low):
        head_grad = jnp.einsum("rd,fd->rf", middle_low, out_lines, preferred_element_type=fp32)
        head_grad = head_grad.astype(bf16).reshape(line_rows, SIDE, local).transpose(1, 0, 2)
        head_grad = exchange(head_grad, GROUPS_A).reshape(rows, local)
        up_weight_grad, up_bias_grad = turned_grad(line_place, normed_two_rows, pieces, 1)
        head_grad, up_weight_grad = lax.optimization_barrier((head_grad, up_weight_grad))
        query_grad, pair_other_grad, slack = other_keys_backward(
            places, query, pair_other, head_grad, heads, level
        )
        pair_from = lax.ppermute(pair_other_grad, "ctx", swap_ctx)
        query_grad, pair_grad = own_keys_backward(
            places, query, pair, head_grad, level, slack, query_grad
        )
        out_weight_grad = jnp.einsum(
            "rf,rd->fd",
            after(heads_line, pair_other_grad),
            middle_low,
            preferred_element_type=fp32,
        ).astype(bf16)
        out_weight_grad = sum_pieces(out_weight_grad, a_at, GROUPS_A).astype(bf16)
        down_weight_grad, _ = turned_grad(line_place, after(grad_low, pair_other_grad), pieces, 0)
        pair_from, pair_grad, query_grad, down_weight_grad = lax.optimization_barrier(
            (pair_from, pair_grad, query_grad, down_weight_grad)
        )
        pair_grad = (pair_grad + pair_from.astype(fp32)).astype(bf16)
        qkv_grad = jnp.concatenate([query_grad, pair_grad[0], pair_grad[1]], axis=1)
        return qkv_grad, up_weight_grad, up_bias_grad, out_weight_grad, down_weight_grad

    qkv_grad, up_weight_grad, up_bias_grad, out_weight_grad, down_weight_grad = stage(
        attention_stage,
        middle_low,
        heads_line,
        pieces,
        normed_two_rows.reshape(rows, width),
        grad_low,
    )
    qkv_grad_line = exchange(qkv_grad.reshape(SIDE, line_rows, 3 * local), GROUPS_A)
    output_sum = sum_pieces(after(partial_mlp, qkv_grad), b_at, GROUPS_B)
    qkv_weight_grad, qkv_bias_grad = projection_grad(normed, qkv_grad)
    qkv_grad_line, output_sum, qkv_weight_grad, qkv_bias_grad = lax.optimization_barrier(
        (qkv_grad_line, output_sum, qkv_weight_grad, qkv_bias_grad)
    )
    output_own = (middle + output_sum + down_bias.astype(fp32)).astype(bf16)
    small_rows = jnp.concatenate(
        [
            down_bias_grad[None],
            jnp.concatenate(
                [
                    up_bias_grad,
                    qkv_bias_grad,
                    jnp.zeros((1, width - hidden_local - 3 * local), fp32),
                ],
                axis=1,
            ),
            jnp.zeros((14, width), fp32),
        ]
    ).astype(bf16)
    out_weight_grad = out_weight_grad.astype(bf16)
    weight_grads = (down_weight_grad, up_weight_grad, qkv_weight_grad, out_weight_grad, small_rows)
    qkv_grad_line, output_own, *weight_grads = lax.optimization_barrier(
        (qkv_grad_line, output_own) + weight_grads
    )
    weight_grads = lax.psum(tuple(weight_grads), ("grp", "ctx"))

    def finish(qkv_grad_line, output_own, qkv_lines, middle_grad, own_tokens, vector_two):
        output_line = join_pieces(output_own, b_at, GROUPS_B)
        normed_grad = line_product(qkv_grad_line, qkv_lines)
        normed_grad, output_line = lax.optimization_barrier((normed_grad, output_line))
        output_pieces = ring(output_line, line_rows // 2, GROUPS_A)
        normed_grad = exchange(normed_grad.reshape(SIDE, own_rows, width), GROUPS_B)
        normed_grad, *first_pieces = lax.optimization_barrier((normed_grad, *output_pieces[:3]))
        output_pieces = (*first_pieces, *output_pieces[3:])
        line = first_norm_backward(
            normed_grad, own_tokens, middle_grad, gain_one[None], vector_two
        )
        line = exchange(line, GROUPS_B)
        line, *first_pieces = lax.optimization_barrier((line, *output_pieces[:3]))
        output_pieces = (*first_pieces, *output_pieces[3:])
        vectors = jnp.sum(line[:, own_rows:].astype(fp32), axis=0).astype(bf16)
        line = jnp.concatenate([line[:, :own_rows].reshape(line_rows, width), vectors])
        input_parts = arriving(lambda step: line, GROUPS_A)
        return lay_lines(line_place, output_pieces, bf16), input_parts

    layer_output, input_parts = stage(
        finish, qkv_grad_line, output_own, qkv_lines, middle_grad, own_tokens, vector_two
    )
    vectors = jnp.stack([part[line_rows : line_rows + 8] for part in input_parts])
    vectors = jnp.sum(vectors.astype(fp32), axis=0)
    vectors = vectors + lax.ppermute(vectors, EVERY, swap_all(1, 0))
    come = lax.ppermute(vectors, EVERY, swap_all(2, 0))
    input_parts = lax.optimization_barrier((vectors, *input_parts))[1:]
    come, input_grad = lax.optimization_barrier(
        (come, widen_parts(line_place, input_parts, line_rows))
    )
    vectors = vectors + come
    come = lax.ppermute(vectors, EVERY, swap_all(0, 1))
    weight_grads = lax.optimization_barrier((vectors, *weight_grads))[1:]
    come, *widened = lax.optimization_barrier((come, *widen_weights(*weight_grads)))
    vectors = vectors + come
    down_weight_grad, up_weight_grad, qkv_weight_grad, out_weight_grad = widened[:4]
    down_bias_grad, up_bias_grad, qv_bias_grad = widened[4:]
    return (
        layer_output.reshape(1, rows, width),
        input_grad.reshape(1, rows, width),
        vectors[0],
        vectors[1],
        qkv_weight_grad.transpose(1, 0, 2),
        qv_bias_grad,
        out_weight_grad,
        vectors[4],
        vectors[2],
        vectors[3],
        up_weight_grad,
        up_bias_grad.reshape(hidden_local),
        down_weight_grad,
        down_bias_grad.reshape(width),
    )


def solution(mesh):
    placed = (
        P("grp", "ctx", None),
        P(),
        P(),
        P(None, None, "tp"),
        P(None, "tp"),
        P("tp", None),
        P(),
        P(),
        P(),
        P(None, "tp"),
        P("tp"),
        P("tp", None),
        P(),
        P("grp", "ctx", None),
        P(),
        P(),
        P(),
    )
    return jax.shard_map(
        per_device,
        mesh=mesh,
        in_specs=placed,
        out_specs=(
            P("grp", "ctx", None),
            P("grp", "ctx", None),
            P(),
            P(),
            P(None, None, "tp"),
            P(None, "tp"),
            P("tp", None),
            P(),
            P(),
            P(),
            P(None, "tp"),
            P("tp"),
            P("tp", None),
            P(),
        ),
        check_vma=False,
    )
```
